256 devices in a mesh: gx: 4 (over z_lo), gy: 8 (over x, core), gz: 8 (over y, z_hi).
Axes of the slice: x: 4, y: 4, z: 8 (z_hi: 2, z_lo: 4; z = z_hi * 4 + z_lo), core: 2. Of those that a mesh axis runs over, the one named last changes fastest.
Arguments:
- vel: float32 [3, 256, 64, 1024], P(None, 'gz', 'gx', 'gy'), may hold values from -6 to 6
- pres: float32 [256, 64, 1024], P('gz', 'gx', 'gy'), may hold values from -6 to 6
- modulus: float32 [256, 64, 1024], P('gz', 'gx', 'gy'), may hold values from 0.05 to 0.5
- adj_vel_in: float32 [3, 256, 64, 1024], P(None, 'gz', 'gx', 'gy'), may hold values from -6 to 6
- adj_pres_in: float32 [256, 64, 1024], P('gz', 'gx', 'gy'), may hold values from -6 to 6
- sensor_values: float32 [8192, 128], P(('gx', 'gy', 'gz')), may hold values from -6 to 6
- sensor_owner: int32 [8192, 1], P(('gx', 'gy', 'gz')), may hold values from 0 to 31; in each aligned block of 32 rows (0 to 31, 32 to 63, ...) at most 4 rows name the same one
- sensor_line: int32 [8192], P(('gx', 'gy', 'gz')), may hold values from 0 to 15
- sensor_step: int32 [8192], P(('gx', 'gy', 'gz')), may hold values from 0 to 1
Outputs:
- adj_vel: float32 [3, 256, 64, 1024], P(None, 'gz', 'gx', 'gy')
- adj_pres: float32 [256, 64, 1024], P('gz', 'gx', 'gy')
- shear_gradient: float32 [256, 64, 1024], P('gz', 'gx', 'gy')
The draws below stay inside these ranges and needn't reach their ends.
Inputs may be any that keep to these rules, and one draw needn't show every extreme that they name: `sensor_owner`: among the 32 rows of one device at most 4 name the same surface brick, and in every draw some device has 4 rows for one brick.
All inputs are finite; a program needn't handle non-finite values.
Results may differ from the reference program's by a relative error of at most 0.00011.
Values sent between devices are 32-bit elements; how exact they have to be, the bound alone decides.
A program may use at most 64 MiB of HBM per device.

```python
import math
import jax
import jax.numpy as jnp
import numpy as np
from jax import lax

CX = 16
CY = 128
STEPS = 2
R_DEV = 32
CAP = 4
NX = 64
NY = 1024
NZ = 256
ROWS = 8192
N_GX = 4
N_GY = 8


def plant(array, key, least, largest):
    longest = array.shape.index(max(array.shape))
    spots = []
    for shift in (0, 1):
        where = [jax.random.randint(jax.random.fold_in(key, axis), (), 0, length) for axis, length in enumerate(array.shape)]
        where[longest] = (where[longest] + shift) % array.shape[longest]
        spots.append(tuple(where))
    return array.at[spots[0]].set(least).at[spots[1]].set(largest)


def shard_levels(key, shape, split, least, largest):
    loudness = 1.0
    for dim, shards_of in split:
        steps = jax.random.uniform(jax.random.fold_in(jax.random.fold_in(key, 6), dim), (shards_of,), jnp.float32, least / len(split), largest / len(split))
        loudness = loudness * jnp.repeat(jnp.exp(steps), shape[dim] // shards_of).reshape((-1,) + (1,) * (len(shape) - 1 - dim))
    return loudness


def assign_block(key, own, number, rows, amount, top, limit, skew):
    sequence = jax.random.permutation(key, amount)
    heavy_load, ordinary = load_shares(amount, rows * top, limit, skew, True), load_shares(amount, rows * top, limit, skew, False)
    places = jnp.arange(amount)

    def named(lengths, turn):
        used = int((lengths > 0).sum())
        fixed = max(1, used // 4)
        shifted = fixed + (places - fixed + turn * (used - fixed)) % max(1, amount - fixed)
        return jnp.zeros((amount,), jnp.int32).at[sequence[jnp.where(places < fixed, places, shifted)]].set(jnp.asarray(lengths, jnp.int32))

    lengths = jnp.where(number % 4 == 0, named(heavy_load, number // 4), named(ordinary, number - number // 4 - 1))
    mixed = jax.random.permutation(jax.random.fold_in(own, 3), amount)
    donor, sink = mixed[0:amount // 2 * 2:2], mixed[1:amount // 2 * 2:2]
    margin = jnp.minimum(lengths[donor] - 1, limit - lengths[sink]) // 2
    margin = jnp.where((donor == sequence[0]) | (sink == sequence[0]) | (lengths[sink] == 0), 0, jnp.maximum(margin, 0))
    shifted = jax.random.randint(jax.random.fold_in(own, 4), (amount // 2,), 0, 1 << 20) % (margin + 1)
    lengths = lengths.at[donor].add(-shifted).at[sink].add(shifted)
    members = jnp.searchsorted(jnp.cumsum(lengths), jnp.arange(rows * top), side="right").astype(jnp.int32)
    listing = members.reshape(top, rows).T
    listing = listing[jax.random.permutation(jax.random.fold_in(own, 1), rows)]
    turn = jax.random.randint(jax.random.fold_in(own, 2), (rows, 1), 0, top)
    return jnp.take_along_axis(listing, (jnp.arange(top)[None, :] + turn) % top, axis=1)


def load_shares(amount, total, most, lean, full):
    weights = [(1 << 20) // math.isqrt(rank ** lean) + 1 for rank in range(1, amount + 1)]
    largest = most if full else min(most, max(-(-total // amount), total * weights[0] // sum(weights)))
    least = 1 if total - largest >= amount - 1 else 0
    counts, surplus = [largest] + [least] * (amount - 1), total - largest - least * (amount - 1)
    while surplus > 0:
        candidates = [i for i in range(1, amount) if counts[i] < largest] or [i for i in range(1, amount) if counts[i] < most]
        mass, left = sum([weights[i] for i in candidates]), surplus
        for i in candidates:
            extra = min(most - counts[i], max(1, left * weights[i] // mass), surplus)
            counts[i] = counts[i] + extra
            surplus = surplus - extra
    return np.array(counts)


def bell_draw(key, dims, deviation, reach, shards=(), kind=jnp.bfloat16):
    values = jax.random.normal(key, dims, jnp.float32) * deviation
    if len(shards) > 0:
        values = shard_levels(key, dims, shards, -0.22, 0.18) * values
    return jnp.clip(values, min=-reach, max=reach).astype(kind)


def setup_inputs(seed: int = 0) -> dict:
    streams_of = jax.random.split(jax.random.key(seed), 10)
    vel = bell_draw(streams_of[0], (3, NZ, NX, NY), 1.0, 6.0, ((1, 8), (2, 4), (3, 8)), jnp.float32)
    pres = bell_draw(streams_of[1], (NZ, NX, NY), 1.0, 6.0, ((0, 8), (1, 4), (2, 8)), jnp.float32)
    modulus = jnp.clip(jnp.exp(math.log(0.5) - 2.3025851 * jax.random.uniform(streams_of[2], (NZ, NX, NY), jnp.float32) ** shard_levels(streams_of[2], (NZ, NX, NY), ((0, 8), (1, 4), (2, 8)), -0.2, 0.2)), 0.05, 0.5)
    adj_vel_in = bell_draw(streams_of[3], (3, NZ, NX, NY), 1.0, 6.0, ((1, 8), (2, 4), (3, 8)), jnp.float32)
    adj_pres_in = bell_draw(streams_of[4], (NZ, NX, NY), 1.0, 6.0, ((0, 8), (1, 4), (2, 8)), jnp.float32)
    sensor_values = bell_draw(streams_of[5], (ROWS, CY), 1.0, 6.0, ((0, 256),), jnp.float32)
    sensor_owner_keys = jax.random.split(jax.random.fold_in(streams_of[6], 1), ROWS // R_DEV)
    sensor_owner_turns = jax.random.permutation(jax.random.fold_in(streams_of[6], 3), ROWS // R_DEV)
    sensor_owner = jax.vmap(lambda own, number: assign_block(jax.random.fold_in(streams_of[6], 2), own, number, R_DEV, N_GX * N_GY, 1, CAP, 2))(sensor_owner_keys, sensor_owner_turns).reshape((ROWS, 1))
    sensor_line = plant(jax.random.randint(streams_of[7], (ROWS,), 0, CX), jax.random.fold_in(streams_of[7], 1), 0, CX - 1).astype(jnp.int32)
    sensor_step = plant(jax.random.randint(streams_of[8], (ROWS,), 0, STEPS), jax.random.fold_in(streams_of[8], 1), 0, STEPS - 1).astype(jnp.int32)
    return {"vel": vel, "pres": pres, "modulus": modulus, "adj_vel_in": adj_vel_in, "adj_pres_in": adj_pres_in, "sensor_values": sensor_values, "sensor_owner": sensor_owner, "sensor_line": sensor_line, "sensor_step": sensor_step}


def lower(field, axis):
    widths = [(0, 0)] * field.ndim
    widths[axis] = (1, 0)
    return lax.slice_in_dim(jnp.pad(field, widths), 0, field.shape[axis], axis=axis)


def upper(field, axis):
    widths = [(0, 0)] * field.ndim
    widths[axis] = (0, 1)
    return lax.slice_in_dim(jnp.pad(field, widths), 1, field.shape[axis] + 1, axis=axis)


def laplace(field):
    total = upper(field, 0) + lower(field, 0) + upper(field, 1) + lower(field, 1)
    total = total + upper(field, 2) + lower(field, 2)
    return total - 6.0 * field


def divergence(vector):
    along_x = vector[0] - lower(vector[0], 1)
    along_y = vector[1] - lower(vector[1], 2)
    along_z = vector[2] - lower(vector[2], 0)
    return along_x + along_y + along_z


def gradient(field):
    return jnp.stack([upper(field, 1) - field, upper(field, 2) - field, upper(field, 0) - field])


def reference(vel, pres, modulus, adj_vel_in, adj_pres_in, sensor_values, sensor_owner, sensor_line, sensor_step):
    owner = sensor_owner[:, 0]
    xs = (owner // N_GY) * CX + sensor_line
    ys = (owner % N_GY)[:, None] * CY + jnp.arange(CY, dtype=jnp.int32)[None, :]
    forcing = jnp.zeros((STEPS, NX, NY), jnp.float32)
    forcing = forcing.at[sensor_step[:, None], xs[:, None], ys].add(sensor_values)
    state_v, state_p = vel, pres
    saved = []
    for step in range(STEPS):
        bend = jnp.stack([laplace(state_v[c]) for c in range(3)])
        saved.append(bend)
        state_p = state_p + 1.0 * divergence(state_v)
        state_v = state_v + 0.25 * (gradient(state_p) + modulus[None] * bend)
    lam_v, lam_p = adj_vel_in, adj_pres_in
    shear = jnp.zeros(pres.shape, jnp.float32)
    for step in reversed(range(STEPS)):
        lam_v = lam_v.at[2, 0].add(forcing[step])
        shear = shear + 0.25 * jnp.sum(lam_v * saved[step], axis=0)
        middle = lam_p - 0.25 * divergence(lam_v)
        weighted = jnp.stack([laplace(modulus * lam_v[c]) for c in range(3)])
        lam_v = lam_v + 0.25 * weighted - 1.0 * gradient(middle)
        lam_p = middle
    return lam_v, lam_p, shear
```

```python
import jax
import jax.numpy as jnp
from jax import lax
from jax.experimental import pallas as pl
from jax.experimental.pallas import tpu as pltpu
from jax.sharding import PartitionSpec as P

MESH = pl.DeviceIdType.MESH
F32 = jnp.float32
CZ, CX, CY = 32, 16, 128
PITCH = 32
LAYERS = CZ + 2
ROWS = LAYERS * PITCH
NGX, NGY, NGZ = 4, 8, 8
HIGH = lax.Precision.HIGHEST


def body(
    vel, pres, modulus, avel, apres, svals, sowner, sline, sstep,
    o_av, o_ap, o_sh,
    v0, a1, ma, md, p1, m1, v1, a0, ma0, m0,
    p0, ap, bend0, lm, lm0, sh, out,
    ys1, yl1, yh1, ys2, yh2, ys3, yl3, yh3, ys4, yh4,
    ys5, yl5, yh5, ys6, yh6, ys7, yl7, yh7, ys8, yh8,
    xa1, xb1, xh1, xl1, xa2, xh2, xa3, xb3, xh3, xl3, xa4, xh4,
    xa5, xb5, xh5, xl5, xa6, xh6, xa7, xb7, xh7, xl7, xa8, xh8,
    zl, zu, cs, gath, dense, hsum, esum, ksum,
    in_sem, out_sem, xs_sem, xr_sem, ys_sem, yr_sem, zs_sem, zr_sem,
    f1s, f1r, f2s, f2r, f3s, f3r,
):
    gx, gy, gz = lax.axis_index("gx"), lax.axis_index("gy"), lax.axis_index("gz")
    has_xm, has_xp = gx > 0, gx < NGX - 1
    has_ym, has_yp = gy > 0, gy < NGY - 1
    has_zm, has_zp = gz > 0, gz < NGZ - 1
    barrier = pltpu.get_barrier_semaphore()

    def grid3(ref):
        if len(ref.shape) == 3:
            return ref.reshape(3, LAYERS, PITCH, CY).at[:, pl.ds(1, CZ), pl.ds(8, CX), :]
        return ref.reshape(LAYERS, PITCH, CY).at[pl.ds(1, CZ), pl.ds(8, CX), :]

    loads = [
        pltpu.make_async_copy(src, dst, in_sem.at[i])
        for i, (src, dst) in enumerate(
            [(avel, grid3(a1)), (modulus, grid3(md)), (vel, grid3(v0)), (pres, p0), (apres, ap)]
        )
    ]
    for copy in loads:
        copy.start()

    lane = lax.broadcasted_iota(jnp.int32, (CX, CY), 1)

    @pl.when(jnp.logical_not(has_ym))
    def _():
        for ref in (yl1, yl3, yl7):
            ref[...] = jnp.zeros(ref.shape, F32)
        yl5[...] = jnp.zeros(yl5.shape, F32)

    @pl.when(jnp.logical_not(has_yp))
    def _():
        for ref in (yh1, yh2, yh3, yh4, yh6, yh7, yh8):
            ref[...] = jnp.zeros(ref.shape, F32)
        yh5[...] = jnp.zeros(yh5.shape, F32)

    def greet(device):
        pl.semaphore_signal(barrier, inc=1, device_id=device, device_id_type=MESH)

    @pl.when(has_zm)
    def _():
        greet((gx, gy, gz - 1))

    @pl.when(has_zp)
    def _():
        greet((gx, gy, gz + 1))

    @pl.when(gz == 0)
    def _():
        for other in range(2, NGZ):
            greet((gx, gy, other))

    for step in range(1, NGY):
        greet((gx, lax.rem(gy + step, NGY), gz))
    for step in range(1, NGX):
        greet((lax.rem(gx + step, NGX), gy, gz))
    expected = (
        NGX - 1 + NGY - 1
        + has_zm.astype(jnp.int32) + has_zp.astype(jnp.int32) + (gz >= 2).astype(jnp.int32)
    )

    def comps(ref):
        return [ref.at[c] for c in range(3)]

    V0, A1, MA, V1, A0, MA0 = (comps(r) for r in (v0, a1, ma, v1, a0, ma0))

    zeros_layer = jnp.zeros((PITCH, CY), F32)
    zeros_rows = jnp.zeros((LAYERS, CY), F32)
    for ref in V0 + A1 + MA + V1 + A0 + MA0 + [p1, m1, m0]:
        ref[0:PITCH, :] = zeros_layer
        ref[ROWS - PITCH:ROWS, :] = zeros_layer

    @pl.when(jnp.logical_not(has_xm))
    def _():
        for ref in V0 + [A1[0]] + MA + V1 + [A0[0]] + MA0:
            ref[pl.ds(7, LAYERS, stride=PITCH), :] = zeros_rows

    @pl.when(jnp.logical_not(has_xp))
    def _():
        for ref in V0 + MA + [A1[2]] + V1 + MA0 + [p1, m1, m0]:
            ref[pl.ds(24, LAYERS, stride=PITCH), :] = zeros_rows

    owner_col = sowner[...].astype(F32)
    r0 = lax.broadcasted_iota(jnp.int32, (32, 32), 0)
    r1 = lax.broadcasted_iota(jnp.int32, (32, 32), 1)
    owner_row = jnp.sum(jnp.where(r0 == r1, owner_col, 0.0), axis=0, keepdims=True)
    rank = jnp.sum(
        jnp.where((owner_col == owner_row) & (r0 < r1), 1.0, 0.0), axis=0, keepdims=True
    ).astype(jnp.int32)
    owner_int = owner_row.astype(jnp.int32)
    own_gx, own_gy = owner_int >> 3, owner_int & 7
    place = own_gy * 32 + own_gx * 8 + rank
    code_row = (own_gx * 32 + sstep[...] * CX + sline[...] + 1).astype(F32)
    code_col = jnp.sum(jnp.where(r0 == r1, code_row, 0.0), axis=1, keepdims=True)
    slot = lax.broadcasted_iota(jnp.int32, (256, 32), 0)
    cs[...] = jnp.dot(
        (slot == place).astype(F32), svals[...], precision=HIGH, preferred_element_type=F32
    ) + jnp.dot(
        (slot == place + 4).astype(F32), jnp.broadcast_to(code_col, (32, CY)),
        precision=HIGH, preferred_element_type=F32,
    )
    mine = pl.ds(pl.multiple_of(gy * 32, 32), 32)
    gath[mine, :] = cs[mine, :]

    def ld(ref, z, dx=0):
        return ref[pl.ds((z + 1) * PITCH + 8 + dx, CX), :]

    def st(ref, z, value):
        ref[pl.ds(pl.multiple_of((z + 1) * PITCH + 8, 8), CX), :] = value

    def ylo(u, blk, z, f):
        shift = (CY - ((z >> 2) * 16 + 2 * f)) & (CY - 1)
        return jnp.where(lane == 0, pltpu.roll(blk[z & 3], shift, 1), pltpu.roll(u, 1, 1))

    def yhi(u, blk, z, f):
        shift = CY - 2 - (z >> 2) * 16 - 2 * f
        return jnp.where(lane == CY - 1, pltpu.roll(blk[z & 3], shift, 1), pltpu.roll(u, CY - 1, 1))

    def lap(ref, z, yl, yh, f):
        c = ld(ref, z)
        total = ld(ref, z, 1) + ld(ref, z, -1) + (ld(ref, z + 1) + ld(ref, z - 1))
        return total + (ylo(c, yl, z, f) + yhi(c, yh, z, f)) - 6.0 * c

    def div(refs, z, yl, f):
        x, y, w = (ld(r, z) for r in refs)
        return (x - ld(refs[0], z, -1)) + (y - ylo(y, yl, z, f)) + (w - ld(refs[2], z - 1))

    def grad(ref, z, yh, f):
        q = ld(ref, z)
        return ld(ref, z, 1) - q, yhi(q, yh, z, f) - q, ld(ref, z + 1) - q

    def s1(z, yl, yh):
        for c in range(3):
            bend0[c, z] = lap(V0[c], z, yl, yh, c)
            lm[c, z] = lap(MA[c], z, yl, yh, 3 + c)
        st(p1, z, p0[z] + div(V0, z, yl, 1))
        st(m1, z, ap[z] - 0.25 * div(A1, z, yl, 6))

    def s2(z, yh):
        gp, gm = grad(p1, z, yh, 0), grad(m1, z, yh, 1)
        g = ld(md, z)
        for c in range(3):
            st(V1[c], z, ld(V0[c], z) + 0.25 * (gp[c] + g * bend0[c, z]))
            new = ld(A1[c], z) + 0.25 * lm[c, z] - gm[c]
            st(A0[c], z, new)
            st(MA0[c], z, g * new)

    def s3(z, yl, yh):
        total = None
        for c in range(3):
            part = ld(A1[c], z) * lap(V1[c], z, yl, yh, c) + ld(A0[c], z) * bend0[c, z]
            total = part if total is None else total + part
            lm0[c, z] = lap(MA0[c], z, yl, yh, 3 + c)
        sh[z] = 0.25 * total
        st(m0, z, ld(m1, z) - 0.25 * div(A0, z, yl, 6))

    def s4(z, yh):
        gm = grad(m0, z, yh, 0)
        for c in range(3):
            out[c, z] = ld(A0[c], z) + 0.25 * lm0[c, z] - gm[c]

    def every(fn, unroll=1):
        def step(z, carry):
            fn(z)
            return carry
        lax.fori_loop(0, CZ, step, 0, unroll=unroll)

    def pack_y(dst, fields, last=None):
        def step(zz, carry):
            acc = jnp.zeros((CX, CY), F32)
            for g in range(8):
                for f, ref in enumerate(fields):
                    s = g * 16 + 2 * f + 1
                    acc = jnp.where((lane >> 1) == (s >> 1), pltpu.roll(ld(ref, g * 4 + zz), s, 1), acc)
            dst[zz] = acc
            return carry
        lax.fori_loop(0, 4, step, 0)
        if last is not None:
            dst[3] = jnp.where(lane >= CY - 2, pltpu.roll(ld(last, CZ), CY - 1, 1), dst[3])

    def face(ref, x):
        return ref[pl.ds(PITCH + 8 + x, CZ, stride=PITCH), :]

    def pack_x(dst, fields, x):
        for i, ref in enumerate(fields):
            dst[i * CZ:(i + 1) * CZ, :] = face(ref, x)

    def unpack_x(src, fields, x):
        for i, ref in enumerate(fields):
            ref[pl.ds(PITCH + 8 + x, CZ, stride=PITCH), :] = src[i * CZ:(i + 1) * CZ, :]

    def rows_of(pairs, x):
        return [(ref, (z + 1) * PITCH + 8 + x) for ref, z in pairs]

    def pack_rows(dst, pairs, x):
        for i, (ref, row) in enumerate(rows_of(pairs, x)):
            dst[i:i + 1, :] = ref[row:row + 1, :]

    def unpack_rows(src, pairs, x):
        for i, (ref, row) in enumerate(rows_of(pairs, x)):
            ref[row:row + 1, :] = src[i:i + 1, :]

    class Link:
        def __init__(self, src, dst, send, recv, device, sends, gets):
            self.copy = pltpu.make_async_remote_copy(
                src_ref=src, dst_ref=dst, send_sem=send, recv_sem=recv,
                device_id=device, device_id_type=MESH,
            )
            self.sends, self.gets = sends, gets

        def start(self):
            pl.when(self.sends)(self.copy.start)

        def arrive(self):
            pl.when(self.gets)(self.copy.wait_recv)

        def flush(self):
            pl.when(self.sends)(self.copy.wait_send)

    links = []
    counts = {"x": 0, "y": 0, "z": 0}

    def link(kind, src, dst, device, sends, gets):
        n = counts[kind]
        counts[kind] += 1
        ss, rs = {"x": (xs_sem, xr_sem), "y": (ys_sem, yr_sem), "z": (zs_sem, zr_sem)}[kind]
        made = Link(src, dst, ss.at[n], rs.at[n], device, sends, gets)
        links.append(made)
        return made

    def x_down(src, dst):
        return link("x", src, dst, (gx - 1, gy, gz), has_xm, has_xp)

    def x_up(src, dst):
        return link("x", src, dst, (gx + 1, gy, gz), has_xp, has_xm)

    def y_down(src, dst):
        return link("y", src, dst, (gx, gy - 1, gz), has_ym, has_yp)

    def y_up(src, dst):
        return link("y", src, dst, (gx, gy + 1, gz), has_yp, has_ym)

    def z_down(src, dst):
        return link("z", src, dst, (gx, gy, gz - 1), has_zm, has_zp)

    def z_up(src, dst):
        return link("z", src, dst, (gx, gy, gz + 1), has_zp, has_zm)

    def go(*those):
        for one in those:
            one.start()

    def got(*those):
        for one in those:
            one.arrive()

    for copy in loads[:2]:
        copy.wait()

    def weight(z):
        g = ld(md, z)
        for c in range(3):
            st(MA[c], z, g * ld(A1[c], z))

    every(weight)
    loads[2].wait()
    lo1 = V0 + MA
    pack_x(xa1, lo1, 0)
    pack_x(xb1, lo1 + [A1[0]], CX - 1)
    pack_y(ys1, lo1 + [A1[1]])

    pl.semaphore_wait(barrier, expected)

    zraw = [
        z_up(vel.at[:, CZ - 1], zl.at[0:3]),
        z_down(vel.at[:, 0], zu.at[0:3]),
        z_up(avel.at[:, CZ - 1], zl.at[3:6]),
        z_down(avel.at[:, 0], zu.at[3:6]),
        z_up(modulus.at[CZ - 1], zl.at[6]),
        z_down(modulus.at[0], zu.at[6]),
    ]
    r1x = [x_down(xa1, xh1), x_up(xb1, xl1)]
    r1y = [y_down(ys1, yh1), y_up(ys1, yl1)]
    go(*r1x, *r1y, *zraw)

    stage1 = []
    for step in range(1, NGY):
        other = lax.rem(gy + step, NGY)
        stage1.append(
            pltpu.make_async_remote_copy(
                src_ref=cs.at[pl.ds(pl.multiple_of(other * 32, 32), 32)],
                dst_ref=gath.at[mine],
                send_sem=f1s.at[step - 1], recv_sem=f1r.at[step - 1],
                device_id=(gx, other, gz), device_id_type=MESH,
            )
        )
        stage1[-1].start()

    loads[3].wait()
    loads[4].wait()
    got(*r1x, *r1y)

    @pl.when(has_xp)
    def _():
        unpack_x(xh1, lo1, CX)

    @pl.when(has_xm)
    def _():
        unpack_x(xl1, lo1 + [A1[0]], -1)

    every(lambda z: s1(z, yl1, yh1))
    pack_x(xa2, [p1, m1], 0)
    r2x = x_down(xa2, xh2)
    go(r2x)
    pack_y(ys2, [p1, m1])
    r2y = y_down(ys2, yh2)
    zpm = [
        z_down(p1.at[pl.ds(PITCH + 8, CX)], zu.at[13]),
        z_down(m1.at[pl.ds(PITCH + 8, CX)], zu.at[14]),
    ]
    go(r2y, *zpm)

    for copy in stage1:
        copy.wait_recv()
    rows = gath[...]
    r256 = lax.broadcasted_iota(jnp.int32, (256, CY), 0)
    l256 = lax.broadcasted_iota(jnp.int32, (256, CY), 1)
    codes = pltpu.roll(rows, 252, 0)
    hot = jnp.where(((r256 & 7) < 4) & (codes == (l256 + 1).astype(F32)), 1.0, 0.0)
    dense[...] = lax.dot_general(
        hot, rows, (((0,), (0,)), ((), ())), precision=HIGH, preferred_element_type=F32
    )
    stage2 = []
    for step in range(1, NGX):
        other = lax.rem(gx + step, NGX)
        stage2.append(
            pltpu.make_async_remote_copy(
                src_ref=dense.at[pl.ds(pl.multiple_of(other * 32, 32), 32)],
                dst_ref=hsum.at[step - 1],
                send_sem=f2s.at[step - 1], recv_sem=f2r.at[step - 1],
                device_id=(other, gy, gz), device_id_type=MESH,
            )
        )
        stage2[-1].start()

    got(r2x, r2y)

    @pl.when(has_xp)
    def _():
        unpack_x(xh2, [p1, m1], CX)

    every(lambda z: s2(z, yh2))

    lo3 = V1 + MA0
    pack_x(xa3, lo3, 0)
    pack_x(xb3, lo3 + [A0[0]], CX - 1)
    r3x = [x_down(xa3, xh3), x_up(xb3, xl3)]
    go(*r3x)
    pack_y(ys3, lo3 + [A0[1]])
    r3y = [y_down(ys3, yh3), y_up(ys3, yl3)]
    go(*r3y)
    first, final = pl.ds(PITCH + 8, CX), pl.ds(CZ * PITCH + 8, CX)
    zpart = [
        z_up(v1.at[:, final], zl.at[7:10]),
        z_down(v1.at[:, first], zu.at[7:10]),
        z_up(a0.at[:, final], zl.at[10:13]),
        z_down(a0.at[:, first], zu.at[10:13]),
    ]
    go(*zpart)

    for copy in stage2:
        copy.wait_recv()
    own = dense[pl.ds(pl.multiple_of(gx * 32, 32), 32), :]
    esum[...] = own + hsum[0] + hsum[1] + hsum[2]

    @pl.when(gz > 0)
    def _():
        to_surface = pltpu.make_async_remote_copy(
            src_ref=esum, dst_ref=ksum.at[gz - 1], send_sem=f3s, recv_sem=f3r.at[gz - 1],
            device_id=(gx, gy, 0), device_id_type=MESH,
        )
        to_surface.start()

    got(*r3x, *r3y)

    @pl.when(has_xp)
    def _():
        unpack_x(xh3, lo3, CX)

    @pl.when(has_xm)
    def _():
        unpack_x(xl3, lo3 + [A0[0]], -1)

    every(lambda z: s3(z, yl3, yh3))
    pack_x(xa4, [m0], 0)
    r4x = x_down(xa4, xh4)
    go(r4x)
    pack_y(ys4, [m0])
    r4y = y_down(ys4, yh4)
    go(r4y)
    got(r4x, r4y)

    @pl.when(has_xp)
    def _():
        unpack_x(xh4, [m0], CX)

    every(lambda z: s4(z, yh4))
    middle = pl.ds(3, CZ - 5)
    early = [
        pltpu.make_async_copy(out.at[:, middle], o_av.at[:, middle], out_sem.at[0]),
        pltpu.make_async_copy(
            m0.reshape(LAYERS, PITCH, CY).at[pl.ds(4, CZ - 5), pl.ds(8, CX), :], o_ap.at[middle], out_sem.at[1]
        ),
        pltpu.make_async_copy(sh.at[middle], o_sh.at[middle], out_sem.at[2]),
    ]
    for copy in early:
        copy.start()

    surface = gz == 0
    r5x = [
        link("x", xa5, xh5, (gx - 1, gy, gz), surface & has_xm, surface & has_xp),
        link("x", xb5, xl5, (gx + 1, gy, gz), surface & has_xp, surface & has_xm),
    ]
    r5y = [
        link("y", ys5, yh5, (gx, gy - 1, gz), surface & has_ym, surface & has_yp),
        link("y", ys5, yl5, (gx, gy + 1, gz), surface & has_yp, surface & has_ym),
    ]

    @pl.when(surface)
    def _():
        for other in range(1, NGZ):
            pltpu.make_async_remote_copy(
                src_ref=esum, dst_ref=ksum.at[other - 1], send_sem=f3s, recv_sem=f3r.at[other - 1],
                device_id=(gx, gy, 1), device_id_type=MESH,
            ).wait_recv()
        total = esum[...]
        for other in range(1, NGZ):
            total = total + ksum[other - 1]
        esum[...] = total
        w = ld(A1[2], 0) + total[CX:2 * CX]
        st(A1[2], 0, w)
        w = w * ld(md, 0)
        st(MA[2], 0, w)
        pack_rows(xa5, [(MA[2], 0)], 0)
        pack_rows(xb5, [(MA[2], 0)], CX - 1)
        ys5[...] = pltpu.roll(w, 11, 1)

    go(*r5x, *r5y)
    got(*r5x, *r5y)

    @pl.when(surface & has_xp)
    def _():
        unpack_rows(xh5, [(MA[2], 0)], CX)

    @pl.when(surface & has_xm)
    def _():
        unpack_rows(xl5, [(MA[2], 0)], -1)

    @pl.when(surface & has_yp)
    def _():
        yh1[0] = jnp.where(lane == 11, yh5[...], yh1[0])

    @pl.when(surface & has_ym)
    def _():
        yl1[0] = jnp.where(lane == 10, yl5[...], yl1[0])

    for one in zpart + zpm:
        one.flush()
    got(*zraw, *zpm, *zpart)

    @pl.when(has_zm)
    def _():
        for c in range(3):
            st(V0[c], -1, zl[c])
            st(MA[c], -1, zl[6] * zl[3 + c])
        st(A1[2], -1, zl[5])

    @pl.when(has_zp)
    def _():
        for c in range(3):
            st(V0[c], CZ, zu[c])
            st(MA[c], CZ, zu[6] * zu[3 + c])
        st(p1, CZ, zu[13] - ld(V0[2], CZ - 1))
        st(m1, CZ, zu[14] + 0.25 * ld(A1[2], CZ - 1))

    def some(fn, layers):
        for z in layers:
            fn(z)

    some(lambda z: s1(z, yl1, yh1), (0, 1, CZ - 1))
    x6 = [(p1, 0), (m1, 0), (m1, 1), (A1[2], CZ - 1)]
    pack_rows(xa6, x6, 0)
    r6x = x_down(xa6, xh6)
    go(r6x)
    pack_y(ys6, [p1, m1, A1[2]])
    r6y = y_down(ys6, yh6)
    go(r6y)
    got(r6x, r6y)

    @pl.when(has_xp)
    def _():
        unpack_rows(xh6, x6, CX)

    some(lambda z: s2(z, yh6), (0, 1, CZ - 1))

    @pl.when(surface)
    def _():
        w = ld(A0[2], 0) + esum[0:CX, :]
        st(A0[2], 0, w)
        st(MA0[2], 0, w * ld(md, 0))

    @pl.when(has_zm)
    def _():
        g = zl[6]
        extra_v, extra_a = ld(p1, 0), ld(m1, 0)
        for c in range(3):
            v = g * ld(V0[c], 0)
            a = 0.25 * ld(MA[c], 0)
            if c == 2:
                v, a = v + extra_v, a - extra_a
            st(V1[c], -1, zl[7 + c] + 0.25 * v)
            a = zl[10 + c] + a
            st(A0[c], -1, a)
            st(MA0[c], -1, g * a)

    @pl.when(has_zp)
    def _():
        g = zu[6]
        top = CZ - 1
        q, w = ld(V0[2], top), ld(A1[2], top)
        gq = (ld(V0[2], top, 1) - q, yhi(q, yh1, top, 2) - q, -q)
        gw = (ld(A1[2], top, 1) - w, yhi(w, yh6, top, 2) - w, -w)
        for c in range(3):
            st(V1[c], CZ, zu[7 + c] + 0.25 * (g * ld(V0[c], top) - gq[c]))
            a = zu[10 + c] + 0.25 * (ld(MA[c], top) - gw[c])
            st(A0[c], CZ, a)
            st(MA0[c], CZ, g * a)

    x7 = [(ref, z) for ref in lo3 for z in (0, 1, CZ - 1)]
    x7up = x7 + [(A0[0], z) for z in (0, 1, CZ - 1, CZ)]
    pack_rows(xa7, x7, 0)
    pack_rows(xb7, x7up, CX - 1)
    r7x = [x_down(xa7, xh7), x_up(xb7, xl7)]
    go(*r7x)
    pack_y(ys7, lo3 + [A0[1]], last=A0[1])
    r7y = [y_down(ys7, yh7), y_up(ys7, yl7)]
    go(*r7y)
    got(*r7x, *r7y)

    @pl.when(has_xp)
    def _():
        unpack_rows(xh7, x7, CX)

    @pl.when(has_xm)
    def _():
        unpack_rows(xl7, x7up, -1)

    edges = (0, 1, 2, CZ - 2, CZ - 1)
    some(lambda z: s3(z, yl7, yh7), edges)

    @pl.when(has_zp)
    def _():
        x, y, w = (ld(r, CZ) for r in A0)
        low = jnp.where(lane == 0, pltpu.roll(yl7[3], 2, 1), pltpu.roll(y, 1, 1))
        d = (x - ld(A0[0], CZ, -1)) + (y - low) + (w - ld(A0[2], CZ - 1))
        st(m0, CZ, ld(m1, CZ) - 0.25 * d)

    x8 = [(m0, z) for z in (0, 1, 2, CZ - 1)]
    pack_rows(xa8, x8, 0)
    r8x = x_down(xa8, xh8)
    go(r8x)
    pack_y(ys8, [m0])
    r8y = y_down(ys8, yh8)
    go(r8y)
    got(r8x, r8y)

    @pl.when(has_xp)
    def _():
        unpack_rows(xh8, x8, CX)

    some(lambda z: s4(z, yh8), edges)
    late = []
    for n, (start, size) in enumerate(((0, 3), (CZ - 2, 2))):
        part = pl.ds(start, size)
        late += [
            pltpu.make_async_copy(out.at[:, part], o_av.at[:, part], out_sem.at[3 + 3 * n]),
            pltpu.make_async_copy(
                m0.reshape(LAYERS, PITCH, CY).at[pl.ds(start + 1, size), pl.ds(8, CX), :],
                o_ap.at[part], out_sem.at[4 + 3 * n],
            ),
            pltpu.make_async_copy(sh.at[part], o_sh.at[part], out_sem.at[5 + 3 * n]),
        ]
    for copy in late:
        copy.start()
    for one in links:
        if one not in zpart and one not in zpm:
            one.flush()
    for copy in stage1 + stage2:
        copy.wait_send()

    @pl.when(gz > 0)
    def _():
        pltpu.make_async_remote_copy(
            src_ref=esum, dst_ref=ksum.at[gz - 1], send_sem=f3s, recv_sem=f3r.at[gz - 1],
            device_id=(gx, gy, 0), device_id_type=MESH,
        ).wait_send()

    for copy in early + late:
        copy.wait()


def shards(vel, pres, modulus, avel, apres, svals, sowner, sline, sstep):
    vector = pltpu.VMEM((3, ROWS, CY), F32)
    scalar = pltpu.VMEM((ROWS, CY), F32)
    flat3 = pltpu.VMEM((3, CZ, CX, CY), F32)
    flat = pltpu.VMEM((CZ, CX, CY), F32)
    pack = pltpu.VMEM((4, CX, CY), F32)
    plane = pltpu.VMEM((CX, CY), F32)

    def lines(n):
        return pltpu.VMEM((n, CY), F32)

    def dma(n):
        return pltpu.SemaphoreType.DMA((n,))

    anywhere, inside = pl.BlockSpec(memory_space=pl.ANY), pl.BlockSpec(memory_space=pltpu.VMEM)
    return pl.pallas_call(
        body,
        out_shape=(
            jax.ShapeDtypeStruct((3, CZ, CX, CY), F32),
            jax.ShapeDtypeStruct((CZ, CX, CY), F32),
            jax.ShapeDtypeStruct((CZ, CX, CY), F32),
        ),
        in_specs=[anywhere] * 5 + [inside] * 4,
        out_specs=(anywhere,) * 3,
        scratch_shapes=[
            vector, vector, vector, scalar, scalar, scalar, vector, vector, vector, scalar,
            flat, flat, flat3, flat3, flat3, flat, flat3,
            pack, pack, pack, pack, pack, pack, pack, pack, pack, pack,
            plane, plane, plane, pack, pack, pack, pack, pack, pack, pack,
            lines(6 * CZ), lines(7 * CZ), lines(6 * CZ), lines(7 * CZ),
            lines(2 * CZ), lines(2 * CZ),
            lines(6 * CZ), lines(7 * CZ), lines(6 * CZ), lines(7 * CZ),
            lines(CZ), lines(CZ),
            lines(8), lines(8), lines(8), lines(8), lines(8), lines(8),
            lines(24), lines(24), lines(24), lines(24), lines(8), lines(8),
            pltpu.VMEM((13, CX, CY), F32), pltpu.VMEM((15, CX, CY), F32),
            lines(256), lines(256), lines(CY), pltpu.VMEM((3, 32, CY), F32), lines(32),
            pltpu.VMEM((NGZ - 1, 32, CY), F32),
            dma(5), dma(9), dma(12), dma(12), dma(12), dma(12), dma(12), dma(12),
            dma(NGY - 1), dma(NGY - 1), dma(NGX - 1), dma(NGX - 1),
            pltpu.SemaphoreType.DMA, dma(NGZ - 1),
        ],
        compiler_params=pltpu.CompilerParams(
            collective_id=0, has_side_effects=True, vmem_limit_bytes=48 * 2**20
        ),
        cost_estimate=pl.CostEstimate(flops=20_000_000, bytes_accessed=3_670_016, transcendentals=0),
        name="adjoint",
    )(vel, pres, modulus, avel, apres, svals, sowner, sline.reshape(1, 32), sstep.reshape(1, 32))


def solution(mesh):
    return jax.shard_map(
        shards,
        mesh=mesh,
        in_specs=(
            P(None, "gz", "gx", "gy"),
            P("gz", "gx", "gy"),
            P("gz", "gx", "gy"),
            P(None, "gz", "gx", "gy"),
            P("gz", "gx", "gy"),
            P(("gx", "gy", "gz"), None),
            P(("gx", "gy", "gz"), None),
            P(("gx", "gy", "gz")),
            P(("gx", "gy", "gz")),
        ),
        out_specs=(P(None, "gz", "gx", "gy"), P("gz", "gx", "gy"), P("gz", "gx", "gy")),
        check_vma=False,
    )
```

```python
import jax
import jax.numpy as jnp
from jax import lax
from jax.experimental import pallas as pl
from jax.experimental.pallas import tpu as pltpu
from jax.sharding import PartitionSpec as P

MESH = pl.DeviceIdType.MESH
F32 = jnp.float32
CZ, CX, CY = 32, 16, 128
PITCH = 32
LAYERS = CZ + 2
ROWS = LAYERS * PITCH
NGX, NGY, NGZ = 4, 8, 8
UNROLL = 4
HIGH = lax.Precision.HIGHEST


def body(
    vel, pres, modulus, avel, apres, svals_h, sowner_h, sline_h, sstep_h,
    o_av, o_ap, o_sh,
    v0, a1, ma, md, p1, m1, v1, a0, ma0, m0,
    p0, ap, bend0, lm, lm0, sh, out,
    ys1, yl1, yh1, ys2, yh2, ys3, yl3, yh3, ys4, yh4,
    c1, c3, c7, ys9, yh9, xa9, xb9, xl9, xh9, xa10, xh10,
    ys5, yl5, yh5, ys6, yh6, ys7, yl7, yh7, ys8, yh8,
    xa1, xb1, xh1, xl1, xa2, xh2, xa3, xb3, xh3, xl3, xa4, xh4,
    xa5, xb5, xh5, xl5, xa6, xh6, xa7, xb7, xh7, xl7, xa8, xh8,
    svals, sowner, sline, sstep,
    zl, zu, cs, gath, dense, hsum, esum, ksum,
    in_sem, out_sem, xs_sem, xr_sem, ys_sem, yr_sem, zs_sem, zr_sem,
    f1s, f1r, f2s, f2r, f3s, f3r,
):
    gx, gy, gz = lax.axis_index("gx"), lax.axis_index("gy"), lax.axis_index("gz")
    has_xm, has_xp = gx > 0, gx < NGX - 1
    has_ym, has_yp = gy > 0, gy < NGY - 1
    has_zm, has_zp = gz > 0, gz < NGZ - 1
    barrier = pltpu.get_barrier_semaphore()

    def grid3(ref):
        if len(ref.shape) == 3:
            return ref.reshape(3, LAYERS, PITCH, CY).at[:, pl.ds(1, CZ), pl.ds(8, CX), :]
        return ref.reshape(LAYERS, PITCH, CY).at[pl.ds(1, CZ), pl.ds(8, CX), :]

    loads = [
        pltpu.make_async_copy(src, dst, in_sem.at[i])
        for i, (src, dst) in enumerate(
            [(avel, grid3(a1)), (modulus, grid3(md)), (vel, grid3(v0)), (pres, p0), (apres, ap)]
        )
    ]
    sensors = [
        pltpu.make_async_copy(src, dst, in_sem.at[5 + i])
        for i, (src, dst) in enumerate(
            [(svals_h, svals), (sowner_h, sowner), (sline_h, sline), (sstep_h, sstep)]
        )
    ]
    for copy in loads + sensors:
        copy.start()

    lane = lax.broadcasted_iota(jnp.int32, (CX, CY), 1)

    @pl.when(jnp.logical_not(has_ym))
    def _():
        for ref in (yl1, yl3, yl7):
            ref[...] = jnp.zeros(ref.shape, F32)
        yl5[...] = jnp.zeros(yl5.shape, F32)

    @pl.when(jnp.logical_not(has_yp))
    def _():
        for ref in (yh1, yh2, yh3, yh4, yh6, yh7, yh8, yh9):
            ref[...] = jnp.zeros(ref.shape, F32)
        yh5[...] = jnp.zeros(yh5.shape, F32)

    def greet(device):
        pl.semaphore_signal(barrier, inc=1, device_id=device, device_id_type=MESH)

    @pl.when(has_zm)
    def _():
        greet((gx, gy, gz - 1))

    @pl.when(has_zp)
    def _():
        greet((gx, gy, gz + 1))

    @pl.when(gz == 0)
    def _():
        for other in range(2, NGZ):
            greet((gx, gy, other))

    for step in range(1, NGY):
        greet((gx, lax.rem(gy + step, NGY), gz))
    for step in range(1, NGX):
        greet((lax.rem(gx + step, NGX), gy, gz))
    expected = (
        NGX - 1 + NGY - 1
        + has_zm.astype(jnp.int32) + has_zp.astype(jnp.int32) + (gz >= 2).astype(jnp.int32)
    )

    def comps(ref):
        return [ref.at[c] for c in range(3)]

    V0, A1, MA, V1, A0, MA0 = (comps(r) for r in (v0, a1, ma, v1, a0, ma0))

    zeros_layer = jnp.zeros((PITCH, CY), F32)
    zeros_rows = jnp.zeros((LAYERS, CY), F32)
    for ref in V0 + A1 + MA + V1 + A0 + MA0 + [p1, m1, m0]:
        ref[0:PITCH, :] = zeros_layer
        ref[ROWS - PITCH:ROWS, :] = zeros_layer

    @pl.when(jnp.logical_not(has_xm))
    def _():
        for ref in V0 + [A1[0]] + MA + V1 + [A0[0]] + MA0:
            ref[pl.ds(7, LAYERS, stride=PITCH), :] = zeros_rows

    @pl.when(jnp.logical_not(has_xp))
    def _():
        for ref in V0 + MA + [A1[2]] + V1 + MA0 + [p1, m1, m0]:
            ref[pl.ds(24, LAYERS, stride=PITCH), :] = zeros_rows

    def ld(ref, z, dx=0):
        return ref[pl.ds((z + 1) * PITCH + 8 + dx, CX), :]

    def st(ref, z, value):
        ref[pl.ds(pl.multiple_of((z + 1) * PITCH + 8, 8), CX), :] = value

    def halo(blk, z, f):
        return pltpu.roll(blk[z & 3], (CY - ((z >> 2) * 16 + 2 * f)) & (CY - 1), 1)

    def ylo(u, blk, z, f):
        return jnp.where(lane == 0, halo(blk, z, f), pltpu.roll(u, 1, 1))

    def yhi(u, blk, z, f):
        shift = CY - 2 - (z >> 2) * 16 - 2 * f
        return jnp.where(lane == CY - 1, pltpu.roll(blk[z & 3], shift, 1), pltpu.roll(u, CY - 1, 1))

    def merge(dst, low, high, planes=range(4)):
        for zz in planes:
            dst[zz] = jnp.where((lane & 1) == 0, low[zz], pltpu.roll(high[zz], CY - 2, 1))

    def lap(ref, z, blk, f):
        c = ld(ref, z)
        h = halo(blk, z, f)
        low = jnp.where(lane == 0, h, pltpu.roll(c, 1, 1))
        high = jnp.where(lane == CY - 1, h, pltpu.roll(c, CY - 1, 1))
        total = ld(ref, z, 1) + ld(ref, z, -1) + (ld(ref, z + 1) + ld(ref, z - 1))
        return total + (low + high) - 6.0 * c, low

    def div(refs, z, low):
        x, y, w = (ld(r, z) for r in refs)
        return (x - ld(refs[0], z, -1)) + (y - low) + (w - ld(refs[2], z - 1))

    def grad(ref, z, yh, f):
        q = ld(ref, z)
        return ld(ref, z, 1) - q, yhi(q, yh, z, f) - q, ld(ref, z + 1) - q

    def s1(z, blk):
        lows = []
        for c in range(3):
            bend0[c, z], low = lap(V0[c], z, blk, c)
            lows.append(low)
            lm[c, z], _ = lap(MA[c], z, blk, 3 + c)
        st(p1, z, p0[z] + div(V0, z, lows[1]))
        st(m1, z, ap[z] - 0.25 * div(A1, z, ylo(ld(A1[1], z), blk, z, 6)))

    def s2(z, yh):
        gp, gm = grad(p1, z, yh, 0), grad(m1, z, yh, 1)
        g = ld(md, z)
        for c in range(3):
            st(V1[c], z, ld(V0[c], z) + 0.25 * (gp[c] + g * bend0[c, z]))
            new = ld(A1[c], z) + 0.25 * lm[c, z] - gm[c]
            st(A0[c], z, new)
            st(MA0[c], z, g * new)

    def s3(z, blk):
        total = None
        for c in range(3):
            part = ld(A1[c], z) * lap(V1[c], z, blk, c)[0] + ld(A0[c], z) * bend0[c, z]
            total = part if total is None else total + part
            lm0[c, z], _ = lap(MA0[c], z, blk, 3 + c)
        sh[z] = 0.25 * total
        st(m0, z, ld(m1, z) - 0.25 * div(A0, z, ylo(ld(A0[1], z), blk, z, 6)))

    def s4(z, yh):
        gm = grad(m0, z, yh, 0)
        for c in range(3):
            out[c, z] = ld(A0[c], z) + 0.25 * lm0[c, z] - gm[c]

    def every(fn, start=0, stop=CZ, unroll=UNROLL):
        turns = (stop - start) // unroll

        def step(n, carry):
            for k in range(unroll):
                fn(start + n * unroll + k)
            return carry

        lax.fori_loop(0, turns, step, 0)
        for z in range(start + turns * unroll, stop):
            fn(z)

    def some(fn, layers):
        for z in layers:
            fn(z)

    def pack_y(dst, fields):
        def step(zz, carry):
            acc = jnp.zeros((CX, CY), F32)
            for g in range(8):
                for f, ref in enumerate(fields):
                    s = g * 16 + 2 * f + 1
                    acc = jnp.where((lane >> 1) == (s >> 1), pltpu.roll(ld(ref, g * 4 + zz), s, 1), acc)
            dst[zz] = acc
            return carry
        lax.fori_loop(0, 4, step, 0)

    def pack_layers(dst, fields, layers, last=None):
        for zz in range(4):
            acc = jnp.zeros((CX, CY), F32)
            for z in layers:
                if z % 4 == zz:
                    for f, ref in enumerate(fields):
                        s = (z // 4) * 16 + 2 * f + 1
                        acc = jnp.where((lane >> 1) == (s >> 1), pltpu.roll(ld(ref, z), s, 1), acc)
            if zz == 3 and last is not None:
                acc = jnp.where(lane >= CY - 2, pltpu.roll(ld(last, CZ), CY - 1, 1), acc)
            dst[zz] = acc

    def face(ref, x):
        return ref[pl.ds(PITCH + 8 + x, CZ, stride=PITCH), :]

    def pack_x(dst, fields, x):
        for i, ref in enumerate(fields):
            dst[i * CZ:(i + 1) * CZ, :] = face(ref, x)

    def unpack_x(src, fields, x):
        for i, ref in enumerate(fields):
            ref[pl.ds(PITCH + 8 + x, CZ, stride=PITCH), :] = src[i * CZ:(i + 1) * CZ, :]

    def rows_of(pairs, x):
        return [(ref, (z + 1) * PITCH + 8 + x) for ref, z in pairs]

    def pack_rows(dst, pairs, x):
        for i, (ref, row) in enumerate(rows_of(pairs, x)):
            dst[i:i + 1, :] = ref[row:row + 1, :]

    def unpack_rows(src, pairs, x):
        for i, (ref, row) in enumerate(rows_of(pairs, x)):
            ref[row:row + 1, :] = src[i:i + 1, :]

    def store(start, size, n):
        part = pl.ds(start, size)
        copies = [
            pltpu.make_async_copy(out.at[:, part], o_av.at[:, part], out_sem.at[3 * n]),
            pltpu.make_async_copy(
                m0.reshape(LAYERS, PITCH, CY).at[pl.ds(start + 1, size), pl.ds(8, CX), :],
                o_ap.at[part], out_sem.at[3 * n + 1],
            ),
            pltpu.make_async_copy(sh.at[part], o_sh.at[part], out_sem.at[3 * n + 2]),
        ]
        for copy in copies:
            copy.start()
        return copies

    class Link:
        def __init__(self, src, dst, send, recv, device, sends, gets):
            self.copy = pltpu.make_async_remote_copy(
                src_ref=src, dst_ref=dst, send_sem=send, recv_sem=recv,
                device_id=device, device_id_type=MESH,
            )
            self.sends, self.gets = sends, gets

        def start(self):
            pl.when(self.sends)(self.copy.start)

        def arrive(self):
            pl.when(self.gets)(self.copy.wait_recv)

        def flush(self):
            pl.when(self.sends)(self.copy.wait_send)

    links = []
    counts = {"x": 0, "y": 0, "z": 0}

    def link(kind, src, dst, device, sends, gets):
        n = counts[kind]
        counts[kind] += 1
        ss, rs = {"x": (xs_sem, xr_sem), "y": (ys_sem, yr_sem), "z": (zs_sem, zr_sem)}[kind]
        made = Link(src, dst, ss.at[n], rs.at[n], device, sends, gets)
        links.append(made)
        return made

    def x_down(src, dst):
        return link("x", src, dst, (gx - 1, gy, gz), has_xm, has_xp)

    def x_up(src, dst):
        return link("x", src, dst, (gx + 1, gy, gz), has_xp, has_xm)

    def y_down(src, dst):
        return link("y", src, dst, (gx, gy - 1, gz), has_ym, has_yp)

    def y_up(src, dst):
        return link("y", src, dst, (gx, gy + 1, gz), has_yp, has_ym)

    def z_down(src, dst):
        return link("z", src, dst, (gx, gy, gz - 1), has_zm, has_zp)

    def z_up(src, dst):
        return link("z", src, dst, (gx, gy, gz + 1), has_zp, has_zm)

    def go(*those):
        for one in those:
            one.start()

    def got(*those):
        for one in those:
            one.arrive()

    for copy in loads:
        copy.wait()

    def weight(z):
        g = ld(md, z)
        for c in range(3):
            st(MA[c], z, g * ld(A1[c], z))

    every(weight)
    lo1 = V0 + MA
    rim = (0, 1, CZ - 1)
    x9 = [(ref, z) for ref in lo1 for z in rim]
    x9up = x9 + [(A1[0], z) for z in rim]
    pack_rows(xa9, x9, 0)
    pack_rows(xb9, x9up, CX - 1)
    pack_y(ys1, lo1 + [A1[1]])

    pl.semaphore_wait(barrier, expected)

    r9x = [x_down(xa9, xh9), x_up(xb9, xl9)]
    r1y = [y_down(ys1, yh1), y_up(ys1, yl1)]
    r1x = [x_down(xa1, xh1), x_up(xb1, xl1)]
    zraw = [
        z_up(vel.at[:, CZ - 1], zl.at[0:3]),
        z_down(vel.at[:, 0], zu.at[0:3]),
        z_up(avel.at[:, CZ - 1], zl.at[3:6]),
        z_down(avel.at[:, 0], zu.at[3:6]),
        z_up(modulus.at[CZ - 1], zl.at[6]),
        z_down(modulus.at[0], zu.at[6]),
    ]
    go(*r9x, *r1y, *zraw)
    pack_x(xa1, lo1, 0)
    pack_x(xb1, lo1 + [A1[0]], CX - 1)
    go(*r1x)

    for copy in sensors:
        copy.wait()
    owner_row = sowner[...].astype(F32)
    r0 = lax.broadcasted_iota(jnp.int32, (32, 32), 0)
    r1 = lax.broadcasted_iota(jnp.int32, (32, 32), 1)
    owner_col = jnp.sum(jnp.where(r0 == r1, owner_row, 0.0), axis=1, keepdims=True)
    rank = jnp.sum(
        jnp.where((owner_col == owner_row) & (r0 < r1), 1.0, 0.0), axis=0, keepdims=True
    ).astype(jnp.int32)
    owner_int = owner_row.astype(jnp.int32)
    own_gx, own_gy = owner_int >> 3, owner_int & 7
    place = own_gy * 32 + own_gx * 8 + rank
    code_row = (own_gx * 32 + sstep[...] * CX + sline[...] + 1).astype(F32)
    code_col = jnp.sum(jnp.where(r0 == r1, code_row, 0.0), axis=1, keepdims=True)
    slot = lax.broadcasted_iota(jnp.int32, (256, 32), 0)
    cs[...] = jnp.dot(
        (slot == place).astype(F32), svals[...], precision=HIGH, preferred_element_type=F32
    ) + jnp.dot(
        (slot == place + 4).astype(F32), jnp.broadcast_to(code_col, (32, CY)),
        precision=HIGH, preferred_element_type=F32,
    )
    mine = pl.ds(pl.multiple_of(gy * 32, 32), 32)
    gath[mine, :] = cs[mine, :]

    stage1 = []
    for step in range(1, NGY):
        other = lax.rem(gy + step, NGY)
        stage1.append(
            pltpu.make_async_remote_copy(
                src_ref=cs.at[pl.ds(pl.multiple_of(other * 32, 32), 32)],
                dst_ref=gath.at[mine],
                send_sem=f1s.at[step - 1], recv_sem=f1r.at[step - 1],
                device_id=(gx, other, gz), device_id_type=MESH,
            )
        )
        stage1[-1].start()

    got(*r9x, *r1y)

    @pl.when(has_xp)
    def _():
        unpack_rows(xh9, x9, CX)

    @pl.when(has_xm)
    def _():
        unpack_rows(xl9, x9up, -1)

    merge(c1, yl1, yh1)
    some(lambda z: s1(z, c1), rim)
    x10 = [(ref, z) for ref in (p1, m1) for z in (0, CZ - 1)]
    pack_rows(xa10, x10, 0)
    r10x = x_down(xa10, xh10)
    go(r10x)
    pack_layers(ys9, [p1, m1], (0, CZ - 1))
    r9y = y_down(ys9, yh9)
    zpm = [
        z_down(p1.at[pl.ds(PITCH + 8, CX)], zu.at[13]),
        z_down(m1.at[pl.ds(PITCH + 8, CX)], zu.at[14]),
    ]
    go(r9y, *zpm)
    got(r10x, r9y)

    @pl.when(has_xp)
    def _():
        unpack_rows(xh10, x10, CX)

    some(lambda z: s2(z, yh9), (0, CZ - 1))
    first, final = pl.ds(PITCH + 8, CX), pl.ds(CZ * PITCH + 8, CX)
    zpart = [
        z_up(v1.at[:, final], zl.at[7:10]),
        z_down(v1.at[:, first], zu.at[7:10]),
        z_up(a0.at[:, final], zl.at[10:13]),
        z_down(a0.at[:, first], zu.at[10:13]),
    ]
    go(*zpart)

    for copy in stage1:
        copy.wait_recv()
    rows = gath[...]
    r256 = lax.broadcasted_iota(jnp.int32, (256, CY), 0)
    l256 = lax.broadcasted_iota(jnp.int32, (256, CY), 1)
    codes = pltpu.roll(rows, 252, 0)
    hot = jnp.where(((r256 & 7) < 4) & (codes == (l256 + 1).astype(F32)), 1.0, 0.0)
    dense[...] = lax.dot_general(
        hot, rows, (((0,), (0,)), ((), ())), precision=HIGH, preferred_element_type=F32
    )
    stage2 = []
    for step in range(1, NGX):
        other = lax.rem(gx + step, NGX)
        stage2.append(
            pltpu.make_async_remote_copy(
                src_ref=dense.at[pl.ds(pl.multiple_of(other * 32, 32), 32)],
                dst_ref=hsum.at[step - 1],
                send_sem=f2s.at[step - 1], recv_sem=f2r.at[step - 1],
                device_id=(other, gy, gz), device_id_type=MESH,
            )
        )
        stage2[-1].start()

    got(*r1x)

    @pl.when(has_xp)
    def _():
        unpack_x(xh1, lo1, CX)

    @pl.when(has_xm)
    def _():
        unpack_x(xl1, lo1 + [A1[0]], -1)

    every(lambda z: s1(z, c1), 2, CZ - 1)
    pack_x(xa2, [p1, m1], 0)
    r2x = x_down(xa2, xh2)
    go(r2x)
    pack_y(ys2, [p1, m1])
    r2y = y_down(ys2, yh2)
    go(r2y)

    for copy in stage2:
        copy.wait_recv()
    own = dense[pl.ds(pl.multiple_of(gx * 32, 32), 32), :]
    esum[...] = own + hsum[0] + hsum[1] + hsum[2]

    @pl.when(gz > 0)
    def _():
        to_surface = pltpu.make_async_remote_copy(
            src_ref=esum, dst_ref=ksum.at[gz - 1], send_sem=f3s, recv_sem=f3r.at[gz - 1],
            device_id=(gx, gy, 0), device_id_type=MESH,
        )
        to_surface.start()

    got(r2x, r2y)

    @pl.when(has_xp)
    def _():
        unpack_x(xh2, [p1, m1], CX)

    every(lambda z: s2(z, yh2), 1, CZ - 1)

    lo3 = V1 + MA0
    pack_x(xa3, lo3, 0)
    pack_x(xb3, lo3 + [A0[0]], CX - 1)
    r3x = [x_down(xa3, xh3), x_up(xb3, xl3)]
    pack_y(ys3, lo3 + [A0[1]])
    r3y = [y_down(ys3, yh3), y_up(ys3, yl3)]
    go(*r3y)

    for one in zpart + zpm:
        one.flush()
    got(*zraw, *zpm)

    surface = gz == 0
    r5x = [
        link("x", xa5, xh5, (gx - 1, gy, gz), surface & has_xm, surface & has_xp),
        link("x", xb5, xl5, (gx + 1, gy, gz), surface & has_xp, surface & has_xm),
    ]
    r5y = [
        link("y", ys5, yh5, (gx, gy - 1, gz), surface & has_ym, surface & has_yp),
        link("y", ys5, yl5, (gx, gy + 1, gz), surface & has_yp, surface & has_ym),
    ]

    @pl.when(surface)
    def _():
        for other in range(1, NGZ):
            pltpu.make_async_remote_copy(
                src_ref=esum, dst_ref=ksum.at[other - 1], send_sem=f3s, recv_sem=f3r.at[other - 1],
                device_id=(gx, gy, 1), device_id_type=MESH,
            ).wait_recv()
        total = esum[...]
        for other in range(1, NGZ):
            total = total + ksum[other - 1]
        esum[...] = total
        w = ld(A1[2], 0) + total[CX:2 * CX]
        st(A1[2], 0, w)
        w = w * ld(md, 0)
        st(MA[2], 0, w)
        pack_rows(xa5, [(MA[2], 0)], 0)
        pack_rows(xb5, [(MA[2], 0)], CX - 1)
        ys5[...] = pltpu.roll(w, 11, 1)

    go(*r5x, *r5y)


    @pl.when(has_zm)
    def _():
        for c in range(3):
            st(V0[c], -1, zl[c])
            st(MA[c], -1, zl[6] * zl[3 + c])
        st(A1[2], -1, zl[5])

    @pl.when(has_zp)
    def _():
        for c in range(3):
            st(V0[c], CZ, zu[c])
            st(MA[c], CZ, zu[6] * zu[3 + c])
        st(p1, CZ, zu[13] - ld(V0[2], CZ - 1))
        st(m1, CZ, zu[14] + 0.25 * ld(A1[2], CZ - 1))

    some(lambda z: s1(z, c1), rim)
    x6 = [(p1, 0), (m1, 0), (m1, 1), (A1[2], CZ - 1)]
    pack_rows(xa6, x6, 0)
    r6x = x_down(xa6, xh6)
    go(r6x)
    pack_layers(ys6, [p1, m1, A1[2]], rim)
    r6y = y_down(ys6, yh6)
    go(r6y)
    go(*r3x)

    got(r6x, r6y, *r5x, *r5y)
    @pl.when(surface & has_xp)
    def _():
        unpack_rows(xh5, [(MA[2], 0)], CX)

    @pl.when(surface & has_xm)
    def _():
        unpack_rows(xl5, [(MA[2], 0)], -1)

    @pl.when(surface & has_yp)
    def _():
        yh1[0] = jnp.where(lane == 11, yh5[...], yh1[0])

    @pl.when(surface & has_ym)
    def _():
        yl1[0] = jnp.where(lane == 10, yl5[...], yl1[0])

    @pl.when(surface)
    def _():
        merge(c1, yl1, yh1, (0,))
        lm[2, 0], _ = lap(MA[2], 0, c1, 5)


    @pl.when(has_xp)
    def _():
        unpack_rows(xh6, x6, CX)

    some(lambda z: s2(z, yh6), rim)
    got(*zpart)

    @pl.when(surface)
    def _():
        w = ld(A0[2], 0) + esum[0:CX, :]
        st(A0[2], 0, w)
        st(MA0[2], 0, w * ld(md, 0))

    @pl.when(has_zm)
    def _():
        g = zl[6]
        extra_v, extra_a = ld(p1, 0), ld(m1, 0)
        for c in range(3):
            v = g * ld(V0[c], 0)
            a = 0.25 * ld(MA[c], 0)
            if c == 2:
                v, a = v + extra_v, a - extra_a
            st(V1[c], -1, zl[7 + c] + 0.25 * v)
            a = zl[10 + c] + a
            st(A0[c], -1, a)
            st(MA0[c], -1, g * a)

    @pl.when(has_zp)
    def _():
        g = zu[6]
        top = CZ - 1
        q, w = ld(V0[2], top), ld(A1[2], top)
        gq = (ld(V0[2], top, 1) - q, yhi(q, yh1, top, 2) - q, -q)
        gw = (ld(A1[2], top, 1) - w, yhi(w, yh6, top, 2) - w, -w)
        for c in range(3):
            st(V1[c], CZ, zu[7 + c] + 0.25 * (g * ld(V0[c], top) - gq[c]))
            a = zu[10 + c] + 0.25 * (ld(MA[c], top) - gw[c])
            st(A0[c], CZ, a)
            st(MA0[c], CZ, g * a)

    x7 = [(ref, z) for ref in lo3 for z in (0, 1, CZ - 1)]
    x7up = x7 + [(A0[0], z) for z in (0, 1, CZ - 1, CZ)]
    pack_rows(xa7, x7, 0)
    pack_rows(xb7, x7up, CX - 1)
    r7x = [x_down(xa7, xh7), x_up(xb7, xl7)]
    go(*r7x)
    edges = (0, 1, 2, CZ - 2, CZ - 1)
    pack_layers(ys7, lo3 + [A0[1]], edges, last=A0[1])
    r7y = [y_down(ys7, yh7), y_up(ys7, yl7)]
    go(*r7y)
    got(*r3x, *r3y)

    @pl.when(has_xp)
    def _():
        unpack_x(xh3, lo3, CX)

    @pl.when(has_xm)
    def _():
        unpack_x(xl3, lo3 + [A0[0]], -1)

    merge(c3, yl3, yh3)
    every(lambda z: s3(z, c3), 3, CZ - 2)
    pack_x(xa4, [m0], 0)
    r4x = x_down(xa4, xh4)
    go(r4x)
    pack_y(ys4, [m0])
    r4y = y_down(ys4, yh4)
    go(r4y)

    got(*r7x, *r7y)

    @pl.when(has_xp)
    def _():
        unpack_rows(xh7, x7, CX)

    @pl.when(has_xm)
    def _():
        unpack_rows(xl7, x7up, -1)

    merge(c7, yl7, yh7)
    some(lambda z: s3(z, c7), edges)

    @pl.when(has_zp)
    def _():
        x, y, w = (ld(r, CZ) for r in A0)
        low = jnp.where(lane == 0, pltpu.roll(yl7[3], 2, 1), pltpu.roll(y, 1, 1))
        d = (x - ld(A0[0], CZ, -1)) + (y - low) + (w - ld(A0[2], CZ - 1))
        st(m0, CZ, ld(m1, CZ) - 0.25 * d)

    x8 = [(m0, z) for z in edges + (CZ - 3,)]
    pack_rows(xa8, x8, 0)
    r8x = x_down(xa8, xh8)
    go(r8x)
    pack_layers(ys8, [m0], edges + (CZ - 3,))
    r8y = y_down(ys8, yh8)
    go(r8y)
    got(r4x, r4y)

    @pl.when(has_xp)
    def _():
        unpack_x(xh4, [m0], CX)

    every(lambda z: s4(z, yh4), 3, CZ - 3)
    early = store(3, CZ - 6, 0)
    got(r8x, r8y)

    @pl.when(has_xp)
    def _():
        unpack_rows(xh8, x8, CX)

    some(lambda z: s4(z, yh8), (0, 1, 2, CZ - 3, CZ - 2, CZ - 1))
    late = store(0, 3, 1) + store(CZ - 3, 3, 2)
    for one in links:
        if one not in zpart and one not in zpm:
            one.flush()
    for copy in stage1 + stage2:
        copy.wait_send()

    @pl.when(gz > 0)
    def _():
        pltpu.make_async_remote_copy(
            src_ref=esum, dst_ref=ksum.at[gz - 1], send_sem=f3s, recv_sem=f3r.at[gz - 1],
            device_id=(gx, gy, 0), device_id_type=MESH,
        ).wait_send()

    for copy in early + late:
        copy.wait()


def hand_out(a, b, c, oa, ob, oc, held, sem_in, sem_out):
    pieces = [(a.at[k], oa.at[k]) for k in range(3)] + [(b, ob), (c, oc)]
    ins = [pltpu.make_async_copy(p[0], held.at[k], sem_in.at[k]) for k, p in enumerate(pieces)]
    outs = [pltpu.make_async_copy(held.at[k], p[1], sem_out.at[k]) for k, p in enumerate(pieces)]
    for copy in ins:
        copy.start()
    for first, second in zip(ins, outs):
        first.wait()
        second.start()
    for copy in outs:
        copy.wait()


def shards(vel, pres, modulus, avel, apres, svals, sowner, sline, sstep):
    vector = pltpu.VMEM((3, ROWS, CY), F32)
    scalar = pltpu.VMEM((ROWS, CY), F32)
    flat3 = pltpu.VMEM((3, CZ, CX, CY), F32)
    flat = pltpu.VMEM((CZ, CX, CY), F32)
    pack = pltpu.VMEM((4, CX, CY), F32)
    plane = pltpu.VMEM((CX, CY), F32)
    ints = pltpu.VMEM((1, 32), jnp.int32)

    def lines(n):
        return pltpu.VMEM((n, CY), F32)

    def dma(n):
        return pltpu.SemaphoreType.DMA((n,))

    anywhere = pl.BlockSpec(memory_space=pl.ANY)
    inner = pl.pallas_call(
        body,
        out_shape=(
            jax.ShapeDtypeStruct((3, CZ, CX, CY), F32),
            jax.ShapeDtypeStruct((CZ, CX, CY), F32),
            jax.ShapeDtypeStruct((CZ, CX, CY), F32),
        ),
        in_specs=[anywhere] * 9,
        out_specs=(anywhere,) * 3,
        scratch_shapes=[
            vector, vector, vector, scalar, scalar, scalar, vector, vector, vector, scalar,
            flat, flat, flat3, flat3, flat3, flat, flat3,
            pack, pack, pack, pack, pack, pack, pack, pack, pack, pack,
            pack, pack, pack, pack, pack, lines(24), lines(24), lines(24), lines(24), lines(8), lines(8),
            plane, plane, plane, pack, pack, pack, pack, pack, pack, pack,
            lines(6 * CZ), lines(7 * CZ), lines(6 * CZ), lines(7 * CZ),
            lines(2 * CZ), lines(2 * CZ),
            lines(6 * CZ), lines(7 * CZ), lines(6 * CZ), lines(7 * CZ),
            lines(CZ), lines(CZ),
            lines(8), lines(8), lines(8), lines(8), lines(8), lines(8),
            lines(24), lines(24), lines(24), lines(24), lines(8), lines(8),
            lines(32), ints, ints, ints,
            pltpu.VMEM((13, CX, CY), F32), pltpu.VMEM((15, CX, CY), F32),
            lines(256), lines(256), lines(CY), pltpu.VMEM((3, 32, CY), F32), lines(32),
            pltpu.VMEM((NGZ - 1, 32, CY), F32),
            dma(9), dma(9), dma(15), dma(15), dma(13), dma(13), dma(12), dma(12),
            dma(NGY - 1), dma(NGY - 1), dma(NGX - 1), dma(NGX - 1),
            pltpu.SemaphoreType.DMA, dma(NGZ - 1),
        ],
        compiler_params=pltpu.CompilerParams(
            collective_id=0, has_side_effects=True, vmem_limit_bytes=62 * 2**20
        ),
        cost_estimate=pl.CostEstimate(flops=20_000_000, bytes_accessed=3_670_016, transcendentals=0),
        name="adjoint",
    )(vel, pres, modulus, avel, apres, svals, sowner.reshape(1, 32), sline.reshape(1, 32), sstep.reshape(1, 32))
    return pl.pallas_call(
        hand_out,
        out_shape=[jax.ShapeDtypeStruct(a.shape, F32) for a in inner],
        in_specs=[anywhere] * 3,
        out_specs=[anywhere] * 3,
        scratch_shapes=[pltpu.VMEM((5, CZ, CX, CY), F32), dma(5), dma(5)],
        compiler_params=pltpu.CompilerParams(vmem_limit_bytes=62 * 2**20),
        name="handout",
    )(*inner)


def solution(mesh):
    return jax.shard_map(
        shards,
        mesh=mesh,
        in_specs=(
            P(None, "gz", "gx", "gy"),
            P("gz", "gx", "gy"),
            P("gz", "gx", "gy"),
            P(None, "gz", "gx", "gy"),
            P("gz", "gx", "gy"),
            P(("gx", "gy", "gz"), None),
            P(("gx", "gy", "gz"), None),
            P(("gx", "gy", "gz")),
            P(("gx", "gy", "gz")),
        ),
        out_specs=(P(None, "gz", "gx", "gy"), P("gz", "gx", "gy"), P("gz", "gx", "gy")),
        check_vma=False,
    )
```

```python
import jax
import jax.numpy as jnp
from jax import lax
from jax.experimental import pallas as pl
from jax.experimental.pallas import tpu as pltpu
from jax.sharding import PartitionSpec as P

MESH = pl.DeviceIdType.MESH
F32 = jnp.float32
CZ, CX, CY = 32, 16, 128
PITCH = 32
LAYERS = CZ + 2
ROWS = LAYERS * PITCH
NGX, NGY, NGZ = 4, 8, 8
UNROLL = 4
HIGH = lax.Precision.HIGHEST


def body(
    vel, pres, modulus, avel, apres, svals_h, sowner_h, sline_h, sstep_h,
    o_av, o_ap, o_sh,
    v0, a1, ma, md, p1, m1, v1, a0, ma0, m0,
    p0, ap, bend0, lm, lm0, sh, out,
    ys1, yl1, yh1, ys2, yh2, ys3, yl3, yh3, ys4, yh4,
    c1, c3, c7, ys9, yh9, xa9, xb9, xl9, xh9, xa10, xh10,
    ys5, yl5, yh5, ys6, yh6, ys7, yl7, yh7, ys8, yh8,
    xa1, xb1, xh1, xl1, xa2, xh2, xa3, xb3, xh3, xl3, xa4, xh4,
    xa5, xb5, xh5, xl5, xa6, xh6, xa7, xb7, xh7, xl7, xa8, xh8,
    svals, sowner, sline, sstep,
    zl, zu, to_up, to_down, from_low, from_high, cs, gath, dense, hsum, esum, ksum,
    in_sem, out_sem, xs_sem, xr_sem, ys_sem, yr_sem, zs_sem, zr_sem,
    f1s, f1r, f2s, f2r, f3s, f3r,
):
    gx, gy, gz = lax.axis_index("gx"), lax.axis_index("gy"), lax.axis_index("gz")
    has_xm, has_xp = gx > 0, gx < NGX - 1
    has_ym, has_yp = gy > 0, gy < NGY - 1
    has_zm, has_zp = gz > 0, gz < NGZ - 1
    barrier = pltpu.get_barrier_semaphore()

    def grid3(ref):
        if len(ref.shape) == 3:
            return ref.reshape(3, LAYERS, PITCH, CY).at[:, pl.ds(1, CZ), pl.ds(8, CX), :]
        return ref.reshape(LAYERS, PITCH, CY).at[pl.ds(1, CZ), pl.ds(8, CX), :]

    loads = [
        pltpu.make_async_copy(src, dst, in_sem.at[i])
        for i, (src, dst) in enumerate(
            [(avel, grid3(a1)), (modulus, grid3(md)), (vel, grid3(v0)), (pres, p0), (apres, ap)]
        )
    ]
    sensors = [
        pltpu.make_async_copy(src, dst, in_sem.at[5 + i])
        for i, (src, dst) in enumerate(
            [(svals_h, svals), (sowner_h, sowner), (sline_h, sline), (sstep_h, sstep)]
        )
    ]
    for copy in loads + sensors:
        copy.start()

    lane = lax.broadcasted_iota(jnp.int32, (CX, CY), 1)

    @pl.when(jnp.logical_not(has_ym))
    def _():
        for ref in (yl1, yl3, yl7):
            ref[...] = jnp.zeros(ref.shape, F32)
        yl5[...] = jnp.zeros(yl5.shape, F32)

    @pl.when(jnp.logical_not(has_yp))
    def _():
        for ref in (yh1, yh2, yh3, yh4, yh6, yh7, yh8, yh9):
            ref[...] = jnp.zeros(ref.shape, F32)
        yh5[...] = jnp.zeros(yh5.shape, F32)

    def greet(device):
        pl.semaphore_signal(barrier, inc=1, device_id=device, device_id_type=MESH)

    @pl.when(has_zm)
    def _():
        greet((gx, gy, gz - 1))

    @pl.when(has_zp)
    def _():
        greet((gx, gy, gz + 1))

    @pl.when(gz == 0)
    def _():
        for other in range(2, NGZ):
            greet((gx, gy, other))

    for step in range(1, NGY):
        greet((gx, lax.rem(gy + step, NGY), gz))
    for step in range(1, NGX):
        greet((lax.rem(gx + step, NGX), gy, gz))
    expected = (
        NGX - 1 + NGY - 1
        + has_zm.astype(jnp.int32) + has_zp.astype(jnp.int32) + (gz >= 2).astype(jnp.int32)
    )

    def comps(ref):
        return [ref.at[c] for c in range(3)]

    V0, A1, MA, V1, A0, MA0 = (comps(r) for r in (v0, a1, ma, v1, a0, ma0))

    zeros_layer = jnp.zeros((PITCH, CY), F32)
    zeros_rows = jnp.zeros((LAYERS, CY), F32)
    for ref in V0 + A1 + MA + V1 + A0 + MA0 + [p1, m1, m0]:
        ref[0:PITCH, :] = zeros_layer
        ref[ROWS - PITCH:ROWS, :] = zeros_layer

    @pl.when(jnp.logical_not(has_xm))
    def _():
        for ref in V0 + [A1[0]] + MA + V1 + [A0[0]] + MA0:
            ref[pl.ds(7, LAYERS, stride=PITCH), :] = zeros_rows

    @pl.when(jnp.logical_not(has_xp))
    def _():
        for ref in V0 + MA + [A1[2]] + V1 + MA0 + [p1, m1, m0]:
            ref[pl.ds(24, LAYERS, stride=PITCH), :] = zeros_rows

    def ld(ref, z, dx=0):
        return ref[pl.ds((z + 1) * PITCH + 8 + dx, CX), :]

    def st(ref, z, value):
        ref[pl.ds(pl.multiple_of((z + 1) * PITCH + 8, 8), CX), :] = value

    def halo(blk, z, f):
        return pltpu.roll(blk[z & 3], (CY - ((z >> 2) * 16 + 2 * f)) & (CY - 1), 1)

    def ylo(u, blk, z, f):
        return jnp.where(lane == 0, halo(blk, z, f), pltpu.roll(u, 1, 1))

    def yhi(u, blk, z, f):
        shift = CY - 2 - (z >> 2) * 16 - 2 * f
        return jnp.where(lane == CY - 1, pltpu.roll(blk[z & 3], shift, 1), pltpu.roll(u, CY - 1, 1))

    def merge(dst, low, high, planes=range(4)):
        for zz in planes:
            dst[zz] = jnp.where((lane & 1) == 0, low[zz], pltpu.roll(high[zz], CY - 2, 1))

    def lap(ref, z, blk, f):
        c = ld(ref, z)
        h = halo(blk, z, f)
        low = jnp.where(lane == 0, h, pltpu.roll(c, 1, 1))
        high = jnp.where(lane == CY - 1, h, pltpu.roll(c, CY - 1, 1))
        total = ld(ref, z, 1) + ld(ref, z, -1) + (ld(ref, z + 1) + ld(ref, z - 1))
        return total + (low + high) - 6.0 * c, low

    def div(refs, z, low):
        x, y, w = (ld(r, z) for r in refs)
        return (x - ld(refs[0], z, -1)) + (y - low) + (w - ld(refs[2], z - 1))

    def grad(ref, z, yh, f):
        q = ld(ref, z)
        return ld(ref, z, 1) - q, yhi(q, yh, z, f) - q, ld(ref, z + 1) - q

    def s1(z, blk):
        lows = []
        for c in range(3):
            bend0[c, z], low = lap(V0[c], z, blk, c)
            lows.append(low)
            lm[c, z], _ = lap(MA[c], z, blk, 3 + c)
        st(p1, z, p0[z] + div(V0, z, lows[1]))
        st(m1, z, ap[z] - 0.25 * div(A1, z, ylo(ld(A1[1], z), blk, z, 6)))

    def s2(z, yh):
        gp, gm = grad(p1, z, yh, 0), grad(m1, z, yh, 1)
        g = ld(md, z)
        for c in range(3):
            st(V1[c], z, ld(V0[c], z) + 0.25 * (gp[c] + g * bend0[c, z]))
            new = ld(A1[c], z) + 0.25 * lm[c, z] - gm[c]
            st(A0[c], z, new)
            st(MA0[c], z, g * new)

    def s3(z, blk):
        total = None
        for c in range(3):
            part = ld(A1[c], z) * lap(V1[c], z, blk, c)[0] + ld(A0[c], z) * bend0[c, z]
            total = part if total is None else total + part
            lm0[c, z], _ = lap(MA0[c], z, blk, 3 + c)
        sh[z] = 0.25 * total
        st(m0, z, ld(m1, z) - 0.25 * div(A0, z, ylo(ld(A0[1], z), blk, z, 6)))

    def s4(z, yh):
        gm = grad(m0, z, yh, 0)
        for c in range(3):
            out[c, z] = ld(A0[c], z) + 0.25 * lm0[c, z] - gm[c]

    def every(fn, start=0, stop=CZ, unroll=UNROLL):
        turns = (stop - start) // unroll

        def step(n, carry):
            for k in range(unroll):
                fn(start + n * unroll + k)
            return carry

        lax.fori_loop(0, turns, step, 0)
        for z in range(start + turns * unroll, stop):
            fn(z)

    def some(fn, layers):
        for z in layers:
            fn(z)

    def pack_y(dst, fields):
        def step(zz, carry):
            acc = jnp.zeros((CX, CY), F32)
            for g in range(8):
                for f, ref in enumerate(fields):
                    s = g * 16 + 2 * f + 1
                    acc = jnp.where((lane >> 1) == (s >> 1), pltpu.roll(ld(ref, g * 4 + zz), s, 1), acc)
            dst[zz] = acc
            return carry
        lax.fori_loop(0, 4, step, 0)

    def pack_layers(dst, fields, layers, last=None):
        for zz in range(4):
            acc = jnp.zeros((CX, CY), F32)
            for z in layers:
                if z % 4 == zz:
                    for f, ref in enumerate(fields):
                        s = (z // 4) * 16 + 2 * f + 1
                        acc = jnp.where((lane >> 1) == (s >> 1), pltpu.roll(ld(ref, z), s, 1), acc)
            if zz == 3 and last is not None:
                acc = jnp.where(lane >= CY - 2, pltpu.roll(ld(last, CZ), CY - 1, 1), acc)
            dst[zz] = acc

    def face(ref, x):
        return ref[pl.ds(PITCH + 8 + x, CZ, stride=PITCH), :]

    def pack_x(dst, fields, x):
        for i, ref in enumerate(fields):
            dst[i * CZ:(i + 1) * CZ, :] = face(ref, x)

    def unpack_x(src, fields, x):
        for i, ref in enumerate(fields):
            ref[pl.ds(PITCH + 8 + x, CZ, stride=PITCH), :] = src[i * CZ:(i + 1) * CZ, :]

    def rows_of(pairs, x):
        return [(ref, (z + 1) * PITCH + 8 + x) for ref, z in pairs]

    def pack_rows(dst, pairs, x):
        for i, (ref, row) in enumerate(rows_of(pairs, x)):
            dst[i:i + 1, :] = ref[row:row + 1, :]

    def unpack_rows(src, pairs, x):
        for i, (ref, row) in enumerate(rows_of(pairs, x)):
            ref[row:row + 1, :] = src[i:i + 1, :]

    def store(start, size, n):
        part = pl.ds(start, size)
        copies = [
            pltpu.make_async_copy(out.at[:, part], o_av.at[:, part], out_sem.at[3 * n]),
            pltpu.make_async_copy(
                m0.reshape(LAYERS, PITCH, CY).at[pl.ds(start + 1, size), pl.ds(8, CX), :],
                o_ap.at[part], out_sem.at[3 * n + 1],
            ),
            pltpu.make_async_copy(sh.at[part], o_sh.at[part], out_sem.at[3 * n + 2]),
        ]
        for copy in copies:
            copy.start()
        return copies

    class Link:
        def __init__(self, src, dst, send, recv, device, sends, gets):
            self.copy = pltpu.make_async_remote_copy(
                src_ref=src, dst_ref=dst, send_sem=send, recv_sem=recv,
                device_id=device, device_id_type=MESH,
            )
            self.sends, self.gets = sends, gets

        def start(self):
            pl.when(self.sends)(self.copy.start)

        def arrive(self):
            pl.when(self.gets)(self.copy.wait_recv)

        def flush(self):
            pl.when(self.sends)(self.copy.wait_send)

    links = []
    counts = {"x": 0, "y": 0, "z": 0}

    def link(kind, src, dst, device, sends, gets):
        n = counts[kind]
        counts[kind] += 1
        ss, rs = {"x": (xs_sem, xr_sem), "y": (ys_sem, yr_sem), "z": (zs_sem, zr_sem)}[kind]
        made = Link(src, dst, ss.at[n], rs.at[n], device, sends, gets)
        links.append(made)
        return made

    def x_down(src, dst):
        return link("x", src, dst, (gx - 1, gy, gz), has_xm, has_xp)

    def x_up(src, dst):
        return link("x", src, dst, (gx + 1, gy, gz), has_xp, has_xm)

    def y_down(src, dst):
        return link("y", src, dst, (gx, gy - 1, gz), has_ym, has_yp)

    def y_up(src, dst):
        return link("y", src, dst, (gx, gy + 1, gz), has_yp, has_ym)

    def z_down(src, dst):
        return link("z", src, dst, (gx, gy, gz - 1), has_zm, has_zp)

    def z_up(src, dst):
        return link("z", src, dst, (gx, gy, gz + 1), has_zp, has_zm)

    def go(*those):
        for one in those:
            one.start()

    def got(*those):
        for one in those:
            one.arrive()

    for copy in loads:
        copy.wait()

    def weight(z):
        g = ld(md, z)
        for c in range(3):
            st(MA[c], z, g * ld(A1[c], z))

    every(weight)
    lo1 = V0 + MA
    rim = (0, 1, CZ - 1)
    x9 = [(ref, z) for ref in lo1 for z in rim]
    x9up = x9 + [(A1[0], z) for z in rim]
    pack_rows(xa9, x9, 0)
    pack_rows(xb9, x9up, CX - 1)
    pack_y(ys1, lo1 + [A1[1]])

    pl.semaphore_wait(barrier, expected)

    r9x = [x_down(xa9, xh9), x_up(xb9, xl9)]
    r1y = [y_down(ys1, yh1), y_up(ys1, yl1)]
    r1x = [x_down(xa1, xh1), x_up(xb1, xl1)]
    zraw = [
        z_up(avel.at[:, CZ - 1], zl.at[3:6]),
        z_down(avel.at[:, 0], zu.at[3:6]),
        z_up(modulus.at[CZ - 1], zl.at[6]),
        z_down(modulus.at[0], zu.at[6]),
        z_up(vel.at[:, CZ - 1], zl.at[0:3]),
        z_down(vel.at[:, 0], zu.at[0:3]),
    ]
    go(*r9x, *r1y, *zraw)
    pack_x(xa1, lo1, 0)
    pack_x(xb1, lo1 + [A1[0]], CX - 1)
    go(*r1x)

    for copy in sensors:
        copy.wait()
    owner_row = sowner[...].astype(F32)
    r0 = lax.broadcasted_iota(jnp.int32, (32, 32), 0)
    r1 = lax.broadcasted_iota(jnp.int32, (32, 32), 1)
    owner_col = jnp.sum(jnp.where(r0 == r1, owner_row, 0.0), axis=1, keepdims=True)
    rank = jnp.sum(
        jnp.where((owner_col == owner_row) & (r0 < r1), 1.0, 0.0), axis=0, keepdims=True
    ).astype(jnp.int32)
    owner_int = owner_row.astype(jnp.int32)
    own_gx, own_gy = owner_int >> 3, owner_int & 7
    place = own_gy * 32 + own_gx * 8 + rank
    code_row = (own_gx * 32 + sstep[...] * CX + sline[...] + 1).astype(F32)
    code_col = jnp.sum(jnp.where(r0 == r1, code_row, 0.0), axis=1, keepdims=True)
    slot = lax.broadcasted_iota(jnp.int32, (256, 32), 0)
    cs[...] = jnp.dot(
        (slot == place).astype(F32), svals[...], precision=HIGH, preferred_element_type=F32
    ) + jnp.dot(
        (slot == place + 4).astype(F32), jnp.broadcast_to(code_col, (32, CY)),
        precision=HIGH, preferred_element_type=F32,
    )
    mine = pl.ds(pl.multiple_of(gy * 32, 32), 32)
    gath[mine, :] = cs[mine, :]

    stage1 = []
    for step in range(1, NGY):
        other = lax.rem(gy + step, NGY)
        stage1.append(
            pltpu.make_async_remote_copy(
                src_ref=cs.at[pl.ds(pl.multiple_of(other * 32, 32), 32)],
                dst_ref=gath.at[mine],
                send_sem=f1s.at[step - 1], recv_sem=f1r.at[step - 1],
                device_id=(gx, other, gz), device_id_type=MESH,
            )
        )
        stage1[-1].start()

    got(*r9x, *r1y)

    @pl.when(has_xp)
    def _():
        unpack_rows(xh9, x9, CX)

    @pl.when(has_xm)
    def _():
        unpack_rows(xl9, x9up, -1)

    merge(c1, yl1, yh1)
    some(lambda z: s1(z, c1), rim)
    x10 = [(ref, z) for ref in (p1, m1) for z in (0, CZ - 1)]
    pack_rows(xa10, x10, 0)
    r10x = x_down(xa10, xh10)
    go(r10x)
    pack_layers(ys9, [p1, m1], (0, CZ - 1))
    r9y = y_down(ys9, yh9)
    zpm = [
        z_down(p1.at[pl.ds(PITCH + 8, CX)], zu.at[10]),
        z_down(m1.at[pl.ds(PITCH + 8, CX)], zu.at[11]),
    ]
    go(r9y, *zpm)
    for copy in stage1:
        copy.wait_recv()
    rows = gath[...]
    r256 = lax.broadcasted_iota(jnp.int32, (256, CY), 0)
    l256 = lax.broadcasted_iota(jnp.int32, (256, CY), 1)
    codes = pltpu.roll(rows, 252, 0)
    hot = jnp.where(((r256 & 7) < 4) & (codes == (l256 + 1).astype(F32)), 1.0, 0.0)
    dense[...] = lax.dot_general(
        hot, rows, (((0,), (0,)), ((), ())), precision=HIGH, preferred_element_type=F32
    )
    stage2 = []
    for step in range(1, NGX):
        other = lax.rem(gx + step, NGX)
        stage2.append(
            pltpu.make_async_remote_copy(
                src_ref=dense.at[pl.ds(pl.multiple_of(other * 32, 32), 32)],
                dst_ref=hsum.at[step - 1],
                send_sem=f2s.at[step - 1], recv_sem=f2r.at[step - 1],
                device_id=(other, gy, gz), device_id_type=MESH,
            )
        )
        stage2[-1].start()

    got(r10x, r9y)

    @pl.when(has_xp)
    def _():
        unpack_rows(xh10, x10, CX)

    some(lambda z: s2(z, yh9), (0, CZ - 1))
    first, final = pl.ds(PITCH + 8, CX), pl.ds(CZ * PITCH + 8, CX)
    zpart = [
        z_up(a0.at[:, final], zl.at[7:10]),
        z_down(a0.at[:, first], zu.at[7:10]),
    ]
    go(*zpart)

    got(*r1x)

    @pl.when(has_xp)
    def _():
        unpack_x(xh1, lo1, CX)

    @pl.when(has_xm)
    def _():
        unpack_x(xl1, lo1 + [A1[0]], -1)

    every(lambda z: s1(z, c1), 2, CZ - 1)
    pack_x(xa2, [p1, m1], 0)
    r2x = x_down(xa2, xh2)
    go(r2x)
    pack_y(ys2, [p1, m1])
    r2y = y_down(ys2, yh2)
    go(r2y)

    for copy in stage2:
        copy.wait_recv()
    own = dense[pl.ds(pl.multiple_of(gx * 32, 32), 32), :]
    esum[...] = own + hsum[0] + hsum[1] + hsum[2]

    @pl.when(gz > 0)
    def _():
        to_surface = pltpu.make_async_remote_copy(
            src_ref=esum, dst_ref=ksum.at[gz - 1], send_sem=f3s, recv_sem=f3r.at[gz - 1],
            device_id=(gx, gy, 0), device_id_type=MESH,
        )
        to_surface.start()

    got(r2x, r2y)

    @pl.when(has_xp)
    def _():
        unpack_x(xh2, [p1, m1], CX)

    every(lambda z: s2(z, yh2), 1, CZ - 1)

    lo3 = V1 + MA0
    pack_x(xa3, lo3, 0)
    pack_x(xb3, lo3 + [A0[0]], CX - 1)
    r3x = [x_down(xa3, xh3), x_up(xb3, xl3)]
    go(*r3x)
    pack_y(ys3, lo3 + [A0[1]])
    r3y = [y_down(ys3, yh3), y_up(ys3, yl3)]
    go(*r3y)

    for one in zpart + zpm:
        one.flush()
    got(*zraw, *zpm)

    surface = gz == 0
    r5x = [
        link("x", xa5, xh5, (gx - 1, gy, gz), surface & has_xm, surface & has_xp),
        link("x", xb5, xl5, (gx + 1, gy, gz), surface & has_xp, surface & has_xm),
    ]
    r5y = [
        link("y", ys5, yh5, (gx, gy - 1, gz), surface & has_ym, surface & has_yp),
        link("y", ys5, yl5, (gx, gy + 1, gz), surface & has_yp, surface & has_ym),
    ]

    @pl.when(surface)
    def _():
        for other in range(1, NGZ):
            pltpu.make_async_remote_copy(
                src_ref=esum, dst_ref=ksum.at[other - 1], send_sem=f3s, recv_sem=f3r.at[other - 1],
                device_id=(gx, gy, 1), device_id_type=MESH,
            ).wait_recv()
        total = esum[...]
        for other in range(1, NGZ):
            total = total + ksum[other - 1]
        esum[...] = total
        w = ld(A1[2], 0) + total[CX:2 * CX]
        st(A1[2], 0, w)
        w = w * ld(md, 0)
        st(MA[2], 0, w)
        pack_rows(xa5, [(MA[2], 0)], 0)
        pack_rows(xb5, [(MA[2], 0)], CX - 1)
        ys5[...] = pltpu.roll(w, 11, 1)

    go(*r5x, *r5y)


    @pl.when(has_zm)
    def _():
        for c in range(3):
            st(V0[c], -1, zl[c])
            st(MA[c], -1, zl[6] * zl[3 + c])
        st(A1[2], -1, zl[5])

    @pl.when(has_zp)
    def _():
        for c in range(3):
            st(V0[c], CZ, zu[c])
            st(MA[c], CZ, zu[6] * zu[3 + c])
        st(p1, CZ, zu[10] - ld(V0[2], CZ - 1))
        st(m1, CZ, zu[11] + 0.25 * ld(A1[2], CZ - 1))

    some(lambda z: s1(z, c1), rim)
    x6 = [(p1, 0), (m1, 0), (m1, 1), (A1[2], CZ - 1)]
    pack_rows(xa6, x6, 0)
    r6x = x_down(xa6, xh6)
    go(r6x)
    pack_layers(ys6, [p1, m1, A1[2]], rim)
    r6y = y_down(ys6, yh6)
    go(r6y)

    got(r6x, r6y, *r5x, *r5y)
    @pl.when(surface & has_xp)
    def _():
        unpack_rows(xh5, [(MA[2], 0)], CX)

    @pl.when(surface & has_xm)
    def _():
        unpack_rows(xl5, [(MA[2], 0)], -1)

    @pl.when(surface & has_yp)
    def _():
        yh1[0] = jnp.where(lane == 11, yh5[...], yh1[0])

    @pl.when(surface & has_ym)
    def _():
        yl1[0] = jnp.where(lane == 10, yl5[...], yl1[0])

    @pl.when(surface)
    def _():
        merge(c1, yl1, yh1, (0,))
        lm[2, 0], _ = lap(MA[2], 0, c1, 5)


    @pl.when(has_xp)
    def _():
        unpack_rows(xh6, x6, CX)

    some(lambda z: s2(z, yh6), rim)

    to_up[...] = sum(ld(V1[c], CZ - 1) * zu[3 + c] for c in range(3))
    to_down[...] = sum(ld(V1[c], 0) * zl[3 + c] for c in range(3))
    zshare = [z_up(to_up, from_low), z_down(to_down, from_high)]
    go(*zshare)
    got(*zpart)

    @pl.when(surface)
    def _():
        w = ld(A0[2], 0) + esum[0:CX, :]
        st(A0[2], 0, w)
        st(MA0[2], 0, w * ld(md, 0))

    @pl.when(has_zm)
    def _():
        g = zl[6]
        extra = ld(m1, 0)
        for c in range(3):
            a = zl[7 + c] + 0.25 * ld(MA[c], 0) - (extra if c == 2 else 0.0)
            st(A0[c], -1, a)
            st(MA0[c], -1, g * a)

    @pl.when(has_zp)
    def _():
        g = zu[6]
        top = CZ - 1
        w = ld(A1[2], top)
        gw = (ld(A1[2], top, 1) - w, yhi(w, yh6, top, 2) - w, -w)
        for c in range(3):
            a = zu[7 + c] + 0.25 * (ld(MA[c], top) - gw[c])
            st(A0[c], CZ, a)
            st(MA0[c], CZ, g * a)

    x7 = [(ref, z) for ref in lo3 for z in (0, 1, CZ - 1)]
    x7up = x7 + [(A0[0], z) for z in (0, 1, CZ - 1, CZ)]
    pack_rows(xa7, x7, 0)
    pack_rows(xb7, x7up, CX - 1)
    r7x = [x_down(xa7, xh7), x_up(xb7, xl7)]
    go(*r7x)
    edges = (0, 1, 2, CZ - 2, CZ - 1)
    pack_layers(ys7, lo3 + [A0[1]], edges, last=A0[1])
    r7y = [y_down(ys7, yh7), y_up(ys7, yl7)]
    go(*r7y)
    got(*r3x, *r3y)

    @pl.when(has_xp)
    def _():
        unpack_x(xh3, lo3, CX)

    @pl.when(has_xm)
    def _():
        unpack_x(xl3, lo3 + [A0[0]], -1)

    merge(c3, yl3, yh3)
    every(lambda z: s3(z, c3), 3, CZ - 2)
    pack_x(xa4, [m0], 0)
    r4x = x_down(xa4, xh4)
    go(r4x)
    pack_y(ys4, [m0])
    r4y = y_down(ys4, yh4)
    go(r4y)

    got(*r7x, *r7y)

    @pl.when(has_xp)
    def _():
        unpack_rows(xh7, x7, CX)

    @pl.when(has_xm)
    def _():
        unpack_rows(xl7, x7up, -1)

    merge(c7, yl7, yh7)
    some(lambda z: s3(z, c7), edges)

    @pl.when(has_zp)
    def _():
        x, y, w = (ld(r, CZ) for r in A0)
        low = jnp.where(lane == 0, pltpu.roll(yl7[3], 2, 1), pltpu.roll(y, 1, 1))
        d = (x - ld(A0[0], CZ, -1)) + (y - low) + (w - ld(A0[2], CZ - 1))
        st(m0, CZ, ld(m1, CZ) - 0.25 * d)

    x8 = [(m0, z) for z in edges + (CZ - 3,)]
    pack_rows(xa8, x8, 0)
    r8x = x_down(xa8, xh8)
    go(r8x)
    pack_layers(ys8, [m0], edges + (CZ - 3,))
    r8y = y_down(ys8, yh8)
    go(r8y)
    got(r4x, r4y)

    @pl.when(has_xp)
    def _():
        unpack_x(xh4, [m0], CX)

    every(lambda z: s4(z, yh4), 3, CZ - 3)
    early = store(3, CZ - 6, 0)
    got(r8x, r8y)

    @pl.when(has_xp)
    def _():
        unpack_rows(xh8, x8, CX)

    some(lambda z: s4(z, yh8), (0, 1, 2, CZ - 3, CZ - 2, CZ - 1))
    got(*zshare)

    @pl.when(has_zm)
    def _():
        sh[0] = sh[0] + 0.25 * from_low[...]

    @pl.when(has_zp)
    def _():
        sh[CZ - 1] = sh[CZ - 1] + 0.25 * from_high[...]

    late = store(0, 3, 1) + store(CZ - 3, 3, 2)
    for one in links:
        if one not in zpart and one not in zpm:
            one.flush()
    for copy in stage1 + stage2:
        copy.wait_send()

    @pl.when(gz > 0)
    def _():
        pltpu.make_async_remote_copy(
            src_ref=esum, dst_ref=ksum.at[gz - 1], send_sem=f3s, recv_sem=f3r.at[gz - 1],
            device_id=(gx, gy, 0), device_id_type=MESH,
        ).wait_send()

    for copy in early + late:
        copy.wait()


def hand_out(a, b, c, oa, ob, oc, held, sem_in, sem_out):
    pieces = [(a.at[k], oa.at[k]) for k in range(3)] + [(b, ob), (c, oc)]
    ins = [pltpu.make_async_copy(p[0], held.at[k], sem_in.at[k]) for k, p in enumerate(pieces)]
    outs = [pltpu.make_async_copy(held.at[k], p[1], sem_out.at[k]) for k, p in enumerate(pieces)]
    for copy in ins:
        copy.start()
    for first, second in zip(ins, outs):
        first.wait()
        second.start()
    for copy in outs:
        copy.wait()


def shards(vel, pres, modulus, avel, apres, svals, sowner, sline, sstep):
    vector = pltpu.VMEM((3, ROWS, CY), F32)
    scalar = pltpu.VMEM((ROWS, CY), F32)
    flat3 = pltpu.VMEM((3, CZ, CX, CY), F32)
    flat = pltpu.VMEM((CZ, CX, CY), F32)
    pack = pltpu.VMEM((4, CX, CY), F32)
    plane = pltpu.VMEM((CX, CY), F32)
    ints = pltpu.VMEM((1, 32), jnp.int32)

    def lines(n):
        return pltpu.VMEM((n, CY), F32)

    def dma(n):
        return pltpu.SemaphoreType.DMA((n,))

    anywhere = pl.BlockSpec(memory_space=pl.ANY)
    inner = pl.pallas_call(
        body,
        out_shape=(
            jax.ShapeDtypeStruct((3, CZ, CX, CY), F32),
            jax.ShapeDtypeStruct((CZ, CX, CY), F32),
            jax.ShapeDtypeStruct((CZ, CX, CY), F32),
        ),
        in_specs=[anywhere] * 9,
        out_specs=(anywhere,) * 3,
        scratch_shapes=[
            vector, vector, vector, scalar, scalar, scalar, vector, vector, vector, scalar,
            flat, flat, flat3, flat3, flat3, flat, flat3,
            pack, pack, pack, pack, pack, pack, pack, pack, pack, pack,
            pack, pack, pack, pack, pack, lines(24), lines(24), lines(24), lines(24), lines(8), lines(8),
            plane, plane, plane, pack, pack, pack, pack, pack, pack, pack,
            lines(6 * CZ), lines(7 * CZ), lines(6 * CZ), lines(7 * CZ),
            lines(2 * CZ), lines(2 * CZ),
            lines(6 * CZ), lines(7 * CZ), lines(6 * CZ), lines(7 * CZ),
            lines(CZ), lines(CZ),
            lines(8), lines(8), lines(8), lines(8), lines(8), lines(8),
            lines(24), lines(24), lines(24), lines(24), lines(8), lines(8),
            lines(32), ints, ints, ints,
            pltpu.VMEM((10, CX, CY), F32), pltpu.VMEM((12, CX, CY), F32),
            plane, plane, plane, plane,
            lines(256), lines(256), lines(CY), pltpu.VMEM((3, 32, CY), F32), lines(32),
            pltpu.VMEM((NGZ - 1, 32, CY), F32),
            dma(9), dma(9), dma(15), dma(15), dma(13), dma(13), dma(12), dma(12),
            dma(NGY - 1), dma(NGY - 1), dma(NGX - 1), dma(NGX - 1),
            pltpu.SemaphoreType.DMA, dma(NGZ - 1),
        ],
        compiler_params=pltpu.CompilerParams(
            collective_id=0, has_side_effects=True, vmem_limit_bytes=62 * 2**20
        ),
        cost_estimate=pl.CostEstimate(flops=20_000_000, bytes_accessed=3_670_016, transcendentals=0),
        name="adjoint",
    )(vel, pres, modulus, avel, apres, svals, sowner.reshape(1, 32), sline.reshape(1, 32), sstep.reshape(1, 32))
    return pl.pallas_call(
        hand_out,
        out_shape=[jax.ShapeDtypeStruct(a.shape, F32) for a in inner],
        in_specs=[anywhere] * 3,
        out_specs=[anywhere] * 3,
        scratch_shapes=[pltpu.VMEM((5, CZ, CX, CY), F32), dma(5), dma(5)],
        compiler_params=pltpu.CompilerParams(vmem_limit_bytes=62 * 2**20),
        name="handout",
    )(*inner)


def solution(mesh):
    return jax.shard_map(
        shards,
        mesh=mesh,
        in_specs=(
            P(None, "gz", "gx", "gy"),
            P("gz", "gx", "gy"),
            P("gz", "gx", "gy"),
            P(None, "gz", "gx", "gy"),
            P("gz", "gx", "gy"),
            P(("gx", "gy", "gz"), None),
            P(("gx", "gy", "gz"), None),
            P(("gx", "gy", "gz")),
            P(("gx", "gy", "gz")),
        ),
        out_specs=(P(None, "gz", "gx", "gy"), P("gz", "gx", "gy"), P("gz", "gx", "gy")),
        check_vma=False,
    )
```

```python
import jax
import jax.numpy as jnp
from jax import lax
from jax.experimental import pallas as pl
from jax.experimental.pallas import tpu as pltpu
from jax.sharding import PartitionSpec as P

MESH = pl.DeviceIdType.MESH
F32 = jnp.float32
CZ, CX, CY = 32, 16, 128
PITCH = 32
LAYERS = CZ + 2
ROWS = LAYERS * PITCH
NGX, NGY, NGZ = 4, 8, 8
UNROLL = 4
HIGH = lax.Precision.HIGHEST


def body(
    vel, pres, modulus, avel, apres, svals_h, sowner_h, sline_h, sstep_h,
    o_av, o_ap, o_sh,
    v0, a1, ma, md, p1, m1, v1, a0, ma0, m0,
    p0, ap, bend0, lm, lm0, sh, out,
    ys1, yl1, yh1, ys2, yh2, ys3, yl3, yh3, ys4, yh4,
    c1, c3, c7, ys9, yh9, xa9, xb9, xl9, xh9, xa10, xh10,
    ys5, yl5, yh5, ys6, yh6, ys7, yl7, yh7, ys8, yh8,
    xa1, xb1, xh1, xl1, xa2, xh2, xa3, xb3, xh3, xl3, xa4, xh4,
    xa5, xb5, xh5, xl5, xa6, xh6, xa7, xb7, xh7, xl7, xa8, xh8,
    svals, sowner, sline, sstep,
    zl, zu, to_up, to_down, from_low, from_high, cs, gath, dense, hsum, esum, ksum,
    in_sem, out_sem, xs_sem, xr_sem, ys_sem, yr_sem, zs_sem, zr_sem,
    f1s, f1r, f2s, f2r, f3s, f3r,
):
    gx, gy, gz = lax.axis_index("gx"), lax.axis_index("gy"), lax.axis_index("gz")
    has_xm, has_xp = gx > 0, gx < NGX - 1
    has_ym, has_yp = gy > 0, gy < NGY - 1
    has_zm, has_zp = gz > 0, gz < NGZ - 1
    barrier = pltpu.get_barrier_semaphore()

    def grid3(ref):
        if len(ref.shape) == 3:
            return ref.reshape(3, LAYERS, PITCH, CY).at[:, pl.ds(1, CZ), pl.ds(8, CX), :]
        return ref.reshape(LAYERS, PITCH, CY).at[pl.ds(1, CZ), pl.ds(8, CX), :]

    loads = [
        pltpu.make_async_copy(src, dst, in_sem.at[i])
        for i, (src, dst) in enumerate(
            [(avel, grid3(a1)), (modulus, grid3(md)), (vel, grid3(v0)), (pres, p0), (apres, ap)]
        )
    ]
    sensors = [
        pltpu.make_async_copy(src, dst, in_sem.at[5 + i])
        for i, (src, dst) in enumerate(
            [(svals_h, svals), (sowner_h, sowner), (sline_h, sline), (sstep_h, sstep)]
        )
    ]
    for copy in loads + sensors:
        copy.start()

    lane = lax.broadcasted_iota(jnp.int32, (CX, CY), 1)

    @pl.when(jnp.logical_not(has_ym))
    def _():
        for ref in (yl1, yl3, yl7):
            ref[...] = jnp.zeros(ref.shape, F32)
        yl5[...] = jnp.zeros(yl5.shape, F32)

    @pl.when(jnp.logical_not(has_yp))
    def _():
        for ref in (yh1, yh2, yh3, yh4, yh6, yh7, yh8, yh9):
            ref[...] = jnp.zeros(ref.shape, F32)
        yh5[...] = jnp.zeros(yh5.shape, F32)

    def greet(device):
        pl.semaphore_signal(barrier, inc=1, device_id=device, device_id_type=MESH)

    @pl.when(has_zm)
    def _():
        greet((gx, gy, gz - 1))

    @pl.when(has_zp)
    def _():
        greet((gx, gy, gz + 1))

    @pl.when(gz == 0)
    def _():
        for other in range(2, NGZ):
            greet((gx, gy, other))

    for step in range(1, NGY):
        greet((gx, lax.rem(gy + step, NGY), gz))
    for step in range(1, NGX):
        greet((lax.rem(gx + step, NGX), gy, gz))
    expected = (
        NGX - 1 + NGY - 1
        + has_zm.astype(jnp.int32) + has_zp.astype(jnp.int32) + (gz >= 2).astype(jnp.int32)
    )

    def comps(ref):
        return [ref.at[c] for c in range(3)]

    V0, A1, MA, V1, A0, MA0 = (comps(r) for r in (v0, a1, ma, v1, a0, ma0))

    zeros_layer = jnp.zeros((PITCH, CY), F32)
    zeros_rows = jnp.zeros((LAYERS, CY), F32)
    for ref in V0 + A1 + MA + V1 + A0 + MA0 + [p1, m1, m0]:
        ref[0:PITCH, :] = zeros_layer
        ref[ROWS - PITCH:ROWS, :] = zeros_layer

    @pl.when(jnp.logical_not(has_xm))
    def _():
        for ref in V0 + [A1[0]] + MA + V1 + [A0[0]] + MA0:
            ref[pl.ds(7, LAYERS, stride=PITCH), :] = zeros_rows

    @pl.when(jnp.logical_not(has_xp))
    def _():
        for ref in V0 + MA + [A1[2]] + V1 + MA0 + [p1, m1, m0]:
            ref[pl.ds(24, LAYERS, stride=PITCH), :] = zeros_rows

    def ld(ref, z, dx=0):
        return ref[pl.ds((z + 1) * PITCH + 8 + dx, CX), :]

    def st(ref, z, value):
        ref[pl.ds(pl.multiple_of((z + 1) * PITCH + 8, 8), CX), :] = value

    def halo(blk, z, f):
        return pltpu.roll(blk[z & 3], (CY - ((z >> 2) * 16 + 2 * f)) & (CY - 1), 1)

    def ylo(u, blk, z, f):
        return jnp.where(lane == 0, halo(blk, z, f), pltpu.roll(u, 1, 1))

    def yhi(u, blk, z, f):
        shift = CY - 2 - (z >> 2) * 16 - 2 * f
        return jnp.where(lane == CY - 1, pltpu.roll(blk[z & 3], shift, 1), pltpu.roll(u, CY - 1, 1))

    def merge(dst, low, high, planes=range(4)):
        for zz in planes:
            dst[zz] = jnp.where((lane & 1) == 0, low[zz], pltpu.roll(high[zz], CY - 2, 1))

    def lap(ref, z, blk, f):
        c = ld(ref, z)
        h = halo(blk, z, f)
        low = jnp.where(lane == 0, h, pltpu.roll(c, 1, 1))
        high = jnp.where(lane == CY - 1, h, pltpu.roll(c, CY - 1, 1))
        total = ld(ref, z, 1) + ld(ref, z, -1) + (ld(ref, z + 1) + ld(ref, z - 1))
        return total + (low + high) - 6.0 * c, low

    def div(refs, z, low):
        x, y, w = (ld(r, z) for r in refs)
        return (x - ld(refs[0], z, -1)) + (y - low) + (w - ld(refs[2], z - 1))

    def grad(ref, z, yh, f):
        q = ld(ref, z)
        return ld(ref, z, 1) - q, yhi(q, yh, z, f) - q, ld(ref, z + 1) - q

    def s1(z, blk):
        lows = []
        for c in range(3):
            bend0[c, z], low = lap(V0[c], z, blk, c)
            lows.append(low)
            lm[c, z], _ = lap(MA[c], z, blk, 3 + c)
        st(p1, z, p0[z] + div(V0, z, lows[1]))
        st(m1, z, ap[z] - 0.25 * div(A1, z, ylo(ld(A1[1], z), blk, z, 6)))

    def s2(z, yh):
        gp, gm = grad(p1, z, yh, 0), grad(m1, z, yh, 1)
        g = ld(md, z)
        for c in range(3):
            st(V1[c], z, ld(V0[c], z) + 0.25 * (gp[c] + g * bend0[c, z]))
            new = ld(A1[c], z) + 0.25 * lm[c, z] - gm[c]
            st(A0[c], z, new)
            st(MA0[c], z, g * new)

    def s3(z, blk):
        total = None
        for c in range(3):
            part = ld(A1[c], z) * lap(V1[c], z, blk, c)[0] + ld(A0[c], z) * bend0[c, z]
            total = part if total is None else total + part
            lm0[c, z], _ = lap(MA0[c], z, blk, 3 + c)
        sh[z] = 0.25 * total
        st(m0, z, ld(m1, z) - 0.25 * div(A0, z, ylo(ld(A0[1], z), blk, z, 6)))

    def s4(z, yh):
        gm = grad(m0, z, yh, 0)
        for c in range(3):
            out[c, z] = ld(A0[c], z) + 0.25 * lm0[c, z] - gm[c]

    def every(fn, start=0, stop=CZ, unroll=UNROLL):
        turns = (stop - start) // unroll

        def step(n, carry):
            for k in range(unroll):
                fn(start + n * unroll + k)
            return carry

        lax.fori_loop(0, turns, step, 0)
        for z in range(start + turns * unroll, stop):
            fn(z)

    def some(fn, layers):
        for z in layers:
            fn(z)

    def pack_y(dst, fields):
        def step(zz, carry):
            acc = jnp.zeros((CX, CY), F32)
            for g in range(8):
                for f, ref in enumerate(fields):
                    s = g * 16 + 2 * f + 1
                    acc = jnp.where((lane >> 1) == (s >> 1), pltpu.roll(ld(ref, g * 4 + zz), s, 1), acc)
            dst[zz] = acc
            return carry
        lax.fori_loop(0, 4, step, 0)

    def pack_layers(dst, fields, layers, last=None):
        for zz in range(4):
            acc = jnp.zeros((CX, CY), F32)
            for z in layers:
                if z % 4 == zz:
                    for f, ref in enumerate(fields):
                        s = (z // 4) * 16 + 2 * f + 1
                        acc = jnp.where((lane >> 1) == (s >> 1), pltpu.roll(ld(ref, z), s, 1), acc)
            if zz == 3 and last is not None:
                acc = jnp.where(lane >= CY - 2, pltpu.roll(ld(last, CZ), CY - 1, 1), acc)
            dst[zz] = acc

    def face(ref, x):
        return ref[pl.ds(PITCH + 8 + x, CZ, stride=PITCH), :]

    def pack_x(dst, fields, x):
        for i, ref in enumerate(fields):
            dst[i * CZ:(i + 1) * CZ, :] = face(ref, x)

    def unpack_x(src, fields, x):
        for i, ref in enumerate(fields):
            ref[pl.ds(PITCH + 8 + x, CZ, stride=PITCH), :] = src[i * CZ:(i + 1) * CZ, :]

    def rows_of(pairs, x):
        return [(ref, (z + 1) * PITCH + 8 + x) for ref, z in pairs]

    def pack_rows(dst, pairs, x):
        for i, (ref, row) in enumerate(rows_of(pairs, x)):
            dst[i:i + 1, :] = ref[row:row + 1, :]

    def unpack_rows(src, pairs, x):
        for i, (ref, row) in enumerate(rows_of(pairs, x)):
            ref[row:row + 1, :] = src[i:i + 1, :]

    def store(start, size, n):
        part = pl.ds(start, size)
        copies = [
            pltpu.make_async_copy(out.at[:, part], o_av.at[:, part], out_sem.at[3 * n]),
            pltpu.make_async_copy(
                m0.reshape(LAYERS, PITCH, CY).at[pl.ds(start + 1, size), pl.ds(8, CX), :],
                o_ap.at[part], out_sem.at[3 * n + 1],
            ),
            pltpu.make_async_copy(sh.at[part], o_sh.at[part], out_sem.at[3 * n + 2]),
        ]
        for copy in copies:
            copy.start()
        return copies

    class Link:
        def __init__(self, src, dst, send, recv, device, sends, gets):
            self.copy = pltpu.make_async_remote_copy(
                src_ref=src, dst_ref=dst, send_sem=send, recv_sem=recv,
                device_id=device, device_id_type=MESH,
            )
            self.sends, self.gets = sends, gets

        def start(self):
            pl.when(self.sends)(self.copy.start)

        def arrive(self):
            pl.when(self.gets)(self.copy.wait_recv)

        def flush(self):
            pl.when(self.sends)(self.copy.wait_send)

    links = []
    counts = {"x": 0, "y": 0, "z": 0}

    def link(kind, src, dst, device, sends, gets):
        n = counts[kind]
        counts[kind] += 1
        ss, rs = {"x": (xs_sem, xr_sem), "y": (ys_sem, yr_sem), "z": (zs_sem, zr_sem)}[kind]
        made = Link(src, dst, ss.at[n], rs.at[n], device, sends, gets)
        links.append(made)
        return made

    def x_down(src, dst):
        return link("x", src, dst, (gx - 1, gy, gz), has_xm, has_xp)

    def x_up(src, dst):
        return link("x", src, dst, (gx + 1, gy, gz), has_xp, has_xm)

    def y_down(src, dst):
        return link("y", src, dst, (gx, gy - 1, gz), has_ym, has_yp)

    def y_up(src, dst):
        return link("y", src, dst, (gx, gy + 1, gz), has_yp, has_ym)

    def z_down(src, dst):
        return link("z", src, dst, (gx, gy, gz - 1), has_zm, has_zp)

    def z_up(src, dst):
        return link("z", src, dst, (gx, gy, gz + 1), has_zp, has_zm)

    def go(*those):
        for one in those:
            one.start()

    def got(*those):
        for one in those:
            one.arrive()

    for copy in loads:
        copy.wait()

    def weight(z):
        g = ld(md, z)
        for c in range(3):
            st(MA[c], z, g * ld(A1[c], z))

    every(weight)
    lo1 = V0 + MA
    rim = (0, 1, CZ - 1)
    x9 = [(ref, z) for ref in lo1 for z in rim]
    x9up = x9 + [(A1[0], z) for z in rim]
    pack_rows(xa9, x9, 0)
    pack_rows(xb9, x9up, CX - 1)
    pack_y(ys1, lo1 + [A1[1]])

    pl.semaphore_wait(barrier, expected)

    r9x = [x_down(xa9, xh9), x_up(xb9, xl9)]
    r1y = [y_down(ys1, yh1), y_up(ys1, yl1)]
    r1x = [x_down(xa1, xh1), x_up(xb1, xl1)]
    zraw = [
        z_up(avel.at[:, CZ - 1], zl.at[3:6]),
        z_down(avel.at[:, 0], zu.at[3:6]),
        z_up(modulus.at[CZ - 1], zl.at[6]),
        z_down(modulus.at[0], zu.at[6]),
        z_up(vel.at[:, CZ - 1], zl.at[0:3]),
        z_down(vel.at[:, 0], zu.at[0:3]),
    ]
    go(*r9x, *r1y, *zraw)
    pack_x(xa1, lo1, 0)
    pack_x(xb1, lo1 + [A1[0]], CX - 1)
    go(*r1x)

    for copy in sensors:
        copy.wait()
    owner_row = sowner[...].astype(F32)
    r0 = lax.broadcasted_iota(jnp.int32, (32, 32), 0)
    r1 = lax.broadcasted_iota(jnp.int32, (32, 32), 1)
    owner_col = jnp.sum(jnp.where(r0 == r1, owner_row, 0.0), axis=1, keepdims=True)
    rank = jnp.sum(
        jnp.where((owner_col == owner_row) & (r0 < r1), 1.0, 0.0), axis=0, keepdims=True
    ).astype(jnp.int32)
    owner_int = owner_row.astype(jnp.int32)
    own_gx, own_gy = owner_int >> 3, owner_int & 7
    place = own_gy * 32 + own_gx * 8 + rank
    code_row = (own_gx * 32 + sstep[...] * CX + sline[...] + 1).astype(F32)
    code_col = jnp.sum(jnp.where(r0 == r1, code_row, 0.0), axis=1, keepdims=True)
    slot = lax.broadcasted_iota(jnp.int32, (256, 32), 0)
    cs[...] = jnp.dot(
        (slot == place).astype(F32), svals[...], precision=HIGH, preferred_element_type=F32
    ) + jnp.dot(
        (slot == place + 4).astype(F32), jnp.broadcast_to(code_col, (32, CY)),
        precision=HIGH, preferred_element_type=F32,
    )
    mine = pl.ds(pl.multiple_of(gy * 32, 32), 32)
    gath[mine, :] = cs[mine, :]

    stage1 = []
    for step in range(1, NGY):
        other = lax.rem(gy + step, NGY)
        stage1.append(
            pltpu.make_async_remote_copy(
                src_ref=cs.at[pl.ds(pl.multiple_of(other * 32, 32), 32)],
                dst_ref=gath.at[mine],
                send_sem=f1s.at[step - 1], recv_sem=f1r.at[step - 1],
                device_id=(gx, other, gz), device_id_type=MESH,
            )
        )
        stage1[-1].start()

    got(*r9x, *r1y)

    @pl.when(has_xp)
    def _():
        unpack_rows(xh9, x9, CX)

    @pl.when(has_xm)
    def _():
        unpack_rows(xl9, x9up, -1)

    merge(c1, yl1, yh1)
    some(lambda z: s1(z, c1), rim)
    x10 = [(ref, z) for ref in (p1, m1) for z in (0, CZ - 1)]
    pack_rows(xa10, x10, 0)
    r10x = x_down(xa10, xh10)
    go(r10x)
    pack_layers(ys9, [p1, m1], (0, CZ - 1))
    r9y = y_down(ys9, yh9)
    zpm = [
        z_down(p1.at[pl.ds(PITCH + 8, CX)], zu.at[10]),
        z_down(m1.at[pl.ds(PITCH + 8, CX)], zu.at[11]),
    ]
    go(r9y, *zpm)
    for copy in stage1:
        copy.wait_recv()
    rows = gath[...]
    r256 = lax.broadcasted_iota(jnp.int32, (256, CY), 0)
    l256 = lax.broadcasted_iota(jnp.int32, (256, CY), 1)
    codes = pltpu.roll(rows, 252, 0)
    hot = jnp.where(((r256 & 7) < 4) & (codes == (l256 + 1).astype(F32)), 1.0, 0.0)
    dense[...] = lax.dot_general(
        hot, rows, (((0,), (0,)), ((), ())), precision=HIGH, preferred_element_type=F32
    )
    stage2 = []
    for step in range(1, NGX):
        other = lax.rem(gx + step, NGX)
        stage2.append(
            pltpu.make_async_remote_copy(
                src_ref=dense.at[pl.ds(pl.multiple_of(other * 32, 32), 32)],
                dst_ref=hsum.at[step - 1],
                send_sem=f2s.at[step - 1], recv_sem=f2r.at[step - 1],
                device_id=(other, gy, gz), device_id_type=MESH,
            )
        )
        stage2[-1].start()

    got(r10x, r9y)

    @pl.when(has_xp)
    def _():
        unpack_rows(xh10, x10, CX)

    some(lambda z: s2(z, yh9), (0, CZ - 1))
    first, final = pl.ds(PITCH + 8, CX), pl.ds(CZ * PITCH + 8, CX)
    zpart = [
        z_up(a0.at[:, final], zl.at[7:10]),
        z_down(a0.at[:, first], zu.at[7:10]),
    ]
    go(*zpart)

    got(*r1x)

    @pl.when(has_xp)
    def _():
        unpack_x(xh1, lo1, CX)

    @pl.when(has_xm)
    def _():
        unpack_x(xl1, lo1 + [A1[0]], -1)

    every(lambda z: s1(z, c1), 2, CZ - 1)
    pack_x(xa2, [p1, m1], 0)
    r2x = x_down(xa2, xh2)
    go(r2x)
    pack_y(ys2, [p1, m1])
    r2y = y_down(ys2, yh2)
    go(r2y)

    for copy in stage2:
        copy.wait_recv()
    own = dense[pl.ds(pl.multiple_of(gx * 32, 32), 32), :]
    esum[...] = own + hsum[0] + hsum[1] + hsum[2]

    @pl.when(gz > 0)
    def _():
        to_surface = pltpu.make_async_remote_copy(
            src_ref=esum, dst_ref=ksum.at[gz - 1], send_sem=f3s, recv_sem=f3r.at[gz - 1],
            device_id=(gx, gy, 0), device_id_type=MESH,
        )
        to_surface.start()

    got(r2x, r2y)

    @pl.when(has_xp)
    def _():
        unpack_x(xh2, [p1, m1], CX)

    every(lambda z: s2(z, yh2), 1, CZ - 1)

    lo3 = V1 + MA0
    pack_x(xa3, lo3, 0)
    pack_x(xb3, lo3 + [A0[0]], CX - 1)
    r3x = [x_down(xa3, xh3), x_up(xb3, xl3)]
    go(*r3x)
    pack_y(ys3, lo3 + [A0[1]])
    r3y = [y_down(ys3, yh3), y_up(ys3, yl3)]
    go(*r3y)

    for one in zpart + zpm:
        one.flush()
    got(*zraw, *zpm)

    surface = gz == 0
    r5x = [
        link("x", xa5, xh5, (gx - 1, gy, gz), surface & has_xm, surface & has_xp),
        link("x", xb5, xl5, (gx + 1, gy, gz), surface & has_xp, surface & has_xm),
    ]
    r5y = [
        link("y", ys5, yh5, (gx, gy - 1, gz), surface & has_ym, surface & has_yp),
        link("y", ys5, yl5, (gx, gy + 1, gz), surface & has_yp, surface & has_ym),
    ]

    @pl.when(surface)
    def _():
        for other in range(1, NGZ):
            pltpu.make_async_remote_copy(
                src_ref=esum, dst_ref=ksum.at[other - 1], send_sem=f3s, recv_sem=f3r.at[other - 1],
                device_id=(gx, gy, 1), device_id_type=MESH,
            ).wait_recv()
        total = esum[...]
        for other in range(1, NGZ):
            total = total + ksum[other - 1]
        esum[...] = total
        w = ld(A1[2], 0) + total[CX:2 * CX]
        st(A1[2], 0, w)
        w = w * ld(md, 0)
        st(MA[2], 0, w)
        pack_rows(xa5, [(MA[2], 0)], 0)
        pack_rows(xb5, [(MA[2], 0)], CX - 1)
        ys5[...] = pltpu.roll(w, 11, 1)

    go(*r5x, *r5y)


    @pl.when(has_zm)
    def _():
        for c in range(3):
            st(V0[c], -1, zl[c])
            st(MA[c], -1, zl[6] * zl[3 + c])
        st(A1[2], -1, zl[5])

    @pl.when(has_zp)
    def _():
        for c in range(3):
            st(V0[c], CZ, zu[c])
            st(MA[c], CZ, zu[6] * zu[3 + c])
        st(p1, CZ, zu[10] - ld(V0[2], CZ - 1))
        st(m1, CZ, zu[11] + 0.25 * ld(A1[2], CZ - 1))

    some(lambda z: s1(z, c1), rim)
    x6 = [(p1, 0), (m1, 0), (m1, 1), (A1[2], CZ - 1)]
    pack_rows(xa6, x6, 0)
    r6x = x_down(xa6, xh6)
    go(r6x)
    pack_layers(ys6, [p1, m1, A1[2]], rim)
    r6y = y_down(ys6, yh6)
    go(r6y)

    got(r6x, r6y, *r5x, *r5y)
    @pl.when(surface & has_xp)
    def _():
        unpack_rows(xh5, [(MA[2], 0)], CX)

    @pl.when(surface & has_xm)
    def _():
        unpack_rows(xl5, [(MA[2], 0)], -1)

    @pl.when(surface & has_yp)
    def _():
        yh1[0] = jnp.where(lane == 11, yh5[...], yh1[0])

    @pl.when(surface & has_ym)
    def _():
        yl1[0] = jnp.where(lane == 10, yl5[...], yl1[0])

    @pl.when(surface)
    def _():
        merge(c1, yl1, yh1, (0,))
        lm[2, 0], _ = lap(MA[2], 0, c1, 5)


    @pl.when(has_xp)
    def _():
        unpack_rows(xh6, x6, CX)

    some(lambda z: s2(z, yh6), rim)

    to_up[...] = sum(ld(V1[c], CZ - 1) * zu[3 + c] for c in range(3))
    to_down[...] = sum(ld(V1[c], 0) * zl[3 + c] for c in range(3))
    zshare = [z_up(to_up, from_low), z_down(to_down, from_high)]
    go(*zshare)
    got(*zpart)

    @pl.when(surface)
    def _():
        w = ld(A0[2], 0) + esum[0:CX, :]
        st(A0[2], 0, w)
        st(MA0[2], 0, w * ld(md, 0))

    @pl.when(has_zm)
    def _():
        g = zl[6]
        extra = ld(m1, 0)
        for c in range(3):
            a = zl[7 + c] + 0.25 * ld(MA[c], 0) - (extra if c == 2 else 0.0)
            st(A0[c], -1, a)
            st(MA0[c], -1, g * a)

    @pl.when(has_zp)
    def _():
        g = zu[6]
        top = CZ - 1
        w = ld(A1[2], top)
        gw = (ld(A1[2], top, 1) - w, yhi(w, yh6, top, 2) - w, -w)
        for c in range(3):
            a = zu[7 + c] + 0.25 * (ld(MA[c], top) - gw[c])
            st(A0[c], CZ, a)
            st(MA0[c], CZ, g * a)

    x7 = [(ref, z) for ref in lo3 for z in (0, 1, CZ - 1)]
    x7up = x7 + [(A0[0], z) for z in (0, 1, CZ - 1, CZ)]
    pack_rows(xa7, x7, 0)
    pack_rows(xb7, x7up, CX - 1)
    r7x = [x_down(xa7, xh7), x_up(xb7, xl7)]
    go(*r7x)
    edges = (0, 1, 2, CZ - 2, CZ - 1)
    pack_layers(ys7, lo3 + [A0[1]], edges, last=A0[1])
    r7y = [y_down(ys7, yh7), y_up(ys7, yl7)]
    go(*r7y)
    got(*r3x, *r3y)

    @pl.when(has_xp)
    def _():
        unpack_x(xh3, lo3, CX)

    @pl.when(has_xm)
    def _():
        unpack_x(xl3, lo3 + [A0[0]], -1)

    merge(c3, yl3, yh3)
    every(lambda z: s3(z, c3), 3, CZ - 2)
    pack_x(xa4, [m0], 0)
    r4x = x_down(xa4, xh4)
    go(r4x)
    pack_y(ys4, [m0])
    r4y = y_down(ys4, yh4)
    go(r4y)

    got(*r7x, *r7y)

    @pl.when(has_xp)
    def _():
        unpack_rows(xh7, x7, CX)

    @pl.when(has_xm)
    def _():
        unpack_rows(xl7, x7up, -1)

    merge(c7, yl7, yh7)
    some(lambda z: s3(z, c7), edges)

    @pl.when(has_zp)
    def _():
        x, y, w = (ld(r, CZ) for r in A0)
        low = jnp.where(lane == 0, pltpu.roll(yl7[3], 2, 1), pltpu.roll(y, 1, 1))
        d = (x - ld(A0[0], CZ, -1)) + (y - low) + (w - ld(A0[2], CZ - 1))
        st(m0, CZ, ld(m1, CZ) - 0.25 * d)

    x8 = [(m0, z) for z in edges + (CZ - 3,)]
    pack_rows(xa8, x8, 0)
    r8x = x_down(xa8, xh8)
    go(r8x)
    pack_layers(ys8, [m0], edges + (CZ - 3,))
    r8y = y_down(ys8, yh8)
    go(r8y)
    got(r4x, r4y)

    @pl.when(has_xp)
    def _():
        unpack_x(xh4, [m0], CX)

    every(lambda z: s4(z, yh4), 3, CZ - 3)
    early = store(3, CZ - 6, 0)
    got(r8x, r8y)

    @pl.when(has_xp)
    def _():
        unpack_rows(xh8, x8, CX)

    some(lambda z: s4(z, yh8), (0, 1, 2, CZ - 3, CZ - 2, CZ - 1))
    got(*zshare)

    @pl.when(has_zm)
    def _():
        sh[0] = sh[0] + 0.25 * from_low[...]

    @pl.when(has_zp)
    def _():
        sh[CZ - 1] = sh[CZ - 1] + 0.25 * from_high[...]

    late = store(0, 3, 1) + store(CZ - 3, 3, 2)
    for one in links:
        if one not in zpart and one not in zpm:
            one.flush()
    for copy in stage1 + stage2:
        copy.wait_send()

    @pl.when(gz > 0)
    def _():
        pltpu.make_async_remote_copy(
            src_ref=esum, dst_ref=ksum.at[gz - 1], send_sem=f3s, recv_sem=f3r.at[gz - 1],
            device_id=(gx, gy, 0), device_id_type=MESH,
        ).wait_send()

    for copy in early + late:
        copy.wait()


def hand_out(a, b, c, oa, ob, oc, sem):
    pieces = [(a.at[k], oa.at[k]) for k in range(3)] + [(b, ob), (c, oc)]
    copies = [pltpu.make_async_copy(p[0], p[1], sem.at[k]) for k, p in enumerate(pieces)]
    for copy in copies:
        copy.start()
    for copy in copies:
        copy.wait()


def shards(vel, pres, modulus, avel, apres, svals, sowner, sline, sstep):
    vector = pltpu.VMEM((3, ROWS, CY), F32)
    scalar = pltpu.VMEM((ROWS, CY), F32)
    flat3 = pltpu.VMEM((3, CZ, CX, CY), F32)
    flat = pltpu.VMEM((CZ, CX, CY), F32)
    pack = pltpu.VMEM((4, CX, CY), F32)
    plane = pltpu.VMEM((CX, CY), F32)
    ints = pltpu.VMEM((1, 32), jnp.int32)

    def lines(n):
        return pltpu.VMEM((n, CY), F32)

    def dma(n):
        return pltpu.SemaphoreType.DMA((n,))

    anywhere = pl.BlockSpec(memory_space=pl.ANY)
    sowner, sline, sstep = (a.reshape(1, 32) for a in (sowner, sline, sstep))
    operands = [
        pltpu.with_memory_space_constraint(a, pltpu.HBM)
        for a in (vel, pres, modulus, avel, apres, svals, sowner, sline, sstep)
    ]
    vel, pres, modulus, avel, apres, svals, sowner, sline, sstep = operands
    inner = pl.pallas_call(
        body,
        out_shape=(
            jax.ShapeDtypeStruct((3, CZ, CX, CY), F32),
            jax.ShapeDtypeStruct((CZ, CX, CY), F32),
            jax.ShapeDtypeStruct((CZ, CX, CY), F32),
        ),
        in_specs=[anywhere] * 9,
        out_specs=(anywhere,) * 3,
        scratch_shapes=[
            vector, vector, vector, scalar, scalar, scalar, vector, vector, vector, scalar,
            flat, flat, flat3, flat3, flat3, flat, flat3,
            pack, pack, pack, pack, pack, pack, pack, pack, pack, pack,
            pack, pack, pack, pack, pack, lines(24), lines(24), lines(24), lines(24), lines(8), lines(8),
            plane, plane, plane, pack, pack, pack, pack, pack, pack, pack,
            lines(6 * CZ), lines(7 * CZ), lines(6 * CZ), lines(7 * CZ),
            lines(2 * CZ), lines(2 * CZ),
            lines(6 * CZ), lines(7 * CZ), lines(6 * CZ), lines(7 * CZ),
            lines(CZ), lines(CZ),
            lines(8), lines(8), lines(8), lines(8), lines(8), lines(8),
            lines(24), lines(24), lines(24), lines(24), lines(8), lines(8),
            lines(32), ints, ints, ints,
            pltpu.VMEM((10, CX, CY), F32), pltpu.VMEM((12, CX, CY), F32),
            plane, plane, plane, plane,
            lines(256), lines(256), lines(CY), pltpu.VMEM((3, 32, CY), F32), lines(32),
            pltpu.VMEM((NGZ - 1, 32, CY), F32),
            dma(9), dma(9), dma(15), dma(15), dma(13), dma(13), dma(12), dma(12),
            dma(NGY - 1), dma(NGY - 1), dma(NGX - 1), dma(NGX - 1),
            pltpu.SemaphoreType.DMA, dma(NGZ - 1),
        ],
        compiler_params=pltpu.CompilerParams(
            collective_id=0, has_side_effects=True, vmem_limit_bytes=40 * 2**20
        ),
        cost_estimate=pl.CostEstimate(flops=20_000_000, bytes_accessed=3_670_016, transcendentals=0),
        name="adjoint",
    )(vel, pres, modulus, avel, apres, svals, sowner, sline, sstep)
    return pl.pallas_call(
        hand_out,
        out_shape=[jax.ShapeDtypeStruct(a.shape, F32) for a in inner],
        in_specs=[pl.BlockSpec(memory_space=pltpu.VMEM)] * 3,
        out_specs=[pl.BlockSpec(memory_space=pltpu.HBM)] * 3,
        scratch_shapes=[dma(5)],
        compiler_params=pltpu.CompilerParams(vmem_limit_bytes=16 * 2**20),
        name="handout",
    )(*inner)


def solution(mesh):
    return jax.shard_map(
        shards,
        mesh=mesh,
        in_specs=(
            P(None, "gz", "gx", "gy"),
            P("gz", "gx", "gy"),
            P("gz", "gx", "gy"),
            P(None, "gz", "gx", "gy"),
            P("gz", "gx", "gy"),
            P(("gx", "gy", "gz"), None),
            P(("gx", "gy", "gz"), None),
            P(("gx", "gy", "gz")),
            P(("gx", "gy", "gz")),
        ),
        out_specs=(P(None, "gz", "gx", "gy"), P("gz", "gx", "gy"), P("gz", "gx", "gy")),
        check_vma=False,
    )
```

```python
import jax
import jax.numpy as jnp
from jax import lax
from jax.experimental import pallas as pl
from jax.experimental.pallas import tpu as pltpu
from jax.sharding import PartitionSpec as P

MESH = pl.DeviceIdType.MESH
F32 = jnp.float32
CZ, CX, CY = 32, 16, 128
PITCH = 32
LAYERS = CZ + 2
ROWS = LAYERS * PITCH
NGX, NGY, NGZ = 4, 8, 8
UNROLL = 8
HIGH = lax.Precision.HIGHEST


def body(
    vel, pres, modulus, avel, apres, svals_h, sowner_h, sline_h, sstep_h,
    o_av, o_ap, o_sh,
    v0, a1, ma, md, p1, m1, v1, a0, ma0, m0,
    p0, ap, bend0, lm, lm0, sh, out,
    ys1, yl1, yh1, ys2, yh2, ys3, yl3, yh3, ys4, yh4,
    c1, c3, c7, ys9, yh9, xa9, xb9, xl9, xh9, xa10, xh10,
    ys5, yl5, yh5, ys6, yh6, ys7, yl7, yh7, ys8, yh8,
    xa1, xb1, xh1, xl1, xa2, xh2, xa3, xb3, xh3, xl3, xa4, xh4,
    xa5, xb5, xh5, xl5, xa6, xh6, xa7, xb7, xh7, xl7, xa8, xh8,
    svals, sowner, sline, sstep,
    zl, zu, to_up, to_down, from_low, from_high, cs, gath, dense, hsum, esum, ksum,
    in_sem, out_sem, xs_sem, xr_sem, ys_sem, yr_sem, zs_sem, zr_sem,
    f1s, f1r, f2s, f2r, f3s, f3r,
):
    gx, gy, gz = lax.axis_index("gx"), lax.axis_index("gy"), lax.axis_index("gz")
    has_xm, has_xp = gx > 0, gx < NGX - 1
    has_ym, has_yp = gy > 0, gy < NGY - 1
    has_zm, has_zp = gz > 0, gz < NGZ - 1
    barrier = pltpu.get_barrier_semaphore()

    def grid3(ref):
        if len(ref.shape) == 3:
            return ref.reshape(3, LAYERS, PITCH, CY).at[:, pl.ds(1, CZ), pl.ds(8, CX), :]
        return ref.reshape(LAYERS, PITCH, CY).at[pl.ds(1, CZ), pl.ds(8, CX), :]

    loads = [
        pltpu.make_async_copy(src, dst, in_sem.at[i])
        for i, (src, dst) in enumerate(
            [(avel, grid3(a1)), (modulus, grid3(md)), (vel, grid3(v0)), (pres, p0), (apres, ap)]
        )
    ]
    sensors = [
        pltpu.make_async_copy(src, dst, in_sem.at[5 + i])
        for i, (src, dst) in enumerate(
            [(svals_h, svals), (sowner_h, sowner), (sline_h, sline), (sstep_h, sstep)]
        )
    ]
    for copy in loads + sensors:
        copy.start()

    lane = lax.broadcasted_iota(jnp.int32, (CX, CY), 1)

    @pl.when(jnp.logical_not(has_ym))
    def _():
        for ref in (yl1, yl3, yl7):
            ref[...] = jnp.zeros(ref.shape, F32)
        yl5[...] = jnp.zeros(yl5.shape, F32)

    @pl.when(jnp.logical_not(has_yp))
    def _():
        for ref in (yh1, yh2, yh3, yh4, yh6, yh7, yh8, yh9):
            ref[...] = jnp.zeros(ref.shape, F32)
        yh5[...] = jnp.zeros(yh5.shape, F32)

    def greet(device):
        pl.semaphore_signal(barrier, inc=1, device_id=device, device_id_type=MESH)

    @pl.when(has_zm)
    def _():
        greet((gx, gy, gz - 1))

    @pl.when(has_zp)
    def _():
        greet((gx, gy, gz + 1))

    @pl.when(gz == 0)
    def _():
        for other in range(2, NGZ):
            greet((gx, gy, other))

    for step in range(1, NGY):
        greet((gx, lax.rem(gy + step, NGY), gz))
    for step in range(1, NGX):
        greet((lax.rem(gx + step, NGX), gy, gz))
    expected = (
        NGX - 1 + NGY - 1
        + has_zm.astype(jnp.int32) + has_zp.astype(jnp.int32) + (gz >= 2).astype(jnp.int32)
    )

    def comps(ref):
        return [ref.at[c] for c in range(3)]

    V0, A1, MA, V1, A0, MA0 = (comps(r) for r in (v0, a1, ma, v1, a0, ma0))

    zeros_layer = jnp.zeros((PITCH, CY), F32)
    zeros_rows = jnp.zeros((LAYERS, CY), F32)
    for ref in V1:
        ref[pl.ds(7, LAYERS, stride=PITCH), :] = zeros_rows
        ref[pl.ds(24, LAYERS, stride=PITCH), :] = zeros_rows
    for ref in V0 + A1 + MA + V1 + A0 + MA0 + [p1, m1, m0]:
        ref[0:PITCH, :] = zeros_layer
        ref[ROWS - PITCH:ROWS, :] = zeros_layer

    @pl.when(jnp.logical_not(has_xm))
    def _():
        for ref in V0 + [A1[0]] + MA + [A0[0]] + MA0:
            ref[pl.ds(7, LAYERS, stride=PITCH), :] = zeros_rows

    @pl.when(jnp.logical_not(has_xp))
    def _():
        for ref in V0 + MA + [A1[2]] + MA0 + [p1, m1, m0]:
            ref[pl.ds(24, LAYERS, stride=PITCH), :] = zeros_rows

    def ld(ref, z, dx=0):
        return ref[pl.ds((z + 1) * PITCH + 8 + dx, CX), :]

    def st(ref, z, value):
        ref[pl.ds(pl.multiple_of((z + 1) * PITCH + 8, 8), CX), :] = value

    def halo(blk, z, f):
        return pltpu.roll(blk[z & 3], (CY - ((z >> 2) * 16 + 2 * f)) & (CY - 1), 1)

    def ylo(u, blk, z, f):
        return jnp.where(lane == 0, halo(blk, z, f), pltpu.roll(u, 1, 1))

    def yhi(u, blk, z, f):
        shift = CY - 2 - (z >> 2) * 16 - 2 * f
        return jnp.where(lane == CY - 1, pltpu.roll(blk[z & 3], shift, 1), pltpu.roll(u, CY - 1, 1))

    def merge(dst, low, high, planes=range(4)):
        for zz in planes:
            dst[zz] = jnp.where((lane & 1) == 0, low[zz], pltpu.roll(high[zz], CY - 2, 1))

    def lap(ref, z, blk, f):
        c = ld(ref, z)
        h = halo(blk, z, f)
        low = jnp.where(lane == 0, h, pltpu.roll(c, 1, 1))
        high = jnp.where(lane == CY - 1, h, pltpu.roll(c, CY - 1, 1))
        total = ld(ref, z, 1) + ld(ref, z, -1) + (ld(ref, z + 1) + ld(ref, z - 1))
        return total + (low + high) - 6.0 * c, low

    def div(refs, z, low):
        x, y, w = (ld(r, z) for r in refs)
        return (x - ld(refs[0], z, -1)) + (y - low) + (w - ld(refs[2], z - 1))

    def grad(ref, z, yh, f):
        q = ld(ref, z)
        return ld(ref, z, 1) - q, yhi(q, yh, z, f) - q, ld(ref, z + 1) - q

    def s1(z, blk):
        lows = []
        for c in range(3):
            bend0[c, z], low = lap(V0[c], z, blk, c)
            lows.append(low)
            lm[c, z], _ = lap(MA[c], z, blk, 3 + c)
        st(p1, z, p0[z] + div(V0, z, lows[1]))
        st(m1, z, ap[z] - 0.25 * div(A1, z, ylo(ld(A1[1], z), blk, z, 6)))

    def s2(z, yh):
        gp, gm = grad(p1, z, yh, 0), grad(m1, z, yh, 1)
        g = ld(md, z)
        for c in range(3):
            st(V1[c], z, ld(V0[c], z) + 0.25 * (gp[c] + g * bend0[c, z]))
            new = ld(A1[c], z) + 0.25 * lm[c, z] - gm[c]
            st(A0[c], z, new)
            st(MA0[c], z, g * new)

    def s3(z, blk):
        total = None
        for c in range(3):
            part = ld(A1[c], z) * lap(V1[c], z, blk, c)[0] + ld(A0[c], z) * bend0[c, z]
            total = part if total is None else total + part
            lm0[c, z], _ = lap(MA0[c], z, blk, 3 + c)
        sh[z] = 0.25 * total
        st(m0, z, ld(m1, z) - 0.25 * div(A0, z, ylo(ld(A0[1], z), blk, z, 6)))

    def s4(z, yh):
        gm = grad(m0, z, yh, 0)
        for c in range(3):
            out[c, z] = ld(A0[c], z) + 0.25 * lm0[c, z] - gm[c]

    def every(fn, start=0, stop=CZ, unroll=UNROLL):
        turns = (stop - start) // unroll

        def step(n, carry):
            for k in range(unroll):
                fn(start + n * unroll + k)
            return carry

        lax.fori_loop(0, turns, step, 0)
        for z in range(start + turns * unroll, stop):
            fn(z)

    def some(fn, layers):
        for z in layers:
            fn(z)

    def pack_y(dst, fields):
        def step(zz, carry):
            acc = jnp.zeros((CX, CY), F32)
            for g in range(8):
                for f, ref in enumerate(fields):
                    s = g * 16 + 2 * f + 1
                    acc = jnp.where((lane >> 1) == (s >> 1), pltpu.roll(ld(ref, g * 4 + zz), s, 1), acc)
            dst[zz] = acc
            return carry
        lax.fori_loop(0, 4, step, 0)

    def pack_layers(dst, fields, layers, last=None):
        for zz in range(4):
            acc = jnp.zeros((CX, CY), F32)
            for z in layers:
                if z % 4 == zz:
                    for f, ref in enumerate(fields):
                        s = (z // 4) * 16 + 2 * f + 1
                        acc = jnp.where((lane >> 1) == (s >> 1), pltpu.roll(ld(ref, z), s, 1), acc)
            if zz == 3 and last is not None:
                acc = jnp.where(lane >= CY - 2, pltpu.roll(ld(last, CZ), CY - 1, 1), acc)
            dst[zz] = acc

    def face(ref, x):
        return ref[pl.ds(PITCH + 8 + x, CZ, stride=PITCH), :]

    def pack_x(dst, fields, x):
        for i, ref in enumerate(fields):
            dst[i * CZ:(i + 1) * CZ, :] = face(ref, x)

    def unpack_x(src, fields, x):
        for i, ref in enumerate(fields):
            ref[pl.ds(PITCH + 8 + x, CZ, stride=PITCH), :] = src[i * CZ:(i + 1) * CZ, :]

    def weigh_x(to, ref, x):
        for c in range(3):
            to[c][pl.ds(PITCH + 8 + x, CZ, stride=PITCH), :] = face(md, x) * face(ref[c], x)

    def row(ref, z, x):
        at = (z + 1) * PITCH + 8 + x
        return ref[at:at + 1, :]

    def weigh_rows(to, ref, layers, x):
        for z in layers:
            at = (z + 1) * PITCH + 8 + x
            for c in range(3):
                to[c][at:at + 1, :] = row(md, z, x) * row(ref[c], z, x)

    def rows_of(pairs, x):
        return [(ref, (z + 1) * PITCH + 8 + x) for ref, z in pairs]

    def pack_rows(dst, pairs, x):
        for i, (ref, row) in enumerate(rows_of(pairs, x)):
            dst[i:i + 1, :] = ref[row:row + 1, :]

    def unpack_rows(src, pairs, x):
        for i, (ref, row) in enumerate(rows_of(pairs, x)):
            ref[row:row + 1, :] = src[i:i + 1, :]

    def store(start, size, n):
        part = pl.ds(start, size)
        copies = [
            pltpu.make_async_copy(out.at[:, part], o_av.at[:, part], out_sem.at[3 * n]),
            pltpu.make_async_copy(
                m0.reshape(LAYERS, PITCH, CY).at[pl.ds(start + 1, size), pl.ds(8, CX), :],
                o_ap.at[part], out_sem.at[3 * n + 1],
            ),
            pltpu.make_async_copy(sh.at[part], o_sh.at[part], out_sem.at[3 * n + 2]),
        ]
        for copy in copies:
            copy.start()
        return copies

    class Link:
        def __init__(self, src, dst, send, recv, device, sends, gets):
            self.copy = pltpu.make_async_remote_copy(
                src_ref=src, dst_ref=dst, send_sem=send, recv_sem=recv,
                device_id=device, device_id_type=MESH,
            )
            self.sends, self.gets = sends, gets

        def start(self):
            pl.when(self.sends)(self.copy.start)

        def arrive(self):
            pl.when(self.gets)(self.copy.wait_recv)

        def flush(self):
            pl.when(self.sends)(self.copy.wait_send)

    links = []
    counts = {"x": 0, "y": 0, "z": 0}

    def link(kind, src, dst, device, sends, gets):
        n = counts[kind]
        counts[kind] += 1
        ss, rs = {"x": (xs_sem, xr_sem), "y": (ys_sem, yr_sem), "z": (zs_sem, zr_sem)}[kind]
        made = Link(src, dst, ss.at[n], rs.at[n], device, sends, gets)
        links.append(made)
        return made

    def x_down(src, dst):
        return link("x", src, dst, (gx - 1, gy, gz), has_xm, has_xp)

    def x_up(src, dst):
        return link("x", src, dst, (gx + 1, gy, gz), has_xp, has_xm)

    def y_down(src, dst):
        return link("y", src, dst, (gx, gy - 1, gz), has_ym, has_yp)

    def y_up(src, dst):
        return link("y", src, dst, (gx, gy + 1, gz), has_yp, has_ym)

    def z_down(src, dst):
        return link("z", src, dst, (gx, gy, gz - 1), has_zm, has_zp)

    def z_up(src, dst):
        return link("z", src, dst, (gx, gy, gz + 1), has_zp, has_zm)

    def go(*those):
        for one in those:
            one.start()

    def got(*those):
        for one in those:
            one.arrive()

    for copy in loads:
        copy.wait()

    def weight(z):
        g = ld(md, z)
        for c in range(3):
            st(MA[c], z, g * ld(A1[c], z))

    every(weight)
    lo1 = V0 + MA
    rim = (0, 1, CZ - 1)
    wide1 = V0 + A1 + [md]
    x9 = [(ref, z) for ref in wide1 for z in rim]
    pack_rows(xa9, x9, 0)
    pack_rows(xb9, x9, CX - 1)
    pack_y(ys1, lo1 + [A1[1]])

    pl.semaphore_wait(barrier, expected)

    r9x = [x_down(xa9, xh9), x_up(xb9, xl9)]
    r1y = [y_down(ys1, yh1), y_up(ys1, yl1)]
    r1x = [x_down(xa1, xh1), x_up(xb1, xl1)]
    zraw = [
        z_up(avel.at[:, CZ - 1], zl.at[3:6]),
        z_down(avel.at[:, 0], zu.at[3:6]),
        z_up(modulus.at[CZ - 1], zl.at[6]),
        z_down(modulus.at[0], zu.at[6]),
        z_up(vel.at[:, CZ - 1], zl.at[0:3]),
        z_down(vel.at[:, 0], zu.at[0:3]),
    ]
    go(*r9x, *r1y, *zraw)
    pack_x(xa1, wide1, 0)
    pack_x(xb1, wide1, CX - 1)
    go(*r1x)

    for copy in sensors:
        copy.wait()
    owner_row = sowner[...].astype(F32)
    r0 = lax.broadcasted_iota(jnp.int32, (32, 32), 0)
    r1 = lax.broadcasted_iota(jnp.int32, (32, 32), 1)
    owner_col = jnp.sum(jnp.where(r0 == r1, owner_row, 0.0), axis=1, keepdims=True)
    rank = jnp.sum(
        jnp.where((owner_col == owner_row) & (r0 < r1), 1.0, 0.0), axis=0, keepdims=True
    ).astype(jnp.int32)
    owner_int = owner_row.astype(jnp.int32)
    own_gx, own_gy = owner_int >> 3, owner_int & 7
    place = own_gy * 32 + own_gx * 8 + rank
    code_row = (own_gx * 32 + sstep[...] * CX + sline[...] + 1).astype(F32)
    code_col = jnp.sum(jnp.where(r0 == r1, code_row, 0.0), axis=1, keepdims=True)
    slot = lax.broadcasted_iota(jnp.int32, (256, 32), 0)
    cs[...] = jnp.dot(
        (slot == place).astype(F32), svals[...], precision=HIGH, preferred_element_type=F32
    ) + jnp.dot(
        (slot == place + 4).astype(F32), jnp.broadcast_to(code_col, (32, CY)),
        precision=HIGH, preferred_element_type=F32,
    )
    mine = pl.ds(pl.multiple_of(gy * 32, 32), 32)
    gath[mine, :] = cs[mine, :]

    stage1 = []
    for step in range(1, NGY):
        other = lax.rem(gy + step, NGY)
        stage1.append(
            pltpu.make_async_remote_copy(
                src_ref=cs.at[pl.ds(pl.multiple_of(other * 32, 32), 32)],
                dst_ref=gath.at[mine],
                send_sem=f1s.at[step - 1], recv_sem=f1r.at[step - 1],
                device_id=(gx, other, gz), device_id_type=MESH,
            )
        )
        stage1[-1].start()

    got(*r9x, *r1y)

    @pl.when(has_xp)
    def _():
        unpack_rows(xh9, x9, CX)
        weigh_rows(MA, A1, rim, CX)

    @pl.when(has_xm)
    def _():
        unpack_rows(xl9, x9, -1)
        weigh_rows(MA, A1, rim, -1)

    merge(c1, yl1, yh1)
    some(lambda z: s1(z, c1), rim)
    x10 = [(ref, z) for ref in (p1, m1) for z in (0, CZ - 1)]
    pack_rows(xa10, x10, 0)
    r10x = x_down(xa10, xh10)
    go(r10x)
    pack_layers(ys9, [p1, m1], (0, CZ - 1))
    r9y = y_down(ys9, yh9)
    zpm = [
        z_down(p1.at[pl.ds(PITCH + 8, CX)], zu.at[10]),
        z_down(m1.at[pl.ds(PITCH + 8, CX)], zu.at[11]),
    ]
    go(r9y, *zpm)
    for copy in stage1:
        copy.wait_recv()
    rows = gath[...]
    r256 = lax.broadcasted_iota(jnp.int32, (256, CY), 0)
    l256 = lax.broadcasted_iota(jnp.int32, (256, CY), 1)
    codes = pltpu.roll(rows, 252, 0)
    hot = jnp.where(((r256 & 7) < 4) & (codes == (l256 + 1).astype(F32)), 1.0, 0.0)
    dense[...] = lax.dot_general(
        hot, rows, (((0,), (0,)), ((), ())), precision=HIGH, preferred_element_type=F32
    )
    stage2 = []
    for step in range(1, NGX):
        other = lax.rem(gx + step, NGX)
        stage2.append(
            pltpu.make_async_remote_copy(
                src_ref=dense.at[pl.ds(pl.multiple_of(other * 32, 32), 32)],
                dst_ref=hsum.at[step - 1],
                send_sem=f2s.at[step - 1], recv_sem=f2r.at[step - 1],
                device_id=(other, gy, gz), device_id_type=MESH,
            )
        )
        stage2[-1].start()

    got(r10x, r9y)

    @pl.when(has_xp)
    def _():
        unpack_rows(xh10, x10, CX)

    some(lambda z: s2(z, yh9), (0, CZ - 1))
    first, final = pl.ds(PITCH + 8, CX), pl.ds(CZ * PITCH + 8, CX)
    zpart = [
        z_up(a0.at[:, final], zl.at[7:10]),
        z_down(a0.at[:, first], zu.at[7:10]),
    ]
    go(*zpart)

    got(*r1x)

    @pl.when(has_xp)
    def _():
        unpack_x(xh1, wide1, CX)
        weigh_x(MA, A1, CX)

    @pl.when(has_xm)
    def _():
        unpack_x(xl1, wide1, -1)
        weigh_x(MA, A1, -1)

    every(lambda z: s1(z, c1), 2, 14)

    for copy in stage2:
        copy.wait_recv()
    own = dense[pl.ds(pl.multiple_of(gx * 32, 32), 32), :]
    esum[...] = own + hsum[0] + hsum[1] + hsum[2]

    @pl.when(gz > 0)
    def _():
        to_surface = pltpu.make_async_remote_copy(
            src_ref=esum, dst_ref=ksum.at[gz - 1], send_sem=f3s, recv_sem=f3r.at[gz - 1],
            device_id=(gx, gy, 0), device_id_type=MESH,
        )
        to_surface.start()

    every(lambda z: s1(z, c1), 14, CZ - 1)
    pack_x(xa2, [p1, m1], 0)
    r2x = x_down(xa2, xh2)
    go(r2x)
    pack_y(ys2, [p1, m1])
    r2y = y_down(ys2, yh2)
    go(r2y)

    got(r2x, r2y)

    @pl.when(has_xp)
    def _():
        unpack_x(xh2, [p1, m1], CX)

    every(lambda z: s2(z, yh2), 1, CZ - 1)

    lo3 = V1 + MA0
    pack_x(xa3, A0, 0)
    pack_x(xb3, A0, CX - 1)
    xa3[3 * CZ:, :] = sum(face(V1[c], 0) * face(A1[c], -1) for c in range(3))
    xb3[3 * CZ:, :] = sum(face(V1[c], CX - 1) * face(A1[c], CX) for c in range(3))
    r3x = [x_down(xa3, xh3), x_up(xb3, xl3)]
    go(*r3x)
    pack_y(ys3, lo3 + [A0[1]])
    r3y = [y_down(ys3, yh3), y_up(ys3, yl3)]
    go(*r3y)

    for one in zpart + zpm:
        one.flush()
    got(*zraw, *zpm)

    surface = gz == 0
    r5x = [
        link("x", xa5, xh5, (gx - 1, gy, gz), surface & has_xm, surface & has_xp),
        link("x", xb5, xl5, (gx + 1, gy, gz), surface & has_xp, surface & has_xm),
    ]
    r5y = [
        link("y", ys5, yh5, (gx, gy - 1, gz), surface & has_ym, surface & has_yp),
        link("y", ys5, yl5, (gx, gy + 1, gz), surface & has_yp, surface & has_ym),
    ]

    @pl.when(surface)
    def _():
        for other in range(1, NGZ):
            pltpu.make_async_remote_copy(
                src_ref=esum, dst_ref=ksum.at[other - 1], send_sem=f3s, recv_sem=f3r.at[other - 1],
                device_id=(gx, gy, 1), device_id_type=MESH,
            ).wait_recv()
        total = esum[...]
        for other in range(1, NGZ):
            total = total + ksum[other - 1]
        esum[...] = total
        w = ld(A1[2], 0) + total[CX:2 * CX]
        st(A1[2], 0, w)
        w = w * ld(md, 0)
        st(MA[2], 0, w)
        pack_rows(xa5, [(A1[2], 0)], 0)
        pack_rows(xb5, [(A1[2], 0)], CX - 1)
        ys5[...] = pltpu.roll(w, 11, 1)

    go(*r5x, *r5y)


    @pl.when(has_zm)
    def _():
        for c in range(3):
            st(V0[c], -1, zl[c])
            st(MA[c], -1, zl[6] * zl[3 + c])
        st(A1[2], -1, zl[5])

    @pl.when(has_zp)
    def _():
        for c in range(3):
            st(V0[c], CZ, zu[c])
            st(MA[c], CZ, zu[6] * zu[3 + c])
        st(p1, CZ, zu[10] - ld(V0[2], CZ - 1))
        st(m1, CZ, zu[11] + 0.25 * ld(A1[2], CZ - 1))

    some(lambda z: s1(z, c1), rim)
    x6 = [(p1, 0), (m1, 0), (m1, 1), (A1[2], CZ - 1)]
    pack_rows(xa6, x6, 0)
    r6x = x_down(xa6, xh6)
    go(r6x)
    pack_layers(ys6, [p1, m1, A1[2]], rim)
    r6y = y_down(ys6, yh6)
    go(r6y)

    got(r6x, r6y, *r5x, *r5y)
    @pl.when(surface & has_xp)
    def _():
        unpack_rows(xh5, [(A1[2], 0)], CX)
        weigh_rows(MA, A1, (0,), CX)

    @pl.when(surface & has_xm)
    def _():
        unpack_rows(xl5, [(A1[2], 0)], -1)
        weigh_rows(MA, A1, (0,), -1)

    @pl.when(surface & has_yp)
    def _():
        yh1[0] = jnp.where(lane == 11, yh5[...], yh1[0])

    @pl.when(surface & has_ym)
    def _():
        yl1[0] = jnp.where(lane == 10, yl5[...], yl1[0])

    @pl.when(surface)
    def _():
        merge(c1, yl1, yh1, (0,))
        lm[2, 0], _ = lap(MA[2], 0, c1, 5)


    @pl.when(has_xp)
    def _():
        unpack_rows(xh6, x6, CX)

    some(lambda z: s2(z, yh6), rim)

    to_up[...] = sum(ld(V1[c], CZ - 1) * zu[3 + c] for c in range(3))
    to_down[...] = sum(ld(V1[c], 0) * zl[3 + c] for c in range(3))
    zshare = [z_up(to_up, from_low), z_down(to_down, from_high)]
    go(*zshare)
    got(*zpart)

    @pl.when(surface)
    def _():
        w = ld(A0[2], 0) + esum[0:CX, :]
        st(A0[2], 0, w)
        st(MA0[2], 0, w * ld(md, 0))

    @pl.when(has_zm)
    def _():
        g = zl[6]
        extra = ld(m1, 0)
        for c in range(3):
            a = zl[7 + c] + 0.25 * ld(MA[c], 0) - (extra if c == 2 else 0.0)
            st(A0[c], -1, a)
            st(MA0[c], -1, g * a)

    @pl.when(has_zp)
    def _():
        g = zu[6]
        top = CZ - 1
        w = ld(A1[2], top)
        gw = (ld(A1[2], top, 1) - w, yhi(w, yh6, top, 2) - w, -w)
        for c in range(3):
            a = zu[7 + c] + 0.25 * (ld(MA[c], top) - gw[c])
            st(A0[c], CZ, a)
            st(MA0[c], CZ, g * a)

    x7 = [(ref, z) for ref in A0 for z in rim]
    x7up = x7 + [(A0[0], CZ)]
    ends = (0, CZ - 1)
    pack_rows(xa7, x7, 0)
    pack_rows(xb7, x7up, CX - 1)
    for n, z in enumerate(ends):
        xa7[16 + n:17 + n, :] = sum(row(V1[c], z, 0) * row(A1[c], z, -1) for c in range(3))
        xb7[16 + n:17 + n, :] = sum(row(V1[c], z, CX - 1) * row(A1[c], z, CX) for c in range(3))
    r7x = [x_down(xa7, xh7), x_up(xb7, xl7)]
    go(*r7x)
    edges = (0, 1, 2, CZ - 2, CZ - 1)
    pack_layers(ys7, lo3 + [A0[1]], edges, last=A0[1])
    r7y = [y_down(ys7, yh7), y_up(ys7, yl7)]
    go(*r7y)
    got(*r3x, *r3y)

    @pl.when(has_xp)
    def _():
        unpack_x(xh3, A0, CX)
        weigh_x(MA0, A0, CX)

    @pl.when(has_xm)
    def _():
        unpack_x(xl3, A0, -1)
        weigh_x(MA0, A0, -1)

    merge(c3, yl3, yh3)
    every(lambda z: s3(z, c3), 3, CZ - 2)
    flat = sh.reshape(CZ * CX, CY)
    low, high = pl.ds(0, CZ, stride=CX), pl.ds(CX - 1, CZ, stride=CX)

    @pl.when(has_xp)
    def _():
        flat[high, :] = flat[high, :] + 0.25 * xh3[3 * CZ:, :]

    @pl.when(has_xm)
    def _():
        flat[low, :] = flat[low, :] + 0.25 * xl3[3 * CZ:, :]

    pack_x(xa4, [m0], 0)
    r4x = x_down(xa4, xh4)
    go(r4x)
    pack_y(ys4, [m0])
    r4y = y_down(ys4, yh4)
    go(r4y)

    got(*r7x, *r7y)

    @pl.when(has_xp)
    def _():
        unpack_rows(xh7, x7, CX)
        weigh_rows(MA0, A0, rim, CX)

    @pl.when(has_xm)
    def _():
        unpack_rows(xl7, x7up, -1)
        weigh_rows(MA0, A0, rim, -1)

    merge(c7, yl7, yh7)
    some(lambda z: s3(z, c7), edges)

    def add_share(x, ends_ref, bulk_ref):
        for z in edges:
            at = ends_ref[16 + ends.index(z):17 + ends.index(z), :] if z in ends else bulk_ref[3 * CZ + z:3 * CZ + z + 1, :]
            sh[z, x:x + 1, :] = sh[z, x:x + 1, :] + 0.25 * at

    @pl.when(has_xp)
    def _():
        add_share(CX - 1, xh7, xh3)

    @pl.when(has_xm)
    def _():
        add_share(0, xl7, xl3)

    @pl.when(has_zp)
    def _():
        x, y, w = (ld(r, CZ) for r in A0)
        low = jnp.where(lane == 0, pltpu.roll(yl7[3], 2, 1), pltpu.roll(y, 1, 1))
        d = (x - ld(A0[0], CZ, -1)) + (y - low) + (w - ld(A0[2], CZ - 1))
        st(m0, CZ, ld(m1, CZ) - 0.25 * d)

    x8 = [(m0, z) for z in edges + (CZ - 3,)]
    pack_rows(xa8, x8, 0)
    r8x = x_down(xa8, xh8)
    go(r8x)
    pack_layers(ys8, [m0], edges + (CZ - 3,))
    r8y = y_down(ys8, yh8)
    go(r8y)
    got(r4x, r4y)

    @pl.when(has_xp)
    def _():
        unpack_x(xh4, [m0], CX)

    every(lambda z: s4(z, yh4), 3, CZ - 3)
    early = store(3, CZ - 6, 0)
    got(r8x, r8y)

    @pl.when(has_xp)
    def _():
        unpack_rows(xh8, x8, CX)

    some(lambda z: s4(z, yh8), (0, 1, 2, CZ - 3, CZ - 2, CZ - 1))
    got(*zshare)

    @pl.when(has_zm)
    def _():
        sh[0] = sh[0] + 0.25 * from_low[...]

    @pl.when(has_zp)
    def _():
        sh[CZ - 1] = sh[CZ - 1] + 0.25 * from_high[...]

    late = store(0, 3, 1) + store(CZ - 3, 3, 2)
    for one in links:
        if one not in zpart and one not in zpm:
            one.flush()
    for copy in stage1 + stage2:
        copy.wait_send()

    @pl.when(gz > 0)
    def _():
        pltpu.make_async_remote_copy(
            src_ref=esum, dst_ref=ksum.at[gz - 1], send_sem=f3s, recv_sem=f3r.at[gz - 1],
            device_id=(gx, gy, 0), device_id_type=MESH,
        ).wait_send()

    for copy in early + late:
        copy.wait()


def hand_out(a, b, c, oa, ob, oc, sem):
    pieces = [(a.at[k], oa.at[k]) for k in range(3)] + [(b, ob), (c, oc)]
    copies = [pltpu.make_async_copy(p[0], p[1], sem.at[k]) for k, p in enumerate(pieces)]
    for copy in copies:
        copy.start()
    for copy in copies:
        copy.wait()


def shards(vel, pres, modulus, avel, apres, svals, sowner, sline, sstep):
    vector = pltpu.VMEM((3, ROWS, CY), F32)
    scalar = pltpu.VMEM((ROWS, CY), F32)
    flat3 = pltpu.VMEM((3, CZ, CX, CY), F32)
    flat = pltpu.VMEM((CZ, CX, CY), F32)
    pack = pltpu.VMEM((4, CX, CY), F32)
    plane = pltpu.VMEM((CX, CY), F32)
    ints = pltpu.VMEM((1, 32), jnp.int32)

    def lines(n):
        return pltpu.VMEM((n, CY), F32)

    def dma(n):
        return pltpu.SemaphoreType.DMA((n,))

    anywhere = pl.BlockSpec(memory_space=pl.ANY)
    sowner, sline, sstep = (a.reshape(1, 32) for a in (sowner, sline, sstep))
    operands = [
        pltpu.with_memory_space_constraint(a, pltpu.HBM)
        for a in (vel, pres, modulus, avel, apres, svals, sowner, sline, sstep)
    ]
    vel, pres, modulus, avel, apres, svals, sowner, sline, sstep = operands
    inner = pl.pallas_call(
        body,
        out_shape=(
            jax.ShapeDtypeStruct((3, CZ, CX, CY), F32),
            jax.ShapeDtypeStruct((CZ, CX, CY), F32),
            jax.ShapeDtypeStruct((CZ, CX, CY), F32),
        ),
        in_specs=[anywhere] * 9,
        out_specs=(anywhere,) * 3,
        scratch_shapes=[
            vector, vector, vector, scalar, scalar, scalar, vector, vector, vector, scalar,
            flat, flat, flat3, flat3, flat3, flat, flat3,
            pack, pack, pack, pack, pack, pack, pack, pack, pack, pack,
            pack, pack, pack, pack, pack, lines(24), lines(24), lines(24), lines(24), lines(8), lines(8),
            plane, plane, plane, pack, pack, pack, pack, pack, pack, pack,
            lines(7 * CZ), lines(7 * CZ), lines(7 * CZ), lines(7 * CZ),
            lines(2 * CZ), lines(2 * CZ),
            lines(4 * CZ), lines(4 * CZ), lines(4 * CZ), lines(4 * CZ),
            lines(CZ), lines(CZ),
            lines(8), lines(8), lines(8), lines(8), lines(8), lines(8),
            lines(24), lines(24), lines(24), lines(24), lines(8), lines(8),
            lines(32), ints, ints, ints,
            pltpu.VMEM((10, CX, CY), F32), pltpu.VMEM((12, CX, CY), F32),
            plane, plane, plane, plane,
            lines(256), lines(256), lines(CY), pltpu.VMEM((3, 32, CY), F32), lines(32),
            pltpu.VMEM((NGZ - 1, 32, CY), F32),
            dma(9), dma(9), dma(15), dma(15), dma(13), dma(13), dma(12), dma(12),
            dma(NGY - 1), dma(NGY - 1), dma(NGX - 1), dma(NGX - 1),
            pltpu.SemaphoreType.DMA, dma(NGZ - 1),
        ],
        compiler_params=pltpu.CompilerParams(
            collective_id=0, has_side_effects=True, vmem_limit_bytes=40 * 2**20
        ),
        cost_estimate=pl.CostEstimate(flops=20_000_000, bytes_accessed=3_670_016, transcendentals=0),
        name="adjoint",
    )(vel, pres, modulus, avel, apres, svals, sowner, sline, sstep)
    return pl.pallas_call(
        hand_out,
        out_shape=[jax.ShapeDtypeStruct(a.shape, F32) for a in inner],
        in_specs=[pl.BlockSpec(memory_space=pltpu.VMEM)] * 3,
        out_specs=[pl.BlockSpec(memory_space=pltpu.HBM)] * 3,
        scratch_shapes=[dma(5)],
        compiler_params=pltpu.CompilerParams(vmem_limit_bytes=16 * 2**20),
        name="handout",
    )(*inner)


def solution(mesh):
    return jax.shard_map(
        shards,
        mesh=mesh,
        in_specs=(
            P(None, "gz", "gx", "gy"),
            P("gz", "gx", "gy"),
            P("gz", "gx", "gy"),
            P(None, "gz", "gx", "gy"),
            P("gz", "gx", "gy"),
            P(("gx", "gy", "gz"), None),
            P(("gx", "gy", "gz"), None),
            P(("gx", "gy", "gz")),
            P(("gx", "gy", "gz")),
        ),
        out_specs=(P(None, "gz", "gx", "gy"), P("gz", "gx", "gy"), P("gz", "gx", "gy")),
        check_vma=False,
    )
```

```python
import jax
import jax.numpy as jnp
from jax import lax
from jax.experimental import pallas as pl
from jax.experimental.pallas import tpu as pltpu
from jax.sharding import PartitionSpec as P

MESH = pl.DeviceIdType.MESH
F32 = jnp.float32
CZ, CX, CY = 32, 16, 128
PITCH = 32
LAYERS = CZ + 2
ROWS = LAYERS * PITCH
NGX, NGY, NGZ = 4, 8, 8
UNROLL = 8
HIGH = lax.Precision.HIGHEST


def body(
    vel, pres, modulus, avel, apres, svals_h, sowner_h, sline_h, sstep_h,
    o_av, o_ap, o_sh,
    v0, a1, ma, md, p1, m1, v1, a0, ma0, m0,
    p0, ap, bend0, lm, lm0, sh, out,
    ys1, yl1, yh1, ys2, yh2, ys3, yl3, yh3, ys4, yh4,
    c1, c3, c7, ys9, yh9, xa9, xb9, xl9, xh9, xa10, xh10,
    ys5, yl5, yh5, ys6, yh6, ys7, yl7, yh7, ys8, yh8,
    xa1, xb1, xh1, xl1, xa2, xh2, xa3, xb3, xh3, xl3, xa4, xh4,
    xa5, xb5, xh5, xl5, xa6, xh6, xa7, xb7, xh7, xl7, xa8, xh8,
    svals, sowner, sline, sstep,
    zl, zu, to_up, to_down, from_low, from_high, cs, gath, dense, hsum, esum, ksum,
    in_sem, out_sem, xs_sem, xr_sem, ys_sem, yr_sem, zs_sem, zr_sem,
    f1s, f1r, f2s, f2r, f3s, f3r,
):
    gx, gy, gz = lax.axis_index("gx"), lax.axis_index("gy"), lax.axis_index("gz")
    has_xm, has_xp = gx > 0, gx < NGX - 1
    has_ym, has_yp = gy > 0, gy < NGY - 1
    has_zm, has_zp = gz > 0, gz < NGZ - 1
    barrier = pltpu.get_barrier_semaphore()

    def grid3(ref):
        if len(ref.shape) == 3:
            return ref.reshape(3, LAYERS, PITCH, CY).at[:, pl.ds(1, CZ), pl.ds(8, CX), :]
        return ref.reshape(LAYERS, PITCH, CY).at[pl.ds(1, CZ), pl.ds(8, CX), :]

    loads = [
        pltpu.make_async_copy(src, dst, in_sem.at[i])
        for i, (src, dst) in enumerate(
            [(avel, grid3(a1)), (modulus, grid3(md)), (vel, grid3(v0)), (pres, p0), (apres, ap)]
        )
    ]
    sensors = [
        pltpu.make_async_copy(src, dst, in_sem.at[5 + i])
        for i, (src, dst) in enumerate(
            [(svals_h, svals), (sowner_h, sowner), (sline_h, sline), (sstep_h, sstep)]
        )
    ]
    for copy in loads + sensors:
        copy.start()

    lane = lax.broadcasted_iota(jnp.int32, (CX, CY), 1)

    @pl.when(jnp.logical_not(has_ym))
    def _():
        for ref in (yl1, yl3, yl7):
            ref[...] = jnp.zeros(ref.shape, F32)
        yl5[...] = jnp.zeros(yl5.shape, F32)

    @pl.when(jnp.logical_not(has_yp))
    def _():
        for ref in (yh1, yh2, yh3, yh4, yh6, yh7, yh8, yh9):
            ref[...] = jnp.zeros(ref.shape, F32)
        yh5[...] = jnp.zeros(yh5.shape, F32)

    def greet(device):
        pl.semaphore_signal(barrier, inc=1, device_id=device, device_id_type=MESH)

    @pl.when(has_zm)
    def _():
        greet((gx, gy, gz - 1))

    @pl.when(has_zp)
    def _():
        greet((gx, gy, gz + 1))

    @pl.when(gz == 0)
    def _():
        for other in range(2, NGZ):
            greet((gx, gy, other))

    for step in range(1, NGY):
        greet((gx, lax.rem(gy + step, NGY), gz))
    for step in range(1, NGX):
        greet((lax.rem(gx + step, NGX), gy, gz))
    expected = (
        NGX - 1 + NGY - 1
        + has_zm.astype(jnp.int32) + has_zp.astype(jnp.int32) + (gz >= 2).astype(jnp.int32)
    )

    def comps(ref):
        return [ref.at[c] for c in range(3)]

    V0, A1, MA, V1, A0, MA0 = (comps(r) for r in (v0, a1, ma, v1, a0, ma0))

    zeros_layer = jnp.zeros((PITCH, CY), F32)
    zeros_rows = jnp.zeros((LAYERS, CY), F32)
    for ref in V1:
        ref[pl.ds(7, LAYERS, stride=PITCH), :] = zeros_rows
        ref[pl.ds(24, LAYERS, stride=PITCH), :] = zeros_rows
    for ref in V0 + A1 + MA + V1 + A0 + MA0 + [p1, m1, m0]:
        ref[0:PITCH, :] = zeros_layer
        ref[ROWS - PITCH:ROWS, :] = zeros_layer

    @pl.when(jnp.logical_not(has_xm))
    def _():
        for ref in V0 + [A1[0]] + MA + [A0[0]] + MA0:
            ref[pl.ds(7, LAYERS, stride=PITCH), :] = zeros_rows

    @pl.when(jnp.logical_not(has_xp))
    def _():
        for ref in V0 + MA + [A1[2]] + MA0 + [p1, m1, m0]:
            ref[pl.ds(24, LAYERS, stride=PITCH), :] = zeros_rows

    def ld(ref, z, dx=0):
        return ref[pl.ds((z + 1) * PITCH + 8 + dx, CX), :]

    def st(ref, z, value):
        ref[pl.ds(pl.multiple_of((z + 1) * PITCH + 8, 8), CX), :] = value

    def halo(blk, z, f):
        return pltpu.roll(blk[z & 3], (CY - ((z >> 2) * 16 + 2 * f)) & (CY - 1), 1)

    def ylo(u, blk, z, f):
        return jnp.where(lane == 0, halo(blk, z, f), pltpu.roll(u, 1, 1))

    def yhi(u, blk, z, f):
        shift = CY - 2 - (z >> 2) * 16 - 2 * f
        return jnp.where(lane == CY - 1, pltpu.roll(blk[z & 3], shift, 1), pltpu.roll(u, CY - 1, 1))

    def merge(dst, low, high, planes=range(4)):
        for zz in planes:
            dst[zz] = jnp.where((lane & 1) == 0, low[zz], pltpu.roll(high[zz], CY - 2, 1))

    def lap(ref, z, blk, f):
        c = ld(ref, z)
        h = halo(blk, z, f)
        low = jnp.where(lane == 0, h, pltpu.roll(c, 1, 1))
        high = jnp.where(lane == CY - 1, h, pltpu.roll(c, CY - 1, 1))
        total = ld(ref, z, 1) + ld(ref, z, -1) + (ld(ref, z + 1) + ld(ref, z - 1))
        return total + (low + high) - 6.0 * c, low

    def div(refs, z, low):
        x, y, w = (ld(r, z) for r in refs)
        return (x - ld(refs[0], z, -1)) + (y - low) + (w - ld(refs[2], z - 1))

    def grad(ref, z, yh, f):
        q = ld(ref, z)
        return ld(ref, z, 1) - q, yhi(q, yh, z, f) - q, ld(ref, z + 1) - q

    def s1(z, blk):
        lows = []
        for c in range(3):
            bend0[c, z], low = lap(V0[c], z, blk, c)
            lows.append(low)
            lm[c, z], _ = lap(MA[c], z, blk, 3 + c)
        st(p1, z, p0[z] + div(V0, z, lows[1]))
        st(m1, z, ap[z] - 0.25 * div(A1, z, ylo(ld(A1[1], z), blk, z, 6)))

    def s2(z, yh):
        gp, gm = grad(p1, z, yh, 0), grad(m1, z, yh, 1)
        g = ld(md, z)
        for c in range(3):
            st(V1[c], z, ld(V0[c], z) + 0.25 * (gp[c] + g * bend0[c, z]))
            new = ld(A1[c], z) + 0.25 * lm[c, z] - gm[c]
            st(A0[c], z, new)
            st(MA0[c], z, g * new)

    def s3(z, blk):
        total = None
        for c in range(3):
            part = ld(A1[c], z) * lap(V1[c], z, blk, c)[0] + ld(A0[c], z) * bend0[c, z]
            total = part if total is None else total + part
            lm0[c, z], _ = lap(MA0[c], z, blk, 3 + c)
        sh[z] = 0.25 * total
        st(m0, z, ld(m1, z) - 0.25 * div(A0, z, ylo(ld(A0[1], z), blk, z, 6)))

    def s4(z, yh):
        gm = grad(m0, z, yh, 0)
        for c in range(3):
            out[c, z] = ld(A0[c], z) + 0.25 * lm0[c, z] - gm[c]

    def every(fn, start=0, stop=CZ, unroll=UNROLL):
        turns = (stop - start) // unroll

        def step(n, carry):
            for k in range(unroll):
                fn(start + n * unroll + k)
            return carry

        lax.fori_loop(0, turns, step, 0)
        for z in range(start + turns * unroll, stop):
            fn(z)

    def some(fn, layers):
        for z in layers:
            fn(z)

    def pack_y(dst, fields):
        def step(zz, carry):
            acc = jnp.zeros((CX, CY), F32)
            for g in range(8):
                for f, ref in enumerate(fields):
                    s = g * 16 + 2 * f + 1
                    acc = jnp.where((lane >> 1) == (s >> 1), pltpu.roll(ld(ref, g * 4 + zz), s, 1), acc)
            dst[zz] = acc
            return carry
        lax.fori_loop(0, 4, step, 0)

    def pack_layers(dst, fields, layers, last=None):
        for zz in range(4):
            acc = jnp.zeros((CX, CY), F32)
            for z in layers:
                if z % 4 == zz:
                    for f, ref in enumerate(fields):
                        s = (z // 4) * 16 + 2 * f + 1
                        acc = jnp.where((lane >> 1) == (s >> 1), pltpu.roll(ld(ref, z), s, 1), acc)
            if zz == 3 and last is not None:
                acc = jnp.where(lane >= CY - 2, pltpu.roll(ld(last, CZ), CY - 1, 1), acc)
            dst[zz] = acc

    def face(ref, x):
        return ref[pl.ds(PITCH + 8 + x, CZ, stride=PITCH), :]

    def pack_x(dst, fields, x):
        for i, ref in enumerate(fields):
            dst[i * CZ:(i + 1) * CZ, :] = face(ref, x)

    def unpack_x(src, fields, x):
        for i, ref in enumerate(fields):
            ref[pl.ds(PITCH + 8 + x, CZ, stride=PITCH), :] = src[i * CZ:(i + 1) * CZ, :]

    def weigh_x(to, ref, x):
        for c in range(3):
            to[c][pl.ds(PITCH + 8 + x, CZ, stride=PITCH), :] = face(md, x) * face(ref[c], x)

    def row(ref, z, x):
        at = (z + 1) * PITCH + 8 + x
        return ref[at:at + 1, :]

    def weigh_rows(to, ref, layers, x):
        for z in layers:
            at = (z + 1) * PITCH + 8 + x
            for c in range(3):
                to[c][at:at + 1, :] = row(md, z, x) * row(ref[c], z, x)

    def rows_of(pairs, x):
        return [(ref, (z + 1) * PITCH + 8 + x) for ref, z in pairs]

    def pack_rows(dst, pairs, x):
        for i, (ref, row) in enumerate(rows_of(pairs, x)):
            dst[i:i + 1, :] = ref[row:row + 1, :]

    def unpack_rows(src, pairs, x):
        for i, (ref, row) in enumerate(rows_of(pairs, x)):
            ref[row:row + 1, :] = src[i:i + 1, :]

    def store(start, size, n):
        part = pl.ds(start, size)
        copies = [
            pltpu.make_async_copy(out.at[:, part], o_av.at[:, part], out_sem.at[3 * n]),
            pltpu.make_async_copy(
                m0.reshape(LAYERS, PITCH, CY).at[pl.ds(start + 1, size), pl.ds(8, CX), :],
                o_ap.at[part], out_sem.at[3 * n + 1],
            ),
            pltpu.make_async_copy(sh.at[part], o_sh.at[part], out_sem.at[3 * n + 2]),
        ]
        for copy in copies:
            copy.start()
        return copies

    class Link:
        def __init__(self, src, dst, send, recv, device, sends, gets):
            self.copy = pltpu.make_async_remote_copy(
                src_ref=src, dst_ref=dst, send_sem=send, recv_sem=recv,
                device_id=device, device_id_type=MESH,
            )
            self.sends, self.gets = sends, gets

        def start(self):
            pl.when(self.sends)(self.copy.start)

        def arrive(self):
            pl.when(self.gets)(self.copy.wait_recv)

        def flush(self):
            pl.when(self.sends)(self.copy.wait_send)

    links = []
    counts = {"x": 0, "y": 0, "z": 0}

    def link(kind, src, dst, device, sends, gets):
        n = counts[kind]
        counts[kind] += 1
        ss, rs = {"x": (xs_sem, xr_sem), "y": (ys_sem, yr_sem), "z": (zs_sem, zr_sem)}[kind]
        made = Link(src, dst, ss.at[n], rs.at[n], device, sends, gets)
        links.append(made)
        return made

    def x_down(src, dst):
        return link("x", src, dst, (gx - 1, gy, gz), has_xm, has_xp)

    def x_up(src, dst):
        return link("x", src, dst, (gx + 1, gy, gz), has_xp, has_xm)

    def y_down(src, dst):
        return link("y", src, dst, (gx, gy - 1, gz), has_ym, has_yp)

    def y_up(src, dst):
        return link("y", src, dst, (gx, gy + 1, gz), has_yp, has_ym)

    def z_down(src, dst):
        return link("z", src, dst, (gx, gy, gz - 1), has_zm, has_zp)

    def z_up(src, dst):
        return link("z", src, dst, (gx, gy, gz + 1), has_zp, has_zm)

    def go(*those):
        for one in those:
            one.start()

    settled = []

    def settle(*those):
        for one in those:
            one.flush()
            settled.append(one)

    def got(*those):
        for one in those:
            one.arrive()

    for copy in loads:
        copy.wait()

    def weight(z):
        g = ld(md, z)
        for c in range(3):
            st(MA[c], z, g * ld(A1[c], z))

    every(weight)
    lo1 = V0 + MA
    rim = (0, 1, CZ - 1)
    wide1 = V0 + A1 + [md]
    x9 = [(ref, z) for ref in wide1 for z in rim]
    pack_rows(xa9, x9, 0)
    pack_rows(xb9, x9, CX - 1)
    pack_y(ys1, lo1 + [A1[1]])

    pl.semaphore_wait(barrier, expected)

    r9x = [x_down(xa9, xh9), x_up(xb9, xl9)]
    r1y = [y_down(ys1, yh1), y_up(ys1, yl1)]
    r1x = [x_down(xa1, xh1), x_up(xb1, xl1)]
    zraw = [
        z_up(avel.at[:, CZ - 1], zl.at[3:6]),
        z_down(avel.at[:, 0], zu.at[3:6]),
        z_up(modulus.at[CZ - 1], zl.at[6]),
        z_down(modulus.at[0], zu.at[6]),
        z_up(vel.at[:, CZ - 1], zl.at[0:3]),
        z_down(vel.at[:, 0], zu.at[0:3]),
    ]
    go(*r9x, *r1y, *zraw)
    pack_x(xa1, wide1, 0)
    pack_x(xb1, wide1, CX - 1)
    go(*r1x)

    for copy in sensors:
        copy.wait()
    owner_row = sowner[...].astype(F32)
    r0 = lax.broadcasted_iota(jnp.int32, (32, 32), 0)
    r1 = lax.broadcasted_iota(jnp.int32, (32, 32), 1)
    owner_col = jnp.sum(jnp.where(r0 == r1, owner_row, 0.0), axis=1, keepdims=True)
    rank = jnp.sum(
        jnp.where((owner_col == owner_row) & (r0 < r1), 1.0, 0.0), axis=0, keepdims=True
    ).astype(jnp.int32)
    owner_int = owner_row.astype(jnp.int32)
    own_gx, own_gy = owner_int >> 3, owner_int & 7
    place = own_gy * 32 + own_gx * 8 + rank
    code_row = (own_gx * 32 + sstep[...] * CX + sline[...] + 1).astype(F32)
    code_col = jnp.sum(jnp.where(r0 == r1, code_row, 0.0), axis=1, keepdims=True)
    slot = lax.broadcasted_iota(jnp.int32, (256, 32), 0)
    cs[...] = jnp.dot(
        (slot == place).astype(F32), svals[...], precision=HIGH, preferred_element_type=F32
    ) + jnp.dot(
        (slot == place + 4).astype(F32), jnp.broadcast_to(code_col, (32, CY)),
        precision=HIGH, preferred_element_type=F32,
    )
    mine = pl.ds(pl.multiple_of(gy * 32, 32), 32)
    gath[mine, :] = cs[mine, :]

    stage1 = []
    for step in range(1, NGY):
        other = lax.rem(gy + step, NGY)
        stage1.append(
            pltpu.make_async_remote_copy(
                src_ref=cs.at[pl.ds(pl.multiple_of(other * 32, 32), 32)],
                dst_ref=gath.at[mine],
                send_sem=f1s.at[step - 1], recv_sem=f1r.at[step - 1],
                device_id=(gx, other, gz), device_id_type=MESH,
            )
        )
        stage1[-1].start()

    got(*r9x, *r1y)

    @pl.when(has_xp)
    def _():
        unpack_rows(xh9, x9, CX)
        weigh_rows(MA, A1, rim, CX)

    @pl.when(has_xm)
    def _():
        unpack_rows(xl9, x9, -1)
        weigh_rows(MA, A1, rim, -1)

    merge(c1, yl1, yh1)
    some(lambda z: s1(z, c1), rim)
    x10 = [(ref, z) for ref in (p1, m1) for z in (0, CZ - 1)]
    pack_rows(xa10, x10, 0)
    r10x = x_down(xa10, xh10)
    go(r10x)
    pack_layers(ys9, [p1, m1], (0, CZ - 1))
    r9y = y_down(ys9, yh9)
    zpm = [
        z_down(p1.at[pl.ds(PITCH + 8, CX)], zu.at[10]),
        z_down(m1.at[pl.ds(PITCH + 8, CX)], zu.at[11]),
    ]
    go(r9y, *zpm)
    for copy in stage1:
        copy.wait_recv()
    rows = gath[...]
    r256 = lax.broadcasted_iota(jnp.int32, (256, CY), 0)
    l256 = lax.broadcasted_iota(jnp.int32, (256, CY), 1)
    codes = pltpu.roll(rows, 252, 0)
    hot = jnp.where(((r256 & 7) < 4) & (codes == (l256 + 1).astype(F32)), 1.0, 0.0)
    dense[...] = lax.dot_general(
        hot, rows, (((0,), (0,)), ((), ())), precision=HIGH, preferred_element_type=F32
    )
    stage2 = []
    for step in range(1, NGX):
        other = lax.rem(gx + step, NGX)
        stage2.append(
            pltpu.make_async_remote_copy(
                src_ref=dense.at[pl.ds(pl.multiple_of(other * 32, 32), 32)],
                dst_ref=hsum.at[step - 1],
                send_sem=f2s.at[step - 1], recv_sem=f2r.at[step - 1],
                device_id=(other, gy, gz), device_id_type=MESH,
            )
        )
        stage2[-1].start()

    got(r10x, r9y)

    @pl.when(has_xp)
    def _():
        unpack_rows(xh10, x10, CX)

    some(lambda z: s2(z, yh9), (0, CZ - 1))
    first, final = pl.ds(PITCH + 8, CX), pl.ds(CZ * PITCH + 8, CX)
    zpart = [
        z_up(a0.at[:, final], zl.at[7:10]),
        z_down(a0.at[:, first], zu.at[7:10]),
    ]
    go(*zpart)

    got(*r1x)

    @pl.when(has_xp)
    def _():
        unpack_x(xh1, wide1, CX)
        weigh_x(MA, A1, CX)

    @pl.when(has_xm)
    def _():
        unpack_x(xl1, wide1, -1)
        weigh_x(MA, A1, -1)

    every(lambda z: s1(z, c1), 2, 14)

    for copy in stage2:
        copy.wait_recv()
    own = dense[pl.ds(pl.multiple_of(gx * 32, 32), 32), :]
    esum[...] = own + hsum[0] + hsum[1] + hsum[2]

    @pl.when(gz > 0)
    def _():
        to_surface = pltpu.make_async_remote_copy(
            src_ref=esum, dst_ref=ksum.at[gz - 1], send_sem=f3s, recv_sem=f3r.at[gz - 1],
            device_id=(gx, gy, 0), device_id_type=MESH,
        )
        to_surface.start()

    every(lambda z: s1(z, c1), 14, CZ - 1)
    pack_x(xa2, [p1, m1], 0)
    r2x = x_down(xa2, xh2)
    go(r2x)
    pack_y(ys2, [p1, m1])
    r2y = y_down(ys2, yh2)
    go(r2y)

    got(r2x, r2y)

    @pl.when(has_xp)
    def _():
        unpack_x(xh2, [p1, m1], CX)

    every(lambda z: s2(z, yh2), 1, CZ - 1)

    lo3 = V1 + MA0
    pack_x(xa3, A0, 0)
    pack_x(xb3, A0, CX - 1)
    xa3[3 * CZ:, :] = sum(face(V1[c], 0) * face(A1[c], -1) for c in range(3))
    xb3[3 * CZ:, :] = sum(face(V1[c], CX - 1) * face(A1[c], CX) for c in range(3))
    r3x = [x_down(xa3, xh3), x_up(xb3, xl3)]
    go(*r3x)
    pack_y(ys3, lo3 + [A0[1]])
    r3y = [y_down(ys3, yh3), y_up(ys3, yl3)]
    go(*r3y)

    for one in zpart + zpm:
        one.flush()
    got(*zraw, *zpm)

    surface = gz == 0
    r5x = [
        link("x", xa5, xh5, (gx - 1, gy, gz), surface & has_xm, surface & has_xp),
        link("x", xb5, xl5, (gx + 1, gy, gz), surface & has_xp, surface & has_xm),
    ]
    r5y = [
        link("y", ys5, yh5, (gx, gy - 1, gz), surface & has_ym, surface & has_yp),
        link("y", ys5, yl5, (gx, gy + 1, gz), surface & has_yp, surface & has_ym),
    ]

    @pl.when(surface)
    def _():
        for other in range(1, NGZ):
            pltpu.make_async_remote_copy(
                src_ref=esum, dst_ref=ksum.at[other - 1], send_sem=f3s, recv_sem=f3r.at[other - 1],
                device_id=(gx, gy, 1), device_id_type=MESH,
            ).wait_recv()
        total = esum[...]
        for other in range(1, NGZ):
            total = total + ksum[other - 1]
        esum[...] = total
        w = ld(A1[2], 0) + total[CX:2 * CX]
        st(A1[2], 0, w)
        w = w * ld(md, 0)
        st(MA[2], 0, w)
        pack_rows(xa5, [(A1[2], 0)], 0)
        pack_rows(xb5, [(A1[2], 0)], CX - 1)
        ys5[...] = pltpu.roll(w, 11, 1)

    go(*r5x, *r5y)


    @pl.when(has_zm)
    def _():
        for c in range(3):
            st(V0[c], -1, zl[c])
            st(MA[c], -1, zl[6] * zl[3 + c])
        st(A1[2], -1, zl[5])

    @pl.when(has_zp)
    def _():
        for c in range(3):
            st(V0[c], CZ, zu[c])
            st(MA[c], CZ, zu[6] * zu[3 + c])
        st(p1, CZ, zu[10] - ld(V0[2], CZ - 1))
        st(m1, CZ, zu[11] + 0.25 * ld(A1[2], CZ - 1))

    some(lambda z: s1(z, c1), rim)
    x6 = [(p1, 0), (m1, 0), (m1, 1), (A1[2], CZ - 1)]
    pack_rows(xa6, x6, 0)
    r6x = x_down(xa6, xh6)
    go(r6x)
    pack_layers(ys6, [p1, m1, A1[2]], rim)
    r6y = y_down(ys6, yh6)
    go(r6y)
    settle(*r9x, *r1y, *r1x, *zraw, r10x, r9y, r2x, r2y)
    for copy in stage1 + stage2:
        copy.wait_send()

    got(r6x, r6y, *r5x, *r5y)
    @pl.when(surface & has_xp)
    def _():
        unpack_rows(xh5, [(A1[2], 0)], CX)
        weigh_rows(MA, A1, (0,), CX)

    @pl.when(surface & has_xm)
    def _():
        unpack_rows(xl5, [(A1[2], 0)], -1)
        weigh_rows(MA, A1, (0,), -1)

    @pl.when(surface & has_yp)
    def _():
        yh1[0] = jnp.where(lane == 11, yh5[...], yh1[0])

    @pl.when(surface & has_ym)
    def _():
        yl1[0] = jnp.where(lane == 10, yl5[...], yl1[0])

    @pl.when(surface)
    def _():
        merge(c1, yl1, yh1, (0,))
        lm[2, 0], _ = lap(MA[2], 0, c1, 5)


    @pl.when(has_xp)
    def _():
        unpack_rows(xh6, x6, CX)

    some(lambda z: s2(z, yh6), rim)

    to_up[...] = sum(ld(V1[c], CZ - 1) * zu[3 + c] for c in range(3))
    to_down[...] = sum(ld(V1[c], 0) * zl[3 + c] for c in range(3))
    zshare = [z_up(to_up, from_low), z_down(to_down, from_high)]
    go(*zshare)
    got(*zpart)

    @pl.when(surface)
    def _():
        w = ld(A0[2], 0) + esum[0:CX, :]
        st(A0[2], 0, w)
        st(MA0[2], 0, w * ld(md, 0))

    @pl.when(has_zm)
    def _():
        g = zl[6]
        extra = ld(m1, 0)
        for c in range(3):
            a = zl[7 + c] + 0.25 * ld(MA[c], 0) - (extra if c == 2 else 0.0)
            st(A0[c], -1, a)
            st(MA0[c], -1, g * a)

    @pl.when(has_zp)
    def _():
        g = zu[6]
        top = CZ - 1
        w = ld(A1[2], top)
        gw = (ld(A1[2], top, 1) - w, yhi(w, yh6, top, 2) - w, -w)
        for c in range(3):
            a = zu[7 + c] + 0.25 * (ld(MA[c], top) - gw[c])
            st(A0[c], CZ, a)
            st(MA0[c], CZ, g * a)

    x7 = [(ref, z) for ref in A0 for z in rim]
    x7up = x7 + [(A0[0], CZ)]
    ends = (0, CZ - 1)
    pack_rows(xa7, x7, 0)
    pack_rows(xb7, x7up, CX - 1)
    for n, z in enumerate(ends):
        xa7[16 + n:17 + n, :] = sum(row(V1[c], z, 0) * row(A1[c], z, -1) for c in range(3))
        xb7[16 + n:17 + n, :] = sum(row(V1[c], z, CX - 1) * row(A1[c], z, CX) for c in range(3))
    r7x = [x_down(xa7, xh7), x_up(xb7, xl7)]
    go(*r7x)
    edges = (0, 1, 2, CZ - 2, CZ - 1)
    pack_layers(ys7, lo3 + [A0[1]], edges, last=A0[1])
    r7y = [y_down(ys7, yh7), y_up(ys7, yl7)]
    go(*r7y)
    got(*r3x, *r3y)

    @pl.when(has_xp)
    def _():
        unpack_x(xh3, A0, CX)
        weigh_x(MA0, A0, CX)

    @pl.when(has_xm)
    def _():
        unpack_x(xl3, A0, -1)
        weigh_x(MA0, A0, -1)

    merge(c3, yl3, yh3)
    every(lambda z: s3(z, c3), 3, CZ - 2)
    flat = sh.reshape(CZ * CX, CY)
    low, high = pl.ds(0, CZ, stride=CX), pl.ds(CX - 1, CZ, stride=CX)

    @pl.when(has_xp)
    def _():
        flat[high, :] = flat[high, :] + 0.25 * xh3[3 * CZ:, :]

    @pl.when(has_xm)
    def _():
        flat[low, :] = flat[low, :] + 0.25 * xl3[3 * CZ:, :]

    pack_x(xa4, [m0], 0)
    r4x = x_down(xa4, xh4)
    go(r4x)
    pack_y(ys4, [m0])
    r4y = y_down(ys4, yh4)
    go(r4y)

    got(*r7x, *r7y)

    @pl.when(has_xp)
    def _():
        unpack_rows(xh7, x7, CX)
        weigh_rows(MA0, A0, rim, CX)

    @pl.when(has_xm)
    def _():
        unpack_rows(xl7, x7up, -1)
        weigh_rows(MA0, A0, rim, -1)

    merge(c7, yl7, yh7)
    some(lambda z: s3(z, c7), edges)

    def add_share(x, ends_ref, bulk_ref):
        for z in edges:
            at = ends_ref[16 + ends.index(z):17 + ends.index(z), :] if z in ends else bulk_ref[3 * CZ + z:3 * CZ + z + 1, :]
            sh[z, x:x + 1, :] = sh[z, x:x + 1, :] + 0.25 * at

    @pl.when(has_xp)
    def _():
        add_share(CX - 1, xh7, xh3)

    @pl.when(has_xm)
    def _():
        add_share(0, xl7, xl3)

    @pl.when(has_zp)
    def _():
        x, y, w = (ld(r, CZ) for r in A0)
        low = jnp.where(lane == 0, pltpu.roll(yl7[3], 2, 1), pltpu.roll(y, 1, 1))
        d = (x - ld(A0[0], CZ, -1)) + (y - low) + (w - ld(A0[2], CZ - 1))
        st(m0, CZ, ld(m1, CZ) - 0.25 * d)

    x8 = [(m0, z) for z in edges + (CZ - 3,)]
    pack_rows(xa8, x8, 0)
    r8x = x_down(xa8, xh8)
    go(r8x)
    pack_layers(ys8, [m0], edges + (CZ - 3,))
    r8y = y_down(ys8, yh8)
    go(r8y)
    got(r4x, r4y)

    @pl.when(has_xp)
    def _():
        unpack_x(xh4, [m0], CX)

    every(lambda z: s4(z, yh4), 3, CZ - 3)
    early = store(3, CZ - 6, 0)
    settle(*r3x, *r3y, *r5x, *r5y, r6x, r6y, *r7x, *r7y)
    got(r8x, r8y)

    @pl.when(has_xp)
    def _():
        unpack_rows(xh8, x8, CX)

    some(lambda z: s4(z, yh8), (0, 1, 2, CZ - 3, CZ - 2, CZ - 1))
    got(*zshare)

    @pl.when(has_zm)
    def _():
        sh[0] = sh[0] + 0.25 * from_low[...]

    @pl.when(has_zp)
    def _():
        sh[CZ - 1] = sh[CZ - 1] + 0.25 * from_high[...]

    late = store(0, 3, 1) + store(CZ - 3, 3, 2)
    for one in links:
        if one not in zpart + zpm + settled:
            one.flush()

    @pl.when(gz > 0)
    def _():
        pltpu.make_async_remote_copy(
            src_ref=esum, dst_ref=ksum.at[gz - 1], send_sem=f3s, recv_sem=f3r.at[gz - 1],
            device_id=(gx, gy, 0), device_id_type=MESH,
        ).wait_send()

    for copy in early + late:
        copy.wait()


def hand_out(a, b, c, oa, ob, oc, sem):
    pieces = [(a.at[k], oa.at[k]) for k in range(3)] + [(b, ob), (c, oc)]
    copies = [pltpu.make_async_copy(p[0], p[1], sem.at[k]) for k, p in enumerate(pieces)]
    for copy in copies:
        copy.start()
    for copy in copies:
        copy.wait()


def shards(vel, pres, modulus, avel, apres, svals, sowner, sline, sstep):
    vector = pltpu.VMEM((3, ROWS, CY), F32)
    scalar = pltpu.VMEM((ROWS, CY), F32)
    flat3 = pltpu.VMEM((3, CZ, CX, CY), F32)
    flat = pltpu.VMEM((CZ, CX, CY), F32)
    pack = pltpu.VMEM((4, CX, CY), F32)
    plane = pltpu.VMEM((CX, CY), F32)
    ints = pltpu.VMEM((1, 32), jnp.int32)

    def lines(n):
        return pltpu.VMEM((n, CY), F32)

    def dma(n):
        return pltpu.SemaphoreType.DMA((n,))

    anywhere = pl.BlockSpec(memory_space=pl.ANY)
    sowner, sline, sstep = (a.reshape(1, 32) for a in (sowner, sline, sstep))
    operands = [
        pltpu.with_memory_space_constraint(a, pltpu.HBM)
        for a in (vel, pres, modulus, avel, apres, svals, sowner, sline, sstep)
    ]
    vel, pres, modulus, avel, apres, svals, sowner, sline, sstep = operands
    inner = pl.pallas_call(
        body,
        out_shape=(
            jax.ShapeDtypeStruct((3, CZ, CX, CY), F32),
            jax.ShapeDtypeStruct((CZ, CX, CY), F32),
            jax.ShapeDtypeStruct((CZ, CX, CY), F32),
        ),
        in_specs=[anywhere] * 9,
        out_specs=(anywhere,) * 3,
        scratch_shapes=[
            vector, vector, vector, scalar, scalar, scalar, vector, vector, vector, scalar,
            flat, flat, flat3, flat3, flat3, flat, flat3,
            pack, pack, pack, pack, pack, pack, pack, pack, pack, pack,
            pack, pack, pack, pack, pack, lines(24), lines(24), lines(24), lines(24), lines(8), lines(8),
            plane, plane, plane, pack, pack, pack, pack, pack, pack, pack,
            lines(7 * CZ), lines(7 * CZ), lines(7 * CZ), lines(7 * CZ),
            lines(2 * CZ), lines(2 * CZ),
            lines(4 * CZ), lines(4 * CZ), lines(4 * CZ), lines(4 * CZ),
            lines(CZ), lines(CZ),
            lines(8), lines(8), lines(8), lines(8), lines(8), lines(8),
            lines(24), lines(24), lines(24), lines(24), lines(8), lines(8),
            lines(32), ints, ints, ints,
            pltpu.VMEM((10, CX, CY), F32), pltpu.VMEM((12, CX, CY), F32),
            plane, plane, plane, plane,
            lines(256), lines(256), lines(CY), pltpu.VMEM((3, 32, CY), F32), lines(32),
            pltpu.VMEM((NGZ - 1, 32, CY), F32),
            dma(9), dma(9), dma(15), dma(15), dma(13), dma(13), dma(12), dma(12),
            dma(NGY - 1), dma(NGY - 1), dma(NGX - 1), dma(NGX - 1),
            pltpu.SemaphoreType.DMA, dma(NGZ - 1),
        ],
        compiler_params=pltpu.CompilerParams(
            collective_id=0, has_side_effects=True, vmem_limit_bytes=40 * 2**20
        ),
        cost_estimate=pl.CostEstimate(flops=20_000_000, bytes_accessed=3_670_016, transcendentals=0),
        name="adjoint",
    )(vel, pres, modulus, avel, apres, svals, sowner, sline, sstep)
    return pl.pallas_call(
        hand_out,
        out_shape=[jax.ShapeDtypeStruct(a.shape, F32) for a in inner],
        in_specs=[pl.BlockSpec(memory_space=pltpu.VMEM)] * 3,
        out_specs=[pl.BlockSpec(memory_space=pltpu.HBM)] * 3,
        scratch_shapes=[dma(5)],
        compiler_params=pltpu.CompilerParams(vmem_limit_bytes=16 * 2**20),
        name="handout",
    )(*inner)


def solution(mesh):
    return jax.shard_map(
        shards,
        mesh=mesh,
        in_specs=(
            P(None, "gz", "gx", "gy"),
            P("gz", "gx", "gy"),
            P("gz", "gx", "gy"),
            P(None, "gz", "gx", "gy"),
            P("gz", "gx", "gy"),
            P(("gx", "gy", "gz"), None),
            P(("gx", "gy", "gz"), None),
            P(("gx", "gy", "gz")),
            P(("gx", "gy", "gz")),
        ),
        out_specs=(P(None, "gz", "gx", "gy"), P("gz", "gx", "gy"), P("gz", "gx", "gy")),
        check_vma=False,
    )
```
